32 devices in a mesh: seq: 16 (over z, y, x), head: 2 (over core).
Axes of the slice: x: 2, y: 2, z: 4, core: 2. Of those that a mesh axis runs over, the one named last changes fastest.
Arguments:
- tokens: bfloat16 [2, 4096, 1024], P(None, 'seq'), may hold values from -6 to 6
- w_query: bfloat16 [1024, 512], P(None, 'head'), may hold values from -0.1875 to 0.1875
- w_key: bfloat16 [1024, 512], P(None, 'head'), may hold values from -0.1875 to 0.1875
- w_value: bfloat16 [1024, 1024], P(None, 'head'), may hold values from -0.1875 to 0.1875
- w_outgate: bfloat16 [1024, 1024], P(None, 'head'), may hold values from -0.1875 to 0.1875
- w_gates: bfloat16 [2, 1024, 4], P(None, None, 'head'), may hold values from -0.1875 to 0.1875
- gate_bias: float32 [2, 4], P(None, 'head'), may hold values from -6.5 to 11.5
- conv_query: float32 [4, 512], P(None, 'head'), may hold values from -3 to 3
- conv_key: float32 [4, 512], P(None, 'head'), may hold values from -3 to 3
- conv_value: float32 [4, 1024], P(None, 'head'), may hold values from -3 to 3
- out_gain: float32 [256], replicated, may hold values from 0.5 to 1.5
- w_out: bfloat16 [1024, 1024], P('head'), may hold values from -0.375 to 0.375
- mix_gain: float32 [1024], replicated, may hold values from 0.5 to 1.5
- ffn_gain: float32 [1024], replicated, may hold values from 0.5 to 1.5
- w_gate: bfloat16 [1024, 2816], P(None, 'head'), may hold values from -0.1875 to 0.1875
- w_up: bfloat16 [1024, 2816], P(None, 'head'), may hold values from -0.1875 to 0.1875
- w_down: bfloat16 [2816, 1024], P('head'), may hold values from -0.15625 to 0.15625
- cotangent: bfloat16 [2, 4096, 1024], P(None, 'seq'), may hold values from -6 to 6
Outputs:
- result: bfloat16 [2, 4096, 1024], P(None, 'seq')
- grad_input: float32 [2, 4096, 1024], P(None, 'seq')
- grad_w_query: float32 [1024, 512], P('seq', 'head')
- grad_w_key: float32 [1024, 512], P('seq', 'head')
- grad_w_value: float32 [1024, 1024], P('seq', 'head')
- grad_w_outgate: float32 [1024, 1024], P('seq', 'head')
- grad_w_gates: float32 [2, 1024, 4], P(None, 'seq', 'head')
- grad_gate_bias: float32 [2, 4], P(None, 'head')
- grad_conv_query: float32 [4, 512], P(None, 'head')
- grad_conv_key: float32 [4, 512], P(None, 'head')
- grad_conv_value: float32 [4, 1024], P(None, 'head')
- grad_out_gain: float32 [256], replicated
- grad_w_out: float32 [1024, 1024], P('head', 'seq')
- grad_mix_gain: float32 [1024], P('seq')
- grad_ffn_gain: float32 [1024], P('seq')
- grad_w_gate: float32 [1024, 2816], P('seq', 'head')
- grad_w_up: float32 [1024, 2816], P('seq', 'head')
- grad_w_down: float32 [2816, 1024], P('head', 'seq')
The draws below stay inside these ranges and needn't reach their ends.
All inputs are finite; a program needn't handle non-finite values.
Results may differ from the reference program's by a relative error of at most 0.013.
Values may be sent and summed in bfloat16 or wider, within the bound.
No kernel may reach another device: no remote copies, remote signals or barrier semaphores. Data moves between devices by JAX's collectives and lax.ppermute only.
A program may use at most 448 MiB of HBM per device.

```python
import jax
import jax.numpy as jnp
from jax import lax

D = 1024
HEADS = 4
DK = 128
DV = 256
FF = 2816
CONV = 4
GROUP = 64
SEQS = 2
SEQLEN = 4096


def draw_gate_bias(key, part):
    key = jax.random.fold_in(key, 7)
    pick_key, noise_key = jax.random.split(key, 2)
    share = 0.5
    quick = jax.random.bernoulli(pick_key, share, (HEADS,))
    noise = jax.random.uniform(noise_key, (2, HEADS), jnp.float32)
    slow_rows = jnp.stack([-6.5 + noise[0], 10.5 + noise[1]])
    quick_rows = jnp.stack([-1.0 + 2.0 * noise[0], 3.0 + noise[1]])
    return jnp.where(quick[None, :], quick_rows, slow_rows).astype(jnp.float32)


def shard_levels(key, dims, cuts, low, largest):
    level, own = 1.0, jax.random.fold_in(key, 6)
    for position, blocks in cuts:
        heights = jnp.exp(jax.random.uniform(jax.random.fold_in(own, position), (blocks,), jnp.float32, low / len(cuts), largest / len(cuts)))
        level = level * jnp.repeat(heights, dims[position] // blocks).reshape([-1 if axis == position else 1 for axis in range(len(dims))])
    return level


def normal_values(key, extent, scale, bound, pieces=(), kind=jnp.bfloat16):
    factor_of = shard_levels(key, extent, pieces, -0.22, 0.18) if pieces else 1.0
    entries = jax.random.normal(key, extent, jnp.float32) * scale * factor_of
    return jnp.minimum(jnp.maximum(entries, -bound), bound).astype(kind)


def setup_inputs(seed: int = 0) -> dict:
    key_list = jax.random.split(jax.random.key(seed), 19)
    tokens = normal_values(key_list[0], (SEQS, SEQLEN, D), 1.0, 6.0, ((1, 16),))
    w_query = normal_values(key_list[1], (D, HEADS * DK), D ** -0.5, 0.1875, ((1, 2),))
    w_key = normal_values(key_list[2], (D, HEADS * DK), D ** -0.5, 0.1875, ((1, 2),))
    w_value = normal_values(key_list[3], (D, HEADS * DV), D ** -0.5, 0.1875, ((1, 2),))
    w_outgate = normal_values(key_list[4], (D, HEADS * DV), D ** -0.5, 0.1875, ((1, 2),))
    w_gates = normal_values(key_list[5], (2, D, HEADS), D ** -0.5, 0.1875, ((2, 2),))
    gate_bias = draw_gate_bias(jax.random.fold_in(key_list[18], 71), 0)
    conv_query = normal_values(key_list[7], (CONV, HEADS * DK), 0.5, 3.0, ((1, 2),), jnp.float32)
    conv_key = normal_values(key_list[8], (CONV, HEADS * DK), 0.5, 3.0, ((1, 2),), jnp.float32)
    conv_value = normal_values(key_list[9], (CONV, HEADS * DV), 0.5, 3.0, ((1, 2),), jnp.float32)
    out_gain = jnp.clip(1.0 + 0.1 * jax.random.normal(key_list[10], (DV,), jnp.float32), 0.5, 1.5)
    w_out = normal_values(key_list[11], (HEADS * DV, D), (HEADS * DV // 4) ** -0.5, 0.375, ((0, 2),))
    mix_gain = jnp.clip(1.0 + 0.1 * jax.random.normal(key_list[12], (D,), jnp.float32), 0.5, 1.5)
    ffn_gain = jnp.clip(1.0 + 0.1 * jax.random.normal(key_list[13], (D,), jnp.float32), 0.5, 1.5)
    w_gate = normal_values(key_list[14], (D, FF), D ** -0.5, 0.1875, ((1, 2),))
    w_up = normal_values(key_list[15], (D, FF), D ** -0.5, 0.1875, ((1, 2),))
    w_down = normal_values(key_list[16], (FF, D), (FF // 2) ** -0.5, 0.15625, ((0, 2),))
    cotangent = normal_values(key_list[17], (SEQS, SEQLEN, D), 1.0, 6.0, ((1, 16),))
    return {"tokens": tokens, "w_query": w_query, "w_key": w_key, "w_value": w_value, "w_outgate": w_outgate, "w_gates": w_gates, "gate_bias": gate_bias, "conv_query": conv_query, "conv_key": conv_key, "conv_value": conv_value, "out_gain": out_gain, "w_out": w_out, "mix_gain": mix_gain, "ffn_gain": ffn_gain, "w_gate": w_gate, "w_up": w_up, "w_down": w_down, "cotangent": cotangent}


@jax.custom_vjp
def low(v):
    return lax.optimization_barrier(v.astype(jnp.bfloat16)).astype(jnp.float32)

@jax.custom_vjp
def low_back(v):
    return v

def low_keep(v):
    return (low(v), None)

def low_pass(kept, grad):
    return (grad,)

def back_keep(v):
    return (v, None)

def back_low(kept, grad):
    return (low(grad),)
low.defvjp(low_keep, low_pass)
low_back.defvjp(back_keep, back_low)
HIGHEST = lax.Precision.HIGHEST

def rms_scale(values, epsilon):
    return lax.rsqrt(lax.optimization_barrier(jnp.mean(values * values, axis=-1, keepdims=True)) + epsilon)

def norm_apply(values, gain):
    return values * rms_scale(values, 1e-06) * gain

def inverse_unit(strict_lower):
    block_size = strict_lower.shape[-1]
    identity_map = jnp.eye(block_size, dtype=strict_lower.dtype)
    power = -strict_lower
    inverse = identity_map + power
    for level in range(1, block_size.bit_length() - 1):
        power = jnp.matmul(power, power, precision=HIGHEST)
        inverse = jnp.matmul(inverse, identity_map + power, precision=HIGHEST)
    return inverse

def group_step(carry_state, block):
    queries, keys_unit, values, beta_rate, logdecay = block
    block_size = keys_unit.shape[1]
    positions = jnp.arange(block_size)
    strict = (positions[:, None] > positions[None, :]).astype(carry_state.dtype)
    within = (positions[:, None] >= positions[None, :]).astype(carry_state.dtype)
    cumulative = jnp.cumsum(jnp.swapaxes(logdecay, 1, 2), axis=-1)
    beta_row = jnp.swapaxes(beta_rate, 1, 2)
    decays = jnp.exp(jnp.minimum(cumulative[..., :, None] - cumulative[..., None, :], 0.0)) * beta_row[..., None, :]
    strict_lower = jnp.einsum('sthd,suhd->shtu', keys_unit, keys_unit, precision=HIGHEST) * decays * strict
    growth = jnp.exp(cumulative)[..., None]
    carried = jnp.einsum('sthd,shde->shte', keys_unit, carry_state, precision=HIGHEST)
    fresh_values = jnp.matmul(inverse_unit(strict_lower), jnp.swapaxes(values, 1, 2) - growth * carried, precision=HIGHEST)
    scores = jnp.einsum('sthd,suhd->shtu', queries, keys_unit, precision=HIGHEST) * decays * within
    output = growth * jnp.einsum('sthd,shde->shte', queries, carry_state, precision=HIGHEST)
    output = output + jnp.matmul(scores, fresh_values, precision=HIGHEST)
    tail_weight = jnp.exp(cumulative[..., -1:] - cumulative) * beta_row
    new_state = jnp.exp(cumulative[..., -1])[..., None, None] * carry_state
    new_state = new_state + jnp.einsum('sht,sthd,shte->shde', tail_weight, keys_unit, fresh_values, precision=HIGHEST)
    return (new_state, jnp.swapaxes(output, 1, 2))

def run_groups(carry_state, queries, keys_unit, values, beta_rate, logdecay):

    def to_blocks(field):
        count = field.shape[1] // GROUP
        return jnp.swapaxes(field.reshape((field.shape[0], count, GROUP) + field.shape[2:]), 0, 1)
    blocks = tuple((to_blocks(field) for field in (queries, keys_unit, values, beta_rate, logdecay)))
    final_state, outputs = lax.scan(jax.checkpoint(group_step), carry_state, blocks)
    outputs = jnp.swapaxes(outputs, 0, 1)
    return (outputs.reshape((outputs.shape[0], outputs.shape[1] * outputs.shape[2]) + outputs.shape[3:]), final_state)

def short_conv(extended, kernel):
    length = extended.shape[1] - CONV + 1
    summed = kernel[0] * extended[:, 0:length]
    for offset in range(1, CONV):
        summed = summed + kernel[offset] * extended[:, offset:offset + length]
    return jax.nn.silu(summed)

def unit_rows(field):
    return field * lax.rsqrt(lax.optimization_barrier(jnp.sum(field * field, axis=-1, keepdims=True)) + 1e-06)

def mixer_inputs(ext_q, ext_k, ext_v, gates, conv_query, conv_key, conv_value, gate_bias):
    conv_q = short_conv(ext_q, conv_query)
    head_shape = conv_q.shape[:2] + (conv_q.shape[2] // DK, DK)
    queries = unit_rows(conv_q.reshape(head_shape)) * DK ** (-0.5)
    keys_unit = unit_rows(short_conv(ext_k, conv_key).reshape(head_shape))
    conv_v = short_conv(ext_v, conv_value)
    values = conv_v.reshape(conv_v.shape[:2] + (conv_v.shape[2] // DV, DV))
    beta_rate = jax.nn.sigmoid(gates[:, :, 0] + gate_bias[0])
    logdecay = jax.nn.log_sigmoid(gates[:, :, 1] + gate_bias[1])
    return (queries, keys_unit, values, beta_rate, logdecay)

def gated_norm(output, proj_g, out_gain):
    gate_value = proj_g.reshape(output.shape)
    normed = output * rms_scale(output, 1e-05) * out_gain * jax.nn.silu(gate_value)
    return normed.reshape(proj_g.shape)

def matmul_high(left, right):
    return jnp.matmul(left, right, precision=HIGHEST)

def forward_layer(inputs, w_query, w_key, w_value, w_outgate, w_gates, gate_bias, conv_query, conv_key, conv_value, out_gain, w_out, mix_gain, ffn_gain, w_gate, w_up, w_down):
    mixed = low(norm_apply(inputs, mix_gain))
    proj_q = low_back(low(matmul_high(mixed, w_query)))
    proj_k = low_back(low(matmul_high(mixed, w_key)))
    proj_v = low_back(low(matmul_high(mixed, w_value)))
    proj_g = low_back(matmul_high(mixed, w_outgate))
    gates = low_back(jnp.einsum('std,cdh->stch', mixed, w_gates, precision=HIGHEST))

    def padded(field):
        return jnp.pad(field, ((0, 0), (CONV - 1, 0), (0, 0)))
    queries, keys_unit, values, beta_rate, logdecay = mixer_inputs(padded(proj_q), padded(proj_k), padded(proj_v), gates, conv_query, conv_key, conv_value, gate_bias)
    start_state = jnp.zeros((inputs.shape[0], keys_unit.shape[2], DK, DV), jnp.float32)
    output, final_state = run_groups(start_state, queries, keys_unit, values, beta_rate, logdecay)
    gated = low(gated_norm(output, proj_g, out_gain))
    resid = inputs + low_back(matmul_high(gated, w_out))
    normed = low(norm_apply(resid, ffn_gain))
    gate_value = low_back(matmul_high(normed, w_gate))
    up_value = low_back(matmul_high(normed, w_up))
    hidden = low(jax.nn.silu(gate_value) * up_value)
    return resid + low_back(matmul_high(hidden, w_down))

def reference(tokens, w_query, w_key, w_value, w_outgate, w_gates, gate_bias, conv_query, conv_key, conv_value, out_gain, w_out, mix_gain, ffn_gain, w_gate, w_up, w_down, cotangent):
    floats = tuple((field.astype(jnp.float32) for field in (tokens, w_query, w_key, w_value, w_outgate, w_gates, gate_bias, conv_query, conv_key, conv_value, out_gain, w_out, mix_gain, ffn_gain, w_gate, w_up, w_down)))
    result, pullback = jax.vjp(forward_layer, *floats)
    grads = pullback(cotangent.astype(jnp.float32))
    return (result.astype(jnp.bfloat16), grads[0], grads[1], grads[2], grads[3], grads[4], grads[5], grads[6], grads[7], grads[8], grads[9], grads[10], grads[11], grads[12], grads[13], grads[14], grads[15], grads[16])
```

```python
import functools

import jax
import jax.numpy as jnp
from jax import lax
from jax.experimental import pallas as pl
from jax.experimental.pallas import tpu as pltpu
from jax.sharding import PartitionSpec as P

DK = 128
DV = 256
CONV = 4
HALO = 16
LANES = 128
SCALE = DK ** (-0.5)
F32 = jnp.float32
BF16 = jnp.bfloat16
NN = ((1,), (0,))
NT = ((1,), (1,))
TN = ((0,), (0,))
VMEM_LIMIT = 56 * 1024 * 1024


def dot(left, right, dims=NN):
    return lax.dot_general(
        left.astype(BF16), right.astype(BF16), (dims, ((), ())), preferred_element_type=F32
    )


def halves(field):
    high = field.astype(BF16)
    return high, (field - high.astype(F32)).astype(BF16)


def dot3(left, right, dims=NN):
    left_high, left_low = halves(left)
    right_high, right_low = halves(right)
    return dot(left_high, right_high, dims) + (
        dot(left_high, right_low, dims) + dot(left_low, right_high, dims)
    )


def ones_dot(ones, field):
    high, low = halves(field)
    lowest = field - high.astype(F32) - low.astype(F32)
    return dot(ones, high) + (dot(ones, low) + dot(ones, lowest))


def rows_cols(size):
    return (
        lax.broadcasted_iota(jnp.int32, (size, size), 0),
        lax.broadcasted_iota(jnp.int32, (size, size), 1),
    )


def log1p_small(value):
    shifted = 1.0 + value
    same = shifted == 1.0
    safe = jnp.where(same, 1.0, shifted - 1.0)
    return jnp.where(same, value, jnp.log(shifted) * (value / safe))


def log_sigmoid(value):
    return jnp.minimum(value, 0.0) - log1p_small(jnp.exp(-jnp.abs(value)))


def sigmoid(value):
    return 1.0 / (1.0 + jnp.exp(-value))


def row_sum(field):
    return jnp.sum(field, axis=-1, keepdims=True)


def inverse_unit(lowers, rows, cols):
    size = lowers[0].shape[0]
    same = (rows // 16) == (cols // 16)
    eye = (rows == cols).astype(F32)
    powers = [jnp.where(same, -lower, 0.0) for lower in lowers]
    inverses = [eye + power for power in powers]
    for _ in range(3):
        powers = [dot3(power, power) for power in powers]
        inverses = [inv + dot3(inv, power) for inv, power in zip(inverses, powers)]
    block = 16
    while block * 2 <= size:
        inside = ((rows // (2 * block)) == (cols // (2 * block))) & (
            (rows // block) != (cols // block)
        )
        parts = [
            dot3(jnp.where(inside, lower, 0.0), inv) for lower, inv in zip(lowers, inverses)
        ]
        inverses = [inv - dot3(inv, part) for inv, part in zip(inverses, parts)]
        block *= 2
    return inverses


def conv_pre(extended, taps):
    total = taps[CONV - 1 : CONV] * extended
    for offset in range(CONV - 1):
        total = total + taps[offset : offset + 1] * pltpu.roll(extended, CONV - 1 - offset, 0)
    return total[HALO:]


def silu(value):
    return value * sigmoid(value)


def silu_slope(value):
    gate = sigmoid(value)
    return gate * (1.0 + value * (1.0 - gate))


def unit(field):
    inverse = lax.rsqrt(row_sum(field * field) + 1e-06)
    return field * inverse, inverse


def first_body(
    heads, x_ref, gain_ref, wq_ref, wk_ref, wv_ref, wg_ref, wgates_ref, bias_ref, cq_ref, ck_ref,
    cv_ref, mixed_ref, proj_ref, pg_ref, gates_ref, sums_ref, inv_ref, mapk_ref, fresh_ref,
    score_ref, reach_ref, local_ref, decay_ref, piece_ref, low_ref,
):
    x = x_ref[0].astype(F32)
    mixed = x * lax.rsqrt(jnp.mean(x * x, axis=-1, keepdims=True) + 1e-06) * gain_ref[...]
    mixed = mixed.astype(BF16)
    main = mixed[HALO:]
    mixed_ref[0] = main
    proj_q = dot(mixed, wq_ref[...]).astype(BF16)
    proj_k = dot(mixed, wk_ref[...]).astype(BF16)
    proj_v = dot(mixed, wv_ref[...]).astype(BF16)
    wide = heads * DK
    proj_ref[0, :, :wide] = proj_q
    proj_ref[0, :, wide : 2 * wide] = proj_k
    proj_ref[0, :, 2 * wide :] = proj_v
    pg_ref[0] = dot(main, wg_ref[...])
    gates = dot(main, wgates_ref[...]) + bias_ref[...]
    gates_ref[0] = gates
    size = main.shape[0]
    rows, cols = rows_cols(size)
    lower = rows >= cols
    strict = rows > cols
    sums = ones_dot(lower.astype(BF16), log_sigmoid(gates))
    sums_ref[0] = sums
    sums_t = jnp.transpose(sums)
    conv_q = silu(conv_pre(proj_q.astype(F32), cq_ref[...]))
    conv_k = silu(conv_pre(proj_k.astype(F32), ck_ref[...]))
    conv_v = silu(conv_pre(proj_v.astype(F32), cv_ref[...]))
    each = range(heads)
    queries = [unit(conv_q[:, h * DK : (h + 1) * DK])[0] * SCALE for h in each]
    keys = [unit(conv_k[:, h * DK : (h + 1) * DK])[0] for h in each]
    values = [conv_v[:, h * DV : (h + 1) * DV] for h in each]
    beta = [sigmoid(gates[:, h : h + 1]) for h in each]
    total = [sums[:, heads + h : heads + h + 1] for h in each]
    decay = [
        jnp.where(
            lower, jnp.exp(jnp.minimum(total[h] - sums_t[heads + h : heads + h + 1, :], 0.0)), 0.0
        )
        for h in each
    ]
    scaled = [beta[h] * keys[h] for h in each]
    lowers = [jnp.where(strict, dot3(keys[h], scaled[h], NT) * decay[h], 0.0) for h in each]
    inverses = inverse_unit(lowers, rows, cols)
    growth = [jnp.exp(total[h]) for h in each]
    last = [total[h][size - 1 : size] for h in each]
    tail = [jnp.exp(last[h] - total[h]) * scaled[h] for h in each]
    mapk = [dot3(inverses[h], growth[h] * keys[h]) for h in each]
    fresh = [dot3(inverses[h], values[h]) for h in each]
    scores = [dot3(queries[h], scaled[h], NT) * decay[h] for h in each]
    moved = [-dot3(tail[h], mapk[h], TN) for h in each]
    shift = [dot3(tail[h], fresh[h], TN) for h in each]
    reach = [growth[h] * queries[h] - dot3(scores[h], mapk[h]) for h in each]
    local = [dot3(scores[h], fresh[h]) for h in each]
    for h in each:
        piece_ref[0, h, :, :DK] = moved[h]
        piece_ref[0, h, :, DK:] = shift[h]
        low_ref[0, h, :, :DK] = moved[h].astype(BF16)
        low_ref[0, h, :, DK:] = shift[h].astype(BF16)
        inv_ref[0, h] = inverses[h]
        mapk_ref[0, h] = mapk[h]
        fresh_ref[0, h] = fresh[h]
        score_ref[0, h] = scores[h]
        reach_ref[0, h] = reach[h]
        local_ref[0, h] = local[h]
        decay_ref[0, h] = decay[h]


def join_body(pairs, level, piece_ref, got_ref, scale_ref, out_ref, low_ref):
    for p in range(pairs):
        own = piece_ref[p]
        got = got_ref[p].astype(F32)
        mine = scale_ref[level, p]
        theirs = scale_ref[level, pairs + p]
        high, low = halves(own[:, :DK])
        moved = dot(high, got_ref[p]) + dot(low, got_ref[p])
        moved = moved + mine * got
        out = jnp.concatenate([moved[:, :DK] + theirs * own[:, :DK], moved[:, DK:] + own[:, DK:]], axis=1)
        out_ref[p] = out
        low_ref[p] = out.astype(BF16)


def map_body(pairs, level, own_ref, got_ref, scale_ref, out_ref, low_ref):
    for p in range(pairs):
        own = own_ref[p]
        got = got_ref[p]
        high, low = halves(own)
        out = dot(got, high) + dot(got, low)
        out = out + scale_ref[level, pairs + p] * own + scale_ref[level, p] * got.astype(F32)
        out_ref[p] = out
        low_ref[p] = out.astype(BF16)


def entry_body(pairs, level, near_ref, far_ref, scale_ref, out_ref):
    for p in range(pairs):
        near = near_ref[p]
        far = far_ref[p]
        moved = dot(near[:, :DK], far) + scale_ref[level, p] * far.astype(F32)
        out_ref[p] = moved + near[:, DK:].astype(F32)


def back_body(pairs, level, map_ref, own_ref, got_ref, scale_ref, out_ref, low_ref):
    for p in range(pairs):
        got = got_ref[p]
        high, low = halves(map_ref[p])
        moved = dot(high, got, TN) + dot(low, got, TN)
        out = own_ref[p] + moved + scale_ref[level, p] * got.astype(F32)
        out_ref[p] = out
        low_ref[p] = out.astype(BF16)


def exit_body(pairs, level, map_ref, near_ref, far_ref, scale_ref, out_ref):
    for p in range(pairs):
        far = far_ref[p]
        moved = dot(map_ref[p], far, TN)
        out_ref[p] = near_ref[p].astype(F32) + moved + scale_ref[level, p] * far.astype(F32)


def mixer_out_body(
    heads, state_ref, fresh_ref, mapk_ref, reach_ref, local_ref, pg_ref, gain_ref, wout_ref,
    made_ref, output_ref, gated_ref, attn_ref,
):
    for h in range(heads):
        state = state_ref[0, h]
        made_ref[0, h] = fresh_ref[0, h] - dot3(mapk_ref[0, h], state)
        output = local_ref[0, h] + dot3(reach_ref[0, h], state)
        output_ref[0, :, h * DV : (h + 1) * DV] = output
        scale = lax.rsqrt(jnp.mean(output * output, axis=-1, keepdims=True) + 1e-05)
        gate = pg_ref[0, :, h * DV : (h + 1) * DV]
        gated_ref[0, :, h * DV : (h + 1) * DV] = (
            output * scale * gain_ref[...] * silu(gate)
        ).astype(BF16)
    attn_ref[0] = dot(gated_ref[0], wout_ref[...]).astype(BF16)


def feed_body(
    x_ref, mine_ref, other_ref, cot_ref, gain_ref, wgate_ref, wup_ref, wdown_ref, resid_ref,
    normed_ref, hidden_ref, dgu_ref, down_ref, dnorm_ref,
):
    units = wgate_ref.shape[1]
    attn = mine_ref[0].astype(F32) + other_ref[0].astype(F32)
    resid = x_ref[0].astype(F32) + attn
    resid_ref[0] = resid
    normed = resid * lax.rsqrt(jnp.mean(resid * resid, axis=-1, keepdims=True) + 1e-06)
    normed = (normed * gain_ref[...]).astype(BF16)
    normed_ref[0] = normed
    gate = dot(normed, wgate_ref[...])
    up = dot(normed, wup_ref[...])
    d_hidden = dot(cot_ref[0], wdown_ref[...], NT)
    sig = sigmoid(gate)
    active = gate * sig
    hidden = (active * up).astype(BF16)
    hidden_ref[0] = hidden
    d_gate = (d_hidden * up * (sig + active * (1.0 - sig))).astype(BF16)
    d_up = (d_hidden * active).astype(BF16)
    dgu_ref[0, :, :units] = d_gate
    dgu_ref[0, :, units:] = d_up
    down_ref[0] = dot(hidden, wdown_ref[...]).astype(BF16)
    dnorm_ref[0] = (dot(d_gate, wgate_ref[...], NT) + dot(d_up, wup_ref[...], NT)).astype(BF16)


def mixer_back_body(
    heads, resid_ref, mine_ref, other_ref, cot_ref, output_ref, pg_ref, reach_ref, gain_ref,
    wout_ref, ogain_ref, dresid_ref, dattn_ref, dout_ref, dpg_ref, back_ref, low_ref, dgain_ref,
    dogain_ref,
):
    step = pl.program_id(0)
    resid = resid_ref[0]
    inverse = lax.rsqrt(jnp.mean(resid * resid, axis=-1, keepdims=True) + 1e-06)
    unit_resid = resid * inverse
    d_normed = mine_ref[0].astype(F32) + other_ref[0].astype(F32)
    d_gain = jnp.sum(d_normed * unit_resid, axis=0, keepdims=True)
    d_unit = d_normed * gain_ref[...]
    d_resid = inverse * (
        d_unit - unit_resid * jnp.mean(d_unit * unit_resid, axis=-1, keepdims=True)
    )
    d_resid = d_resid + cot_ref[0].astype(F32)
    dresid_ref[0] = d_resid
    d_attn = d_resid.astype(BF16)
    dattn_ref[0] = d_attn
    d_gated = dot(d_attn, wout_ref[...], NT)
    d_ogain = jnp.zeros((1, DV), F32)
    for h in range(heads):
        part = slice(h * DV, (h + 1) * DV)
        output = output_ref[0, :, part]
        inverse = lax.rsqrt(jnp.mean(output * output, axis=-1, keepdims=True) + 1e-05)
        unit_out = output * inverse
        gate = pg_ref[0, :, part]
        grad = d_gated[:, part]
        active = silu(gate)
        d_ogain = d_ogain + jnp.sum(grad * unit_out * active, axis=0, keepdims=True)
        dpg_ref[0, :, part] = (grad * unit_out * ogain_ref[...] * silu_slope(gate)).astype(BF16)
        d_unit = grad * ogain_ref[...] * active
        d_out = inverse * (d_unit - unit_out * jnp.mean(d_unit * unit_out, axis=-1, keepdims=True))
        dout_ref[0, :, part] = d_out
        back = dot3(reach_ref[0, h], d_out, TN)
        back_ref[0, h] = back
        low_ref[0, h] = back.astype(BF16)

    @pl.when(step == 0)
    def _():
        dgain_ref[...] = d_gain
        dogain_ref[...] = d_ogain

    @pl.when(step > 0)
    def _():
        dgain_ref[...] += d_gain
        dogain_ref[...] += d_ogain


def conv_back(grad, extended, taps, pre):
    d_pre = grad * silu_slope(pre)
    padded = jnp.concatenate([jnp.zeros((HALO, d_pre.shape[1]), F32), d_pre], axis=0)
    length = padded.shape[0]
    d_ext = taps[CONV - 1 : CONV] * padded
    d_taps = []
    for offset in range(CONV):
        back = CONV - 1 - offset
        if back:
            d_ext = d_ext + taps[offset : offset + 1] * pltpu.roll(padded, length - back, 0)
            shifted = pltpu.roll(extended, back, 0)
        else:
            shifted = extended
        d_taps.append(jnp.sum(padded * shifted, axis=0, keepdims=True))
    return d_ext, jnp.concatenate(d_taps, axis=0)


def early_body(
    heads, proj_ref, gates_ref, sums_ref, dout_ref, state_ref, made_ref, inv_ref, score_ref,
    decay_ref, cq_ref, ck_ref, xone_ref, xmap_ref, dkey_ref, dcol_ref, dext_ref, dtap_ref,
):
    step = pl.program_id(0)
    wide = heads * DK
    ext_q = proj_ref[0, :, :wide].astype(F32)
    ext_k = proj_ref[0, :, wide : 2 * wide].astype(F32)
    pre_q = conv_pre(ext_q, cq_ref[...])
    conv_q = silu(pre_q)
    conv_k = silu(conv_pre(ext_k, ck_ref[...]))
    gates = gates_ref[0]
    sums = sums_ref[0]
    size = gates.shape[0]
    each = range(heads)
    units = [unit(conv_q[:, h * DK : (h + 1) * DK]) for h in each]
    queries = [units[h][0] * SCALE for h in each]
    keys = [unit(conv_k[:, h * DK : (h + 1) * DK])[0] for h in each]
    beta = [sigmoid(gates[:, h : h + 1]) for h in each]
    total = [sums[:, heads + h : heads + h + 1] for h in each]
    growth = [jnp.exp(total[h]) for h in each]
    tail = [jnp.exp(total[h][size - 1 : size] - total[h]) * beta[h] * keys[h] for h in each]
    d_out = [dout_ref[0, :, h * DV : (h + 1) * DV] for h in each]
    d_made = [dot3(score_ref[0, h], d_out[h], TN) for h in each]
    d_score = [dot3(d_out[h], made_ref[0, h], NT) * decay_ref[0, h] for h in each]
    d_query = [
        dot3(d_score[h], beta[h] * keys[h]) + dot3(growth[h] * d_out[h], state_ref[0, h], NT)
        for h in each
    ]
    d_key = [dot3(d_score[h], queries[h], TN) for h in each]
    x_one = [dot3(inv_ref[0, h], d_made[h], TN) for h in each]
    x_map = [dot3(inv_ref[0, h], tail[h], TN) for h in each]
    lanes = lax.broadcasted_iota(jnp.int32, (size, LANES), 1)
    cols = jnp.zeros((size, LANES), F32)
    grads = []
    for h in each:
        xone_ref[0, h] = x_one[h]
        xmap_ref[0, h] = x_map[h]
        dkey_ref[0, h] = beta[h] * d_key[h]
        key_sum = row_sum(d_key[h] * keys[h])
        cols = cols + jnp.where(lanes == h, key_sum, 0.0)
        d_total = row_sum(d_query[h] * queries[h]) - beta[h] * key_sum
        cols = cols + jnp.where(lanes == heads + h, d_total, 0.0)
        unit_q, inverse = units[h]
        d_unit = d_query[h] * SCALE
        grads.append(inverse * (d_unit - unit_q * row_sum(d_unit * unit_q)))
    dcol_ref[0] = cols
    d_ext, d_taps = conv_back(jnp.concatenate(grads, axis=1), ext_q, cq_ref[...], pre_q)
    dext_ref[0] = d_ext

    @pl.when(step == 0)
    def _():
        dtap_ref[...] = d_taps

    @pl.when(step > 0)
    def _():
        dtap_ref[...] += d_taps


def late_body(
    heads, proj_ref, gates_ref, sums_ref, dend_ref, state_ref, made_ref, decay_ref, xone_ref,
    xmap_ref, dkey_ref, dcol_ref, dextq_ref, ck_ref, cv_ref, dext_ref, dgates_ref, dtap_ref, dbias_ref,
):
    step = pl.program_id(0)
    wide = heads * DK
    ext_k = proj_ref[0, :, wide : 2 * wide].astype(F32)
    ext_v = proj_ref[0, :, 2 * wide :].astype(F32)
    pre_k = conv_pre(ext_k, ck_ref[...])
    pre_v = conv_pre(ext_v, cv_ref[...])
    conv_k = silu(pre_k)
    gates = gates_ref[0]
    sums = sums_ref[0]
    size = gates.shape[0]
    rows, cols = rows_cols(size)
    strict = rows > cols
    each = range(heads)
    units = [unit(conv_k[:, h * DK : (h + 1) * DK]) for h in each]
    keys = [units[h][0] for h in each]
    beta = [sigmoid(gates[:, h : h + 1]) for h in each]
    total = [sums[:, heads + h : heads + h + 1] for h in each]
    growth = [jnp.exp(total[h]) for h in each]
    left = [jnp.exp(total[h][size - 1 : size] - total[h]) for h in each]
    d_end = [dend_ref[0, h] for h in each]
    made = [made_ref[0, h] for h in each]
    state = [state_ref[0, h] for h in each]
    d_rhs = [xone_ref[0, h] + dot3(xmap_ref[0, h], d_end[h]) for h in each]
    d_tail = [dot3(made[h], d_end[h], NT) for h in each]
    d_lower = [
        jnp.where(strict, -dot3(d_rhs[h], made[h], NT) * decay_ref[0, h], 0.0) for h in each
    ]
    d_plain = [
        dot3(d_lower[h], beta[h] * keys[h]) - dot3(growth[h] * d_rhs[h], state[h], NT) for h in each
    ]
    d_turned = [dot3(d_lower[h], keys[h], TN) for h in each]
    lanes = lax.broadcasted_iota(jnp.int32, (size, LANES), 1)
    places = lax.broadcasted_iota(jnp.int32, (size, 1), 0)
    d_col = dcol_ref[0]
    grads_k = []
    for h in each:
        turned = row_sum(d_turned[h] * keys[h])
        tails = row_sum(d_tail[h] * keys[h])
        tail_weight = left[h] * beta[h]
        d_key = d_plain[h] + beta[h] * d_turned[h] + tail_weight * d_tail[h] + dkey_ref[0, h]
        d_total = row_sum(d_plain[h] * keys[h]) - beta[h] * turned - tail_weight * tails
        ended = jnp.sum(tail_weight * tails, axis=0, keepdims=True)
        whole = jnp.sum(row_sum(d_end[h] * state[h]), axis=0, keepdims=True)
        ended = ended + growth[h][size - 1 : size] * whole
        d_total = d_total + jnp.where(places == size - 1, ended, 0.0)
        d_col = d_col + jnp.where(lanes == h, turned + left[h] * tails, 0.0)
        d_col = d_col + jnp.where(lanes == heads + h, d_total, 0.0)
        unit_k, inverse = units[h]
        grads_k.append(inverse * (d_key - unit_k * row_sum(d_key * unit_k)))
    upper = (rows <= cols).astype(BF16)
    d_decay = ones_dot(upper, d_col)
    rate = sigmoid(gates)
    d_gates = jnp.where(
        lanes < heads, d_col * rate * (1.0 - rate), d_decay / (1.0 + jnp.exp(gates))
    )
    d_gates = jnp.where(lanes < 2 * heads, d_gates, 0.0)
    dgates_ref[0] = d_gates.astype(BF16)
    d_bias = jnp.sum(d_gates, axis=0, keepdims=True)
    dext_k, dtaps_k = conv_back(jnp.concatenate(grads_k, axis=1), ext_k, ck_ref[...], pre_k)
    dext_v, dtaps_v = conv_back(jnp.concatenate(d_rhs, axis=1), ext_v, cv_ref[...], pre_v)
    dext_ref[0, :, :wide] = dextq_ref[0]
    dext_ref[0, :, wide : 2 * wide] = dext_k
    dext_ref[0, :, 2 * wide :] = dext_v

    @pl.when(step == 0)
    def _():
        dtap_ref[:, :wide] = dtaps_k
        dtap_ref[:, wide:] = dtaps_v
        dbias_ref[...] = d_bias

    @pl.when(step > 0)
    def _():
        dtap_ref[:, :wide] += dtaps_k
        dtap_ref[:, wide:] += dtaps_v
        dbias_ref[...] += d_bias


def input_back_body(
    dext_ref, edge_ref, dpg_ref, dgates_ref, wq_ref, wk_ref, wv_ref, wg_ref, wgates_ref, dproj_ref,
    dmixed_ref,
):
    wide = wq_ref.shape[1]
    own = dext_ref[0, HALO:]
    size = own.shape[0]
    d_proj = jnp.concatenate([own[: size - HALO], own[size - HALO :] + edge_ref[0]], axis=0)
    d_proj = d_proj.astype(BF16)
    dproj_ref[0] = d_proj
    d_mixed = dot(d_proj[:, :wide], wq_ref[...], NT)
    d_mixed = d_mixed + dot(d_proj[:, wide : 2 * wide], wk_ref[...], NT)
    d_mixed = d_mixed + dot(d_proj[:, 2 * wide :], wv_ref[...], NT)
    d_mixed = d_mixed + dot(dpg_ref[0], wg_ref[...], NT)
    d_mixed = d_mixed + dot(dgates_ref[0], wgates_ref[...], NT)
    dmixed_ref[0] = d_mixed.astype(BF16)


def last_body(x_ref, mine_ref, other_ref, dresid_ref, gain_ref, grad_ref, dgain_ref):
    step = pl.program_id(0)
    x = x_ref[0].astype(F32)
    inverse = lax.rsqrt(jnp.mean(x * x, axis=-1, keepdims=True) + 1e-06)
    unit_x = x * inverse
    d_mixed = mine_ref[0].astype(F32) + other_ref[0].astype(F32)
    d_gain = jnp.sum(d_mixed * unit_x, axis=0, keepdims=True)
    d_unit = d_mixed * gain_ref[...]
    back = inverse * (d_unit - unit_x * jnp.mean(d_unit * unit_x, axis=-1, keepdims=True))
    grad_ref[0] = dresid_ref[0] + back

    @pl.when(step == 0)
    def _():
        dgain_ref[...] = d_gain

    @pl.when(step > 0)
    def _():
        dgain_ref[...] += d_gain


def by_seq(shape):
    rest = len(shape) - 1
    return pl.BlockSpec((1,) + tuple(shape[1:]), lambda s: (s,) + (0,) * rest)


def whole(shape):
    rest = len(shape)
    return pl.BlockSpec(tuple(shape), lambda s: (0,) * rest)


def call(body, name, seqs, parts, shared, outs, sums=(), flops=0):
    operands = list(parts) + list(shared)
    out_shape = [jax.ShapeDtypeStruct(shape, kind) for shape, kind in list(outs) + list(sums)]
    moved = sum(a.size * a.dtype.itemsize for a in operands)
    moved += sum(a.size * a.dtype.itemsize for a in out_shape)
    return pl.pallas_call(
        body,
        grid=(seqs,),
        in_specs=[by_seq(a.shape) for a in parts] + [whole(a.shape) for a in shared],
        out_specs=[by_seq(shape) for shape, _ in outs] + [whole(shape) for shape, _ in sums],
        out_shape=out_shape,
        compiler_params=pltpu.CompilerParams(vmem_limit_bytes=VMEM_LIMIT),
        cost_estimate=pl.CostEstimate(flops=int(flops), bytes_accessed=int(moved), transcendentals=0),
        name=name,
    )(*operands)


def small_call(body, name, arrays, scales, outs):
    operands = list(arrays) + [scales]
    out_shape = [jax.ShapeDtypeStruct(shape, kind) for shape, kind in outs]
    moved = sum(a.size * a.dtype.itemsize for a in list(arrays) + out_shape)
    return pl.pallas_call(
        body,
        in_specs=[pl.BlockSpec(memory_space=pltpu.VMEM)] * len(arrays)
        + [pl.BlockSpec(memory_space=pltpu.SMEM)],
        out_specs=[pl.BlockSpec(memory_space=pltpu.VMEM)] * len(outs),
        out_shape=out_shape,
        compiler_params=pltpu.CompilerParams(vmem_limit_bytes=VMEM_LIMIT),
        cost_estimate=pl.CostEstimate(flops=200_000_000, bytes_accessed=int(moved), transcendentals=0),
        name=name,
    )(*operands)


def passed_along(block, axis, distance):
    devices = range(lax.axis_size(axis))
    route = [(i - distance, i) for i in devices if i - distance in devices]
    return lax.ppermute(block, axis, route)


def swapped(block):
    count = lax.axis_size("head")
    return lax.ppermute(block, "head", [(i, i ^ 1) for i in range(count)])


def on_device(
    tokens, w_query, w_key, w_value, w_outgate, w_gates, gate_bias, conv_query, conv_key,
    conv_value, out_gain, w_out, mix_gain, ffn_gain, w_gate, w_up, w_down, cotangent,
):
    seqs, size, width = tokens.shape
    heads = gate_bias.shape[1]
    pairs = seqs * heads
    units = w_gate.shape[1]
    count, me = lax.axis_size("seq"), lax.axis_index("seq")
    wide = heads * DK
    out_wide = heads * DV
    proj_wide = 2 * wide + out_wide

    halo = passed_along(tokens[:, size - HALO :], "seq", 1)
    x_ext = jnp.concatenate([halo, tokens], axis=1)
    gates_w = jnp.swapaxes(w_gates, 0, 1).reshape(width, 2 * heads)
    gates_w = jnp.pad(gates_w, ((0, 0), (0, LANES - 2 * heads)))
    bias = jnp.pad(gate_bias.reshape(1, 2 * heads), ((0, 0), (0, LANES - 2 * heads)))
    mix_row = mix_gain.reshape(1, width)
    ffn_row = ffn_gain.reshape(1, width)
    out_row = out_gain.reshape(1, DV)
    square = (seqs, heads, size, size)
    by_key = (seqs, heads, size, DK)
    by_value = (seqs, heads, size, DV)
    (
        mixed, proj, proj_g, gates, sums, inv, mapk, fresh, score, reach, local, decay, piece, low,
    ) = call(
        functools.partial(first_body, heads), "project_and_local", seqs, [x_ext],
        [mix_row, w_query, w_key, w_value, w_outgate, gates_w, bias, conv_query, conv_key, conv_value],
        [
            ((seqs, size, width), BF16), ((seqs, size + HALO, proj_wide), BF16),
            ((seqs, size, out_wide), F32), ((seqs, size, LANES), F32), ((seqs, size, LANES), F32),
            (square, F32), (by_key, F32), (by_value, F32), (square, F32), (by_key, F32),
            (by_value, F32), (square, F32), ((seqs, heads, DK, DK + DV), F32),
            ((seqs, heads, DK, DK + DV), BF16),
        ],
        flops=1e10,
    )

    ended = sums[:, size - 1, heads : 2 * heads].reshape(pairs)
    all_ended = lax.all_gather(ended, "seq")
    spans = []
    dists = []
    reach_by = 1
    while reach_by * 2 < count:
        dists.append(reach_by)
        reach_by *= 2
    for d in dists:
        spans.append(((me - d + 1, me), (me - 2 * d + 1, me - d)))
    spans.append(((me - reach_by, me - 1), (me, me - 1)))
    for d in dists:
        spans.append(((me, me + d - 1), (me + d, me + 2 * d - 1)))
    spans.append(((me + 1, me + reach_by), (me, me - 1)))
    low_end = jnp.stack([jnp.stack([a[0] for a in pair]) for pair in spans])[..., None]
    high_end = jnp.stack([jnp.stack([a[1] for a in pair]) for pair in spans])[..., None]
    index = jnp.arange(count)
    within = ((index >= low_end) & (index <= high_end)).astype(F32)
    scales = jnp.exp(jnp.sum(within[..., None] * all_ended, axis=2)).reshape(len(spans), 2 * pairs)

    piece = piece.reshape(pairs, DK, DK + DV)
    low = low.reshape(pairs, DK, DK + DV)
    back_maps = [piece[:, :, :DK]]
    back_low = low[:, :, :DK]
    joined, state_shape = (piece, (pairs, DK, DV))
    for level, d in enumerate(dists):
        got = passed_along(low, "seq", d)
        joined, low = small_call(
            functools.partial(join_body, pairs, level), "join", [joined, got], scales,
            [(piece.shape, F32), (piece.shape, BF16)],
        )
    near = passed_along(low, "seq", 1)
    far = passed_along(low[:, :, DK:], "seq", 1 + reach_by)
    (state,) = small_call(
        functools.partial(entry_body, pairs, len(dists)), "entry", [near, far], scales,
        [(state_shape, F32)],
    )
    state = state.reshape(seqs, heads, DK, DV)

    made, output, gated, attn = call(
        functools.partial(mixer_out_body, heads), "mixer_out", seqs,
        [state, fresh, mapk, reach, local, proj_g], [out_row, w_out],
        [
            (by_value, F32), ((seqs, size, out_wide), F32), ((seqs, size, out_wide), BF16),
            ((seqs, size, width), BF16),
        ],
        flops=1.5e9,
    )
    attn_other = swapped(attn)

    resid, normed, hidden, d_gu, down, d_norm = call(
        feed_body, "feed_forward", seqs, [tokens, attn, attn_other, cotangent],
        [ffn_row, w_gate, w_up, w_down],
        [
            ((seqs, size, width), F32), ((seqs, size, width), BF16), ((seqs, size, units), BF16),
            ((seqs, size, 2 * units), BF16), ((seqs, size, width), BF16),
            ((seqs, size, width), BF16),
        ],
        flops=1.2e10,
    )
    d_norm_other = swapped(d_norm)
    down_other = swapped(down)

    level0 = len(dists) + 1
    for level, d in enumerate(dists):
        got = passed_along(back_low, "seq", -d)
        new_map, back_low = small_call(
            functools.partial(map_body, pairs, level0 + level), "join_maps", [back_maps[-1], got],
            scales, [((pairs, DK, DK), F32), ((pairs, DK, DK), BF16)],
        )
        back_maps.append(new_map)
    near_map = passed_along(back_low, "seq", -1)

    d_resid, d_attn, d_out, d_pg, back, low, d_ffn_gain, d_out_gain = call(
        functools.partial(mixer_back_body, heads), "mixer_back", seqs,
        [resid, d_norm, d_norm_other, cotangent, output, proj_g, reach],
        [ffn_row, w_out, out_row],
        [
            ((seqs, size, width), F32), ((seqs, size, width), BF16), ((seqs, size, out_wide), F32),
            ((seqs, size, out_wide), BF16), ((seqs, heads, DK, DV), F32),
            ((seqs, heads, DK, DV), BF16),
        ],
        [((1, width), F32), ((1, DV), F32)],
        flops=1.5e9,
    )

    back = back.reshape(state_shape)
    low = low.reshape(state_shape)
    for level, d in enumerate(dists):
        got = passed_along(low, "seq", -d)
        back, low = small_call(
            functools.partial(back_body, pairs, level0 + level), "join_back",
            [back_maps[level], back, got], scales, [(state_shape, F32), (state_shape, BF16)],
        )
    near = passed_along(low, "seq", -1)
    far = passed_along(low, "seq", -1 - reach_by)
    (d_end,) = small_call(
        functools.partial(exit_body, pairs, level0 + len(dists)), "exit", [near_map, near, far],
        scales, [(state_shape, F32)],
    )
    d_end = d_end.reshape(seqs, heads, DK, DV)

    x_one, x_map, d_key, d_col, dext_q, dtap_q = call(
        functools.partial(early_body, heads), "delta_back_early", seqs,
        [proj, gates, sums, d_out, state, made, inv, score, decay], [conv_query, conv_key],
        [
            (by_value, F32), (by_key, F32), (by_key, F32), ((seqs, size, LANES), F32),
            ((seqs, size + HALO, wide), F32),
        ],
        [((CONV, wide), F32)],
        flops=3e9,
    )
    d_ext, d_gates, dtap_kv, d_bias = call(
        functools.partial(late_body, heads), "delta_back_late", seqs,
        [
            proj, gates, sums, d_end, state, made, decay, x_one, x_map, d_key, d_col, dext_q,
        ],
        [conv_key, conv_value],
        [((seqs, size + HALO, proj_wide), F32), ((seqs, size, LANES), BF16)],
        [((CONV, wide + out_wide), F32), ((1, LANES), F32)],
        flops=3e9,
    )
    edges = passed_along(d_ext[:, :HALO], "seq", -1)
    d_proj, d_mixed = call(
        input_back_body, "input_back", seqs, [d_ext, edges, d_pg, d_gates],
        [w_query, w_key, w_value, w_outgate, gates_w],
        [((seqs, size, proj_wide), BF16), ((seqs, size, width), BF16)],
        flops=1.7e9,
    )
    d_mixed_other = swapped(d_mixed)
    grad_input, d_mix_gain = call(
        last_body, "first_norm_back", seqs, [tokens, d_mixed, d_mixed_other, d_resid], [mix_row],
        [((seqs, size, width), F32)], [((1, width), F32)],
    )
    result = (resid + (down.astype(F32) + down_other.astype(F32))).astype(BF16)

    def weight_grad(left, right):
        return jnp.einsum("spa,spb->ab", left, right, preferred_element_type=F32).astype(BF16)

    def scattered(grad):
        return lax.psum_scatter(grad, "seq", scatter_dimension=0, tiled=True).astype(F32)

    gate_up = scattered(weight_grad(normed, d_gu))
    down_t = scattered(weight_grad(cotangent, hidden))
    out_t = scattered(weight_grad(d_attn, gated))
    right = jnp.concatenate([d_proj, d_pg, d_gates], axis=2)
    ins = scattered(weight_grad(mixed, right))

    out_gain_sum = d_out_gain + swapped(d_out_gain)
    small = jnp.concatenate(
        [
            dtap_q.reshape(-1), dtap_kv.reshape(-1), d_bias.reshape(-1), out_gain_sum.reshape(-1),
            d_mix_gain.reshape(-1), d_ffn_gain.reshape(-1),
        ]
    )
    small = lax.psum(small, "seq")
    cuts = [0]
    for length in (CONV * wide, CONV * (wide + out_wide), LANES, DV, width, width):
        cuts.append(cuts[-1] + length)
    pieces = [small[a:b] for a, b in zip(cuts[:-1], cuts[1:])]
    taps_kv = pieces[1].reshape(CONV, wide + out_wide)
    share = width // count
    g0 = proj_wide + out_wide
    grad_gates = jnp.swapaxes(ins[:, g0 : g0 + 2 * heads].reshape(share, 2, heads), 0, 1)
    return (
        result,
        grad_input,
        ins[:, :wide],
        ins[:, wide : 2 * wide],
        ins[:, 2 * wide : proj_wide],
        ins[:, proj_wide : proj_wide + out_wide],
        grad_gates,
        pieces[2][: 2 * heads].reshape(2, heads),
        pieces[0].reshape(CONV, wide),
        taps_kv[:, :wide],
        taps_kv[:, wide:],
        pieces[3],
        jnp.swapaxes(out_t, 0, 1),
        lax.dynamic_slice_in_dim(pieces[4], me * share, share),
        lax.dynamic_slice_in_dim(pieces[5], me * share, share),
        gate_up[:, :units],
        gate_up[:, units:],
        jnp.swapaxes(down_t, 0, 1),
    )


def solution(mesh):
    return jax.shard_map(
        on_device,
        mesh=mesh,
        in_specs=(
            P(None, "seq", None),
            P(None, "head"),
            P(None, "head"),
            P(None, "head"),
            P(None, "head"),
            P(None, None, "head"),
            P(None, "head"),
            P(None, "head"),
            P(None, "head"),
            P(None, "head"),
            P(),
            P("head", None),
            P(),
            P(),
            P(None, "head"),
            P(None, "head"),
            P("head", None),
            P(None, "seq", None),
        ),
        out_specs=(
            P(None, "seq", None),
            P(None, "seq", None),
            P("seq", "head"),
            P("seq", "head"),
            P("seq", "head"),
            P("seq", "head"),
            P(None, "seq", "head"),
            P(None, "head"),
            P(None, "head"),
            P(None, "head"),
            P(None, "head"),
            P(),
            P("head", "seq"),
            P("seq"),
            P("seq"),
            P("seq", "head"),
            P("seq", "head"),
            P("head", "seq"),
        ),
        check_vma=False,
    )
```

```python
import functools

import jax
import jax.numpy as jnp
from jax import lax
from jax.experimental import pallas as pl
from jax.experimental.pallas import tpu as pltpu
from jax.sharding import PartitionSpec as P

DK = 128
DV = 256
CONV = 4
HALO = 16
LANES = 128
SCALE = DK ** (-0.5)
F32 = jnp.float32
BF16 = jnp.bfloat16
NN = ((1,), (0,))
NT = ((1,), (1,))
TN = ((0,), (0,))
NOTE = 16
VMEM_LIMIT = 56 * 1024 * 1024


def dot(left, right, dims=NN):
    return lax.dot_general(
        left.astype(BF16), right.astype(BF16), (dims, ((), ())), preferred_element_type=F32
    )


def halves(field):
    high = field.astype(BF16)
    return high, (field - high.astype(F32)).astype(BF16)


def dot3(left, right, dims=NN):
    left_high, left_low = halves(left)
    right_high, right_low = halves(right)
    return dot(left_high, right_high, dims) + (
        dot(left_high, right_low, dims) + dot(left_low, right_high, dims)
    )


def ones_dot(ones, field):
    high, low = halves(field)
    lowest = field - high.astype(F32) - low.astype(F32)
    return dot(ones, high) + (dot(ones, low) + dot(ones, lowest))


def rows_cols(size):
    return (
        lax.broadcasted_iota(jnp.int32, (size, size), 0),
        lax.broadcasted_iota(jnp.int32, (size, size), 1),
    )


def log1p_small(value):
    shifted = 1.0 + value
    same = shifted == 1.0
    safe = jnp.where(same, 1.0, shifted - 1.0)
    return jnp.where(same, value, jnp.log(shifted) * (value / safe))


def log_sigmoid(value):
    return jnp.minimum(value, 0.0) - log1p_small(jnp.exp(-jnp.abs(value)))


def sigmoid(value):
    return 1.0 / (1.0 + jnp.exp(-value))


def row_sum(field):
    return jnp.sum(field, axis=-1, keepdims=True)


def inverse_unit(lowers, rows, cols):
    size = lowers[0].shape[0]
    same = (rows // 16) == (cols // 16)
    eye = (rows == cols).astype(F32)
    powers = [jnp.where(same, -lower, 0.0) for lower in lowers]
    inverses = [eye + power for power in powers]
    for _ in range(3):
        powers = [dot3(power, power) for power in powers]
        inverses = [inv + dot3(inv, power) for inv, power in zip(inverses, powers)]
    block = 16
    while block * 2 <= size:
        inside = ((rows // (2 * block)) == (cols // (2 * block))) & (
            (rows // block) != (cols // block)
        )
        parts = [
            dot3(jnp.where(inside, lower, 0.0), inv) for lower, inv in zip(lowers, inverses)
        ]
        inverses = [inv - dot3(inv, part) for inv, part in zip(inverses, parts)]
        block *= 2
    return inverses


def conv_pre(extended, taps):
    total = taps[CONV - 1 : CONV] * extended
    for offset in range(CONV - 1):
        total = total + taps[offset : offset + 1] * pltpu.roll(extended, CONV - 1 - offset, 0)
    return total[HALO:]


def silu(value):
    return value * sigmoid(value)


def silu_slope(value):
    gate = sigmoid(value)
    return gate * (1.0 + value * (1.0 - gate))


def unit(field):
    inverse = lax.rsqrt(row_sum(field * field) + 1e-06)
    return field * inverse, inverse


def first_body(
    heads, x_ref, gain_ref, wq_ref, wk_ref, wv_ref, wg_ref, wgates_ref, bias_ref, cq_ref, ck_ref,
    cv_ref, proj_ref, pg_ref, gates_ref, sums_ref, inv_ref, mapk_ref, fresh_ref,
    score_ref, reach_ref, local_ref, decay_ref, piece_ref, low_ref, map_ref, maplow_ref, log_ref,
    turned_ref,
):
    x = x_ref[0].astype(F32)
    mixed = x * lax.rsqrt(jnp.mean(x * x, axis=-1, keepdims=True) + 1e-06) * gain_ref[...]
    mixed = mixed.astype(BF16)
    main = mixed[HALO:]
    turned_ref[...] = jnp.transpose(main)
    proj_q = dot(mixed, wq_ref[...]).astype(BF16)
    proj_k = dot(mixed, wk_ref[...]).astype(BF16)
    proj_v = dot(mixed, wv_ref[...]).astype(BF16)
    wide = heads * DK
    proj_ref[0, :, :wide] = proj_q
    proj_ref[0, :, wide : 2 * wide] = proj_k
    proj_ref[0, :, 2 * wide :] = proj_v
    pg_ref[0] = dot(main, wg_ref[...])
    gates = dot(main, wgates_ref[...]) + bias_ref[...]
    gates_ref[0] = gates
    size = main.shape[0]
    rows, cols = rows_cols(size)
    lower = rows >= cols
    strict = rows > cols
    sums = ones_dot(lower.astype(BF16), log_sigmoid(gates))
    sums_ref[0] = sums
    sums_t = jnp.transpose(sums)
    conv_q = silu(conv_pre(proj_q.astype(F32), cq_ref[...]))
    conv_k = silu(conv_pre(proj_k.astype(F32), ck_ref[...]))
    conv_v = silu(conv_pre(proj_v.astype(F32), cv_ref[...]))
    each = range(heads)
    queries = [unit(conv_q[:, h * DK : (h + 1) * DK])[0] * SCALE for h in each]
    keys = [unit(conv_k[:, h * DK : (h + 1) * DK])[0] for h in each]
    values = [conv_v[:, h * DV : (h + 1) * DV] for h in each]
    beta = [sigmoid(gates[:, h : h + 1]) for h in each]
    total = [sums[:, heads + h : heads + h + 1] for h in each]
    decay = [
        jnp.where(
            lower, jnp.exp(jnp.minimum(total[h] - sums_t[heads + h : heads + h + 1, :], 0.0)), 0.0
        )
        for h in each
    ]
    scaled = [beta[h] * keys[h] for h in each]
    lowers = [jnp.where(strict, dot3(keys[h], scaled[h], NT) * decay[h], 0.0) for h in each]
    inverses = inverse_unit(lowers, rows, cols)
    growth = [jnp.exp(total[h]) for h in each]
    last = [total[h][size - 1 : size] for h in each]
    tail = [jnp.exp(last[h] - total[h]) * scaled[h] for h in each]
    mapk = [dot3(inverses[h], growth[h] * keys[h]) for h in each]
    fresh = [dot3(inverses[h], values[h]) for h in each]
    scores = [dot3(queries[h], scaled[h], NT) * decay[h] for h in each]
    moved = [-dot3(tail[h], mapk[h], TN) for h in each]
    shift = [dot3(tail[h], fresh[h], TN) for h in each]
    reach = [growth[h] * queries[h] - dot3(scores[h], mapk[h]) for h in each]
    local = [dot3(scores[h], fresh[h]) for h in each]
    for h in each:
        piece_ref[0, h, :, :DK] = moved[h]
        piece_ref[0, h, :, DK:] = shift[h]
        map_ref[0, h] = moved[h]
        note = log_rows(last[h])
        log_ref[0, h] = jnp.broadcast_to(last[h], (8, LANES))
        maplow_ref[0, h, :DK] = moved[h].astype(BF16)
        maplow_ref[0, h, DK:] = note
        low_ref[0, h, :DK, :DK] = moved[h].astype(BF16)
        low_ref[0, h, :DK, DK:] = shift[h].astype(BF16)
        low_ref[0, h, DK:] = jnp.concatenate([note] * (1 + DV // DK), axis=1)
        inv_ref[0, h] = inverses[h]
        mapk_ref[0, h] = mapk[h]
        fresh_ref[0, h] = fresh[h]
        score_ref[0, h] = scores[h]
        reach_ref[0, h] = reach[h]
        local_ref[0, h] = local[h]
        decay_ref[0, h] = decay[h]


def log_rows(log):
    log = jnp.broadcast_to(log, (1, LANES))
    high = log.astype(BF16).astype(F32)
    middle = (log - high).astype(BF16).astype(F32)
    rest = log - high - middle
    place = lax.broadcasted_iota(jnp.int32, (NOTE, LANES), 0)
    zero = jnp.zeros((NOTE, LANES), F32)
    rows = jnp.where(place == 0, high, jnp.where(place == 1, middle, jnp.where(place == 2, rest, zero)))
    return rows.astype(BF16)


def log_of(rows):
    return jnp.sum(rows.astype(F32), axis=0, keepdims=True)


def join_body(pairs, last, piece_ref, log_ref, got_ref, out_ref, newlog_ref, low_ref, *far_ref):
    wide = 1 + DV // DK
    for p in range(pairs):
        own = piece_ref[p]
        got_low = got_ref[p, :DK]
        got = got_low.astype(F32)
        own_log = log_ref[p, :1]
        got_log = log_of(got_ref[p, DK:, :LANES])
        mine = jnp.concatenate([jnp.exp(own_log)] * wide, axis=1)
        high, low = halves(own[:, :DK])
        moved = dot(high, got_low) + dot(low, got_low) + mine * got
        map_part = moved[:, :DK] + jnp.exp(got_log) * own[:, :DK]
        shift_part = moved[:, DK:] + own[:, DK:]
        new_log = own_log + got_log
        out_ref[p, :, :DK] = map_part
        out_ref[p, :, DK:] = shift_part
        newlog_ref[p] = jnp.broadcast_to(new_log, (8, LANES))
        low_ref[p, :DK, :DK] = map_part.astype(BF16)
        low_ref[p, :DK, DK:] = shift_part.astype(BF16)
        low_ref[p, DK:] = jnp.concatenate([log_rows(new_log)] * wide, axis=1)
        if last:
            far_ref[0][p] = shift_part.astype(BF16)


def map_body(pairs, own_ref, log_ref, got_ref, out_ref, newlog_ref, low_ref):
    for p in range(pairs):
        own = own_ref[p]
        got_low = got_ref[p, :DK]
        own_log = log_ref[p, :1]
        got_log = log_of(got_ref[p, DK:])
        high, low = halves(own)
        out = dot(got_low, high) + dot(got_low, low)
        out = out + jnp.exp(got_log) * own + jnp.exp(own_log) * got_low.astype(F32)
        new_log = own_log + got_log
        out_ref[p] = out
        newlog_ref[p] = jnp.broadcast_to(new_log, (8, LANES))
        low_ref[p, :DK] = out.astype(BF16)
        low_ref[p, DK:] = log_rows(new_log)


def entry_body(pairs, near_ref, far_ref, out_ref):
    for p in range(pairs):
        far = far_ref[p]
        scale = jnp.exp(log_of(near_ref[p, DK:, DK:]))
        moved = dot(near_ref[p, :DK, :DK], far) + scale * far.astype(F32)
        out_ref[p] = moved + near_ref[p, :DK, DK:].astype(F32)


def back_body(pairs, map_ref, log_ref, own_ref, got_ref, out_ref, low_ref):
    for p in range(pairs):
        got = got_ref[p]
        high, low = halves(map_ref[p])
        scale = jnp.concatenate([jnp.exp(log_ref[p, :1])] * (DV // DK), axis=1)
        out = own_ref[p] + dot(high, got, TN) + dot(low, got, TN) + scale * got.astype(F32)
        out_ref[p] = out
        low_ref[p] = out.astype(BF16)


def exit_body(pairs, map_ref, near_ref, far_ref, out_ref):
    for p in range(pairs):
        far = far_ref[p]
        scale = jnp.concatenate([jnp.exp(log_of(map_ref[p, DK:]))] * (DV // DK), axis=1)
        moved = dot(map_ref[p, :DK], far, TN) + scale * far.astype(F32)
        out_ref[p] = near_ref[p].astype(F32) + moved


def mixer_out_body(
    heads, state_ref, fresh_ref, mapk_ref, reach_ref, local_ref, pg_ref, gain_ref, wout_ref,
    made_ref, output_ref, gated_ref, attn_ref,
):
    for h in range(heads):
        state = state_ref[0, h]
        made_ref[0, h] = fresh_ref[0, h] - dot3(mapk_ref[0, h], state)
        output = local_ref[0, h] + dot3(reach_ref[0, h], state)
        output_ref[0, :, h * DV : (h + 1) * DV] = output
        scale = lax.rsqrt(jnp.mean(output * output, axis=-1, keepdims=True) + 1e-05)
        gate = pg_ref[0, :, h * DV : (h + 1) * DV]
        gated_ref[0, :, h * DV : (h + 1) * DV] = (
            output * scale * gain_ref[...] * silu(gate)
        ).astype(BF16)
    attn_ref[0] = dot(gated_ref[0], wout_ref[...]).astype(BF16)


def feed_body(
    x_ref, mine_ref, other_ref, cot_ref, gain_ref, wgate_ref, wup_ref, wdown_ref, resid_ref,
    hidden_ref, dgu_ref, down_ref, dnorm_ref, normed_ref, cot_turned_ref,
):
    units = wgate_ref.shape[1]
    attn = mine_ref[0].astype(F32) + other_ref[0].astype(F32)
    resid = x_ref[0].astype(F32) + attn
    resid_ref[0] = resid
    normed = resid * lax.rsqrt(jnp.mean(resid * resid, axis=-1, keepdims=True) + 1e-06)
    normed = (normed * gain_ref[...]).astype(BF16)
    normed_ref[...] = jnp.transpose(normed)
    cot_turned_ref[...] = jnp.transpose(cot_ref[0])
    gate = dot(normed, wgate_ref[...])
    up = dot(normed, wup_ref[...])
    d_hidden = dot(cot_ref[0], wdown_ref[...], NT)
    sig = sigmoid(gate)
    active = gate * sig
    hidden = (active * up).astype(BF16)
    hidden_ref[0] = hidden
    d_gate = (d_hidden * up * (sig + active * (1.0 - sig))).astype(BF16)
    d_up = (d_hidden * active).astype(BF16)
    dgu_ref[0, :, :units] = d_gate
    dgu_ref[0, :, units:] = d_up
    down_ref[0] = dot(hidden, wdown_ref[...]).astype(BF16)
    dnorm_ref[0] = (dot(d_gate, wgate_ref[...], NT) + dot(d_up, wup_ref[...], NT)).astype(BF16)


def mixer_back_body(
    heads, resid_ref, mine_ref, other_ref, cot_ref, output_ref, pg_ref, reach_ref, gain_ref,
    wout_ref, ogain_ref, dresid_ref, dout_ref, dpg_ref, back_ref, low_ref, dattn_ref, dgain_ref,
    dogain_ref,
):
    step = pl.program_id(0)
    resid = resid_ref[0]
    inverse = lax.rsqrt(jnp.mean(resid * resid, axis=-1, keepdims=True) + 1e-06)
    unit_resid = resid * inverse
    d_normed = mine_ref[0].astype(F32) + other_ref[0].astype(F32)
    d_gain = jnp.sum(d_normed * unit_resid, axis=0, keepdims=True)
    d_unit = d_normed * gain_ref[...]
    d_resid = inverse * (
        d_unit - unit_resid * jnp.mean(d_unit * unit_resid, axis=-1, keepdims=True)
    )
    d_resid = d_resid + cot_ref[0].astype(F32)
    dresid_ref[0] = d_resid
    d_attn = d_resid.astype(BF16)
    dattn_ref[...] = jnp.transpose(d_attn)
    d_gated = dot(d_attn, wout_ref[...], NT)
    d_ogain = jnp.zeros((1, DV), F32)
    for h in range(heads):
        part = slice(h * DV, (h + 1) * DV)
        output = output_ref[0, :, part]
        inverse = lax.rsqrt(jnp.mean(output * output, axis=-1, keepdims=True) + 1e-05)
        unit_out = output * inverse
        gate = pg_ref[0, :, part]
        grad = d_gated[:, part]
        active = silu(gate)
        d_ogain = d_ogain + jnp.sum(grad * unit_out * active, axis=0, keepdims=True)
        dpg_ref[0, :, part] = (grad * unit_out * ogain_ref[...] * silu_slope(gate)).astype(BF16)
        d_unit = grad * ogain_ref[...] * active
        d_out = inverse * (d_unit - unit_out * jnp.mean(d_unit * unit_out, axis=-1, keepdims=True))
        dout_ref[0, :, part] = d_out
        back = dot3(reach_ref[0, h], d_out, TN)
        back_ref[0, h] = back
        low_ref[0, h] = back.astype(BF16)

    @pl.when(step == 0)
    def _():
        dgain_ref[...] = d_gain
        dogain_ref[...] = d_ogain

    @pl.when(step > 0)
    def _():
        dgain_ref[...] += d_gain
        dogain_ref[...] += d_ogain


def conv_back(grad, extended, taps, pre):
    d_pre = grad * silu_slope(pre)
    padded = jnp.concatenate([jnp.zeros((HALO, d_pre.shape[1]), F32), d_pre], axis=0)
    length = padded.shape[0]
    d_ext = taps[CONV - 1 : CONV] * padded
    d_taps = []
    for offset in range(CONV):
        back = CONV - 1 - offset
        if back:
            d_ext = d_ext + taps[offset : offset + 1] * pltpu.roll(padded, length - back, 0)
            shifted = pltpu.roll(extended, back, 0)
        else:
            shifted = extended
        d_taps.append(jnp.sum(padded * shifted, axis=0, keepdims=True))
    return d_ext, jnp.concatenate(d_taps, axis=0)


def early_body(
    heads, proj_ref, gates_ref, sums_ref, dout_ref, state_ref, made_ref, inv_ref, score_ref,
    decay_ref, cq_ref, ck_ref, xone_ref, xmap_ref, dkey_ref, dcol_ref, dext_ref, dtap_ref,
):
    step = pl.program_id(0)
    wide = heads * DK
    ext_q = proj_ref[0, :, :wide].astype(F32)
    ext_k = proj_ref[0, :, wide : 2 * wide].astype(F32)
    pre_q = conv_pre(ext_q, cq_ref[...])
    conv_q = silu(pre_q)
    conv_k = silu(conv_pre(ext_k, ck_ref[...]))
    gates = gates_ref[0]
    sums = sums_ref[0]
    size = gates.shape[0]
    each = range(heads)
    units = [unit(conv_q[:, h * DK : (h + 1) * DK]) for h in each]
    queries = [units[h][0] * SCALE for h in each]
    keys = [unit(conv_k[:, h * DK : (h + 1) * DK])[0] for h in each]
    beta = [sigmoid(gates[:, h : h + 1]) for h in each]
    total = [sums[:, heads + h : heads + h + 1] for h in each]
    growth = [jnp.exp(total[h]) for h in each]
    tail = [jnp.exp(total[h][size - 1 : size] - total[h]) * beta[h] * keys[h] for h in each]
    d_out = [dout_ref[0, :, h * DV : (h + 1) * DV] for h in each]
    d_made = [dot3(score_ref[0, h], d_out[h], TN) for h in each]
    d_score = [dot3(d_out[h], made_ref[0, h], NT) * decay_ref[0, h] for h in each]
    d_query = [
        dot3(d_score[h], beta[h] * keys[h]) + dot3(growth[h] * d_out[h], state_ref[0, h], NT)
        for h in each
    ]
    d_key = [dot3(d_score[h], queries[h], TN) for h in each]
    x_one = [dot3(inv_ref[0, h], d_made[h], TN) for h in each]
    x_map = [dot3(inv_ref[0, h], tail[h], TN) for h in each]
    lanes = lax.broadcasted_iota(jnp.int32, (size, LANES), 1)
    cols = jnp.zeros((size, LANES), F32)
    grads = []
    for h in each:
        xone_ref[0, h] = x_one[h]
        xmap_ref[0, h] = x_map[h]
        dkey_ref[0, h] = beta[h] * d_key[h]
        key_sum = row_sum(d_key[h] * keys[h])
        cols = cols + jnp.where(lanes == h, key_sum, 0.0)
        d_total = row_sum(d_query[h] * queries[h]) - beta[h] * key_sum
        cols = cols + jnp.where(lanes == heads + h, d_total, 0.0)
        unit_q, inverse = units[h]
        d_unit = d_query[h] * SCALE
        grads.append(inverse * (d_unit - unit_q * row_sum(d_unit * unit_q)))
    dcol_ref[0] = cols
    d_ext, d_taps = conv_back(jnp.concatenate(grads, axis=1), ext_q, cq_ref[...], pre_q)
    dext_ref[0] = d_ext

    @pl.when(step == 0)
    def _():
        dtap_ref[...] = d_taps

    @pl.when(step > 0)
    def _():
        dtap_ref[...] += d_taps


def late_body(
    heads, proj_ref, gates_ref, sums_ref, dend_ref, state_ref, made_ref, decay_ref, xone_ref,
    xmap_ref, dkey_ref, dcol_ref, dextq_ref, ck_ref, cv_ref, dext_ref, dgates_ref, dtap_ref, dbias_ref,
):
    step = pl.program_id(0)
    wide = heads * DK
    ext_k = proj_ref[0, :, wide : 2 * wide].astype(F32)
    ext_v = proj_ref[0, :, 2 * wide :].astype(F32)
    pre_k = conv_pre(ext_k, ck_ref[...])
    pre_v = conv_pre(ext_v, cv_ref[...])
    conv_k = silu(pre_k)
    gates = gates_ref[0]
    sums = sums_ref[0]
    size = gates.shape[0]
    rows, cols = rows_cols(size)
    strict = rows > cols
    each = range(heads)
    units = [unit(conv_k[:, h * DK : (h + 1) * DK]) for h in each]
    keys = [units[h][0] for h in each]
    beta = [sigmoid(gates[:, h : h + 1]) for h in each]
    total = [sums[:, heads + h : heads + h + 1] for h in each]
    growth = [jnp.exp(total[h]) for h in each]
    left = [jnp.exp(total[h][size - 1 : size] - total[h]) for h in each]
    d_end = [dend_ref[0, h] for h in each]
    made = [made_ref[0, h] for h in each]
    state = [state_ref[0, h] for h in each]
    d_rhs = [xone_ref[0, h] + dot3(xmap_ref[0, h], d_end[h]) for h in each]
    d_tail = [dot3(made[h], d_end[h], NT) for h in each]
    d_lower = [
        jnp.where(strict, -dot3(d_rhs[h], made[h], NT) * decay_ref[0, h], 0.0) for h in each
    ]
    d_plain = [
        dot3(d_lower[h], beta[h] * keys[h]) - dot3(growth[h] * d_rhs[h], state[h], NT) for h in each
    ]
    d_turned = [dot3(d_lower[h], keys[h], TN) for h in each]
    lanes = lax.broadcasted_iota(jnp.int32, (size, LANES), 1)
    places = lax.broadcasted_iota(jnp.int32, (size, 1), 0)
    d_col = dcol_ref[0]
    grads_k = []
    for h in each:
        turned = row_sum(d_turned[h] * keys[h])
        tails = row_sum(d_tail[h] * keys[h])
        tail_weight = left[h] * beta[h]
        d_key = d_plain[h] + beta[h] * d_turned[h] + tail_weight * d_tail[h] + dkey_ref[0, h]
        d_total = row_sum(d_plain[h] * keys[h]) - beta[h] * turned - tail_weight * tails
        ended = jnp.sum(tail_weight * tails, axis=0, keepdims=True)
        whole = jnp.sum(row_sum(d_end[h] * state[h]), axis=0, keepdims=True)
        ended = ended + growth[h][size - 1 : size] * whole
        d_total = d_total + jnp.where(places == size - 1, ended, 0.0)
        d_col = d_col + jnp.where(lanes == h, turned + left[h] * tails, 0.0)
        d_col = d_col + jnp.where(lanes == heads + h, d_total, 0.0)
        unit_k, inverse = units[h]
        grads_k.append(inverse * (d_key - unit_k * row_sum(d_key * unit_k)))
    upper = (rows <= cols).astype(BF16)
    d_decay = ones_dot(upper, d_col)
    rate = sigmoid(gates)
    d_gates = jnp.where(
        lanes < heads, d_col * rate * (1.0 - rate), d_decay / (1.0 + jnp.exp(gates))
    )
    d_gates = jnp.where(lanes < 2 * heads, d_gates, 0.0)
    dgates_ref[0] = d_gates.astype(BF16)
    d_bias = jnp.sum(d_gates, axis=0, keepdims=True)
    dext_k, dtaps_k = conv_back(jnp.concatenate(grads_k, axis=1), ext_k, ck_ref[...], pre_k)
    dext_v, dtaps_v = conv_back(jnp.concatenate(d_rhs, axis=1), ext_v, cv_ref[...], pre_v)
    dext_ref[0, :, :wide] = dextq_ref[0]
    dext_ref[0, :, wide : 2 * wide] = dext_k
    dext_ref[0, :, 2 * wide :] = dext_v

    @pl.when(step == 0)
    def _():
        dtap_ref[:, :wide] = dtaps_k
        dtap_ref[:, wide:] = dtaps_v
        dbias_ref[...] = d_bias

    @pl.when(step > 0)
    def _():
        dtap_ref[:, :wide] += dtaps_k
        dtap_ref[:, wide:] += dtaps_v
        dbias_ref[...] += d_bias


def input_back_body(
    dext_ref, edge_ref, dpg_ref, dgates_ref, x_ref, wq_ref, wk_ref, wv_ref, wg_ref, wgates_ref,
    dproj_ref, dmixed_ref, dgain_ref,
):
    step = pl.program_id(0)
    wide = wq_ref.shape[1]
    own = dext_ref[0, HALO:]
    size = own.shape[0]
    d_proj = jnp.concatenate([own[: size - HALO], own[size - HALO :] + edge_ref[0]], axis=0)
    d_proj = d_proj.astype(BF16)
    dproj_ref[0] = d_proj
    d_mixed = dot(d_proj[:, :wide], wq_ref[...], NT)
    d_mixed = d_mixed + dot(d_proj[:, wide : 2 * wide], wk_ref[...], NT)
    d_mixed = d_mixed + dot(d_proj[:, 2 * wide :], wv_ref[...], NT)
    d_mixed = d_mixed + dot(dpg_ref[0], wg_ref[...], NT)
    d_mixed = d_mixed + dot(dgates_ref[0], wgates_ref[...], NT)
    dmixed_ref[0] = d_mixed.astype(BF16)
    x = x_ref[0].astype(F32)
    unit_x = x * lax.rsqrt(jnp.mean(x * x, axis=-1, keepdims=True) + 1e-06)
    d_gain = jnp.sum(d_mixed * unit_x, axis=0, keepdims=True)

    @pl.when(step == 0)
    def _():
        dgain_ref[...] = d_gain

    @pl.when(step > 0)
    def _():
        dgain_ref[...] += d_gain


def last_body(x_ref, mine_ref, other_ref, dresid_ref, gain_ref, grad_ref):
    x = x_ref[0].astype(F32)
    inverse = lax.rsqrt(jnp.mean(x * x, axis=-1, keepdims=True) + 1e-06)
    unit_x = x * inverse
    d_mixed = mine_ref[0].astype(F32) + other_ref[0].astype(F32)
    d_unit = d_mixed * gain_ref[...]
    back = inverse * (d_unit - unit_x * jnp.mean(d_unit * unit_x, axis=-1, keepdims=True))
    grad_ref[0] = dresid_ref[0] + back


def weight_body(terms, first, blocks, lefts, index_ref, *refs):
    left_refs, right_refs = refs[:lefts], refs[lefts:-2]
    out_ref, held = refs[-2:]
    share = left_refs[0].shape[1]
    for number, left_ref in enumerate(left_refs):
        for place in range(blocks):
            held[number, place * share : (place + 1) * share] = left_ref[index_ref[first + place]]
    at = 0
    for left, right, begin, width in terms:
        product = dot(held[left], right_refs[right][:, begin : begin + width])
        out_ref[:, at : at + width] = product.astype(out_ref.dtype)
        at += width


def by_seq(shape):
    rest = len(shape) - 1
    return pl.BlockSpec((1,) + tuple(shape[1:]), lambda s: (s,) + (0,) * rest)


def whole(shape):
    rest = len(shape)
    return pl.BlockSpec(tuple(shape), lambda s: (0,) * rest)


def call(body, name, seqs, parts, shared, outs, sums=(), turned=(), flops=0):
    operands = list(parts) + list(shared)
    listed = list(outs) + list(turned) + list(sums)
    out_shape = [jax.ShapeDtypeStruct(shape, kind) for shape, kind in listed]
    moved = sum(a.size * a.dtype.itemsize for a in operands + out_shape)
    return pl.pallas_call(
        body,
        grid=(seqs,),
        in_specs=[by_seq(a.shape) for a in parts] + [whole(a.shape) for a in shared],
        out_specs=[by_seq(shape) for shape, _ in outs]
        + [pl.BlockSpec((shape[0], shape[1] // seqs), lambda s: (0, s)) for shape, _ in turned]
        + [whole(shape) for shape, _ in sums],
        out_shape=out_shape,
        compiler_params=pltpu.CompilerParams(vmem_limit_bytes=VMEM_LIMIT),
        cost_estimate=pl.CostEstimate(flops=int(flops), bytes_accessed=int(moved), transcendentals=0),
        name=name,
    )(*operands)


def small_call(body, name, arrays, outs):
    out_shape = [jax.ShapeDtypeStruct(shape, kind) for shape, kind in outs]
    moved = sum(a.size * a.dtype.itemsize for a in list(arrays) + out_shape)
    return pl.pallas_call(
        body,
        in_specs=[pl.BlockSpec(memory_space=pltpu.VMEM)] * len(arrays),
        out_specs=[pl.BlockSpec(memory_space=pltpu.VMEM)] * len(outs),
        out_shape=out_shape,
        compiler_params=pltpu.CompilerParams(vmem_limit_bytes=VMEM_LIMIT),
        cost_estimate=pl.CostEstimate(flops=200_000_000, bytes_accessed=int(moved), transcendentals=0),
        name=name,
    )(*arrays)


def weight_call(name, index, lefts, rights, terms, first, blocks, kind):
    _, share, tokens = lefts[0].shape
    columns = sum(width for _, _, _, width in terms)
    out_shape = jax.ShapeDtypeStruct((blocks * share, columns), kind)
    operands = list(lefts) + list(rights)
    moved = sum(a.size * a.dtype.itemsize for a in operands + [out_shape])
    return pl.pallas_call(
        functools.partial(weight_body, terms, first, blocks, len(lefts)),
        in_specs=[pl.BlockSpec(memory_space=pltpu.SMEM)]
        + [pl.BlockSpec(memory_space=pltpu.VMEM)] * len(operands),
        out_specs=pl.BlockSpec(memory_space=pltpu.VMEM),
        out_shape=out_shape,
        scratch_shapes=[pltpu.VMEM((len(lefts), blocks * share, tokens), BF16)],
        compiler_params=pltpu.CompilerParams(vmem_limit_bytes=VMEM_LIMIT),
        cost_estimate=pl.CostEstimate(
            flops=2 * blocks * share * tokens * columns, bytes_accessed=int(moved), transcendentals=0
        ),
        name=name,
    )(index, *operands)


def halving_order(count, first):
    bits = list(range(count.bit_length() - 1))
    return bits[first : first + 1] + bits[:first] + bits[first + 1 :]


def block_index(order, me):
    count = 1 << len(order)
    moved = [
        sum(((place >> (len(order) - 1 - step)) & 1) << bit for step, bit in enumerate(order))
        for place in range(count)
    ]
    return jnp.bitwise_xor(jnp.array(moved, jnp.int32), me)


def traded(block, bit):
    count = lax.axis_size("seq")
    return lax.ppermute(block, "seq", [(i, i ^ (1 << bit)) for i in range(count)])


def halved(send, keep, order):
    for step, bit in enumerate(order):
        got = traded(send, bit).astype(F32)
        if step + 1 < len(order):
            half = keep.shape[0] // 2
            send = (keep[half:] + got[half:]).astype(BF16)
            keep = keep[:half] + got[:half]
    return keep + got


def passed_along(block, axis, distance):
    devices = range(lax.axis_size(axis))
    route = [(i - distance, i) for i in devices if i - distance in devices]
    return lax.ppermute(block, axis, route)


def swapped(block):
    count = lax.axis_size("head")
    return lax.ppermute(block, "head", [(i, i ^ 1) for i in range(count)])


def on_device(
    tokens, w_query, w_key, w_value, w_outgate, w_gates, gate_bias, conv_query, conv_key,
    conv_value, out_gain, w_out, mix_gain, ffn_gain, w_gate, w_up, w_down, cotangent,
):
    seqs, size, width = tokens.shape
    heads = gate_bias.shape[1]
    pairs = seqs * heads
    units = w_gate.shape[1]
    count, me = lax.axis_size("seq"), lax.axis_index("seq")
    wide = heads * DK
    out_wide = heads * DV
    proj_wide = 2 * wide + out_wide

    halo = passed_along(tokens[:, size - HALO :], "seq", 1)
    x_ext = jnp.concatenate([halo, tokens], axis=1)
    gates_w = jnp.swapaxes(w_gates, 0, 1).reshape(width, 2 * heads)
    gates_w = jnp.pad(gates_w, ((0, 0), (0, LANES - 2 * heads)))
    bias = jnp.pad(gate_bias.reshape(1, 2 * heads), ((0, 0), (0, LANES - 2 * heads)))
    mix_row = mix_gain.reshape(1, width)
    ffn_row = ffn_gain.reshape(1, width)
    out_row = out_gain.reshape(1, DV)
    square = (seqs, heads, size, size)
    by_key = (seqs, heads, size, DK)
    by_value = (seqs, heads, size, DV)
    tokens_here = seqs * size
    order_a, order_b = halving_order(count, 0), halving_order(count, 1)
    index_a, index_b = block_index(order_a, me), block_index(order_b, me)
    turned_shape = (width, tokens_here)
    share = width // count

    def in_blocks(turned):
        return turned.reshape(count, share, tokens_here)

    def flat(field):
        return field.reshape(tokens_here, field.shape[2])

    (
        proj, proj_g, gates, sums, inv, mapk, fresh, score, reach, local, decay, piece, low,
        back_map, back_low, log, mixed_t,
    ) = call(
        functools.partial(first_body, heads), "project_and_local", seqs, [x_ext],
        [mix_row, w_query, w_key, w_value, w_outgate, gates_w, bias, conv_query, conv_key, conv_value],
        [
            ((seqs, size + HALO, proj_wide), BF16),
            ((seqs, size, out_wide), F32), ((seqs, size, LANES), F32), ((seqs, size, LANES), F32),
            (square, F32), (by_key, F32), (by_value, F32), (square, F32), (by_key, F32),
            (by_value, F32), (square, F32), ((seqs, heads, DK, DK + DV), F32),
            ((seqs, heads, DK + NOTE, DK + DV), BF16), ((seqs, heads, DK, DK), F32),
            ((seqs, heads, DK + NOTE, DK), BF16), ((seqs, heads, 8, LANES), F32),
        ],
        turned=[(turned_shape, BF16)],
        flops=1e10,
    )

    piece = piece.reshape(pairs, DK, DK + DV)
    low = low.reshape(pairs, DK + NOTE, DK + DV)
    log = log.reshape(pairs, 8, LANES)
    back_maps = [back_map.reshape(pairs, DK, DK)]
    back_low = back_low.reshape(pairs, DK + NOTE, DK)
    back_logs = [log]
    state_shape = (pairs, DK, DV)
    dists = []
    reach_by = 1
    while reach_by * 2 < count:
        dists.append(reach_by)
        reach_by *= 2
    for level, d in enumerate(dists):
        got = passed_along(low, "seq", d)
        got_back = passed_along(back_low, "seq", -d)
        if level:
            got, _ = lax.optimization_barrier((got, back_low))
        last = level + 1 == len(dists)
        outs = [(piece.shape, F32), (log.shape, F32), (low.shape, BF16)]
        if last:
            outs.append((state_shape, BF16))
        piece, log, low, *far = small_call(
            functools.partial(join_body, pairs, last), "join", [piece, log, got], outs
        )
        new_map, new_log, back_low = small_call(
            functools.partial(map_body, pairs), "join_maps", [back_maps[-1], back_logs[-1], got_back],
            [(back_maps[0].shape, F32), (log.shape, F32), (back_low.shape, BF16)],
        )
        back_maps.append(new_map)
        back_logs.append(new_log)
    near = passed_along(low, "seq", 1)
    far = passed_along(far[0], "seq", 1 + reach_by)
    near_map = passed_along(back_low, "seq", -1)
    far, _ = lax.optimization_barrier((far, back_low))
    (state,) = small_call(
        functools.partial(entry_body, pairs), "entry", [near, far], [(state_shape, F32)]
    )
    state = state.reshape(seqs, heads, DK, DV)

    made, output, gated, attn = call(
        functools.partial(mixer_out_body, heads), "mixer_out", seqs,
        [state, fresh, mapk, reach, local, proj_g], [out_row, w_out],
        [
            (by_value, F32), ((seqs, size, out_wide), F32), ((seqs, size, out_wide), BF16),
            ((seqs, size, width), BF16),
        ],
        flops=1.5e9,
    )
    attn_other = swapped(attn)

    resid, hidden, d_gu, down, d_norm, normed_t, cot_t = call(
        feed_body, "feed_forward", seqs, [tokens, attn, attn_other, cotangent],
        [ffn_row, w_gate, w_up, w_down],
        [
            ((seqs, size, width), F32), ((seqs, size, units), BF16),
            ((seqs, size, 2 * units), BF16), ((seqs, size, width), BF16),
            ((seqs, size, width), BF16),
        ],
        turned=[(turned_shape, BF16), (turned_shape, BF16)],
        flops=1.2e10,
    )
    d_norm_other = swapped(d_norm)
    down_other = swapped(down)

    d_resid, d_out, d_pg, back, low, d_attn_t, d_ffn_gain, d_out_gain = call(
        functools.partial(mixer_back_body, heads), "mixer_back", seqs,
        [resid, d_norm, d_norm_other, cotangent, output, proj_g, reach],
        [ffn_row, w_out, out_row],
        [
            ((seqs, size, width), F32), ((seqs, size, out_wide), F32),
            ((seqs, size, out_wide), BF16), ((seqs, heads, DK, DV), F32),
            ((seqs, heads, DK, DV), BF16),
        ],
        [((1, width), F32), ((1, DV), F32)],
        turned=[(turned_shape, BF16)],
        flops=1.5e9,
    )

    half_units = (units // 2 + LANES - 1) // LANES * LANES
    blocks = count // 2

    def summed(name, index, order, lefts, rights, terms):
        send = weight_call(name + "_send", index, lefts, rights, terms, blocks, blocks, BF16)
        keep = weight_call(name + "_keep", index, lefts, rights, terms, 0, blocks, F32)
        return halved(send, keep, order)

    normed_b, cot_b = in_blocks(normed_t), in_blocks(cot_t)
    feed_a = summed(
        "feed_a", index_a, order_a, [normed_b, cot_b], [flat(d_gu), flat(hidden)],
        ((0, 0, 0, units), (1, 1, 0, half_units)),
    )
    feed_b = summed(
        "feed_b", index_b, order_b, [normed_b, cot_b], [flat(d_gu), flat(hidden)],
        ((0, 0, units, units), (1, 1, half_units, units - half_units)),
    )
    mixed_b = in_blocks(mixed_t)
    out_t = summed(
        "out_grad", index_a, order_a, [in_blocks(d_attn_t)], [flat(gated)], ((0, 0, 0, out_wide),)
    )
    grad_g = summed("outgate", index_b, order_b, [mixed_b], [flat(d_pg)], ((0, 0, 0, out_wide),))

    back = back.reshape(state_shape)
    low = low.reshape(state_shape)
    for level, d in enumerate(dists):
        got = passed_along(low, "seq", -d)
        back, low = small_call(
            functools.partial(back_body, pairs), "join_back",
            [back_maps[level], back_logs[level], back, got], [(state_shape, F32), (state_shape, BF16)],
        )
    near = passed_along(low, "seq", -1)
    far = passed_along(low, "seq", -1 - reach_by)
    (d_end,) = small_call(
        functools.partial(exit_body, pairs), "exit", [near_map, near, far], [(state_shape, F32)]
    )
    d_end = d_end.reshape(seqs, heads, DK, DV)

    x_one, x_map, d_key, d_col, dext_q, dtap_q = call(
        functools.partial(early_body, heads), "delta_back_early", seqs,
        [proj, gates, sums, d_out, state, made, inv, score, decay], [conv_query, conv_key],
        [
            (by_value, F32), (by_key, F32), (by_key, F32), ((seqs, size, LANES), F32),
            ((seqs, size + HALO, wide), F32),
        ],
        [((CONV, wide), F32)],
        flops=3e9,
    )
    d_ext, d_gates, dtap_kv, d_bias = call(
        functools.partial(late_body, heads), "delta_back_late", seqs,
        [
            proj, gates, sums, d_end, state, made, decay, x_one, x_map, d_key, d_col, dext_q,
        ],
        [conv_key, conv_value],
        [((seqs, size + HALO, proj_wide), F32), ((seqs, size, LANES), BF16)],
        [((CONV, wide + out_wide), F32), ((1, LANES), F32)],
        flops=3e9,
    )
    edges = passed_along(d_ext[:, :HALO], "seq", -1)
    d_proj, d_mixed, d_mix_gain = call(
        input_back_body, "input_back", seqs, [d_ext, edges, d_pg, d_gates, tokens],
        [w_query, w_key, w_value, w_outgate, gates_w],
        [((seqs, size, proj_wide), BF16), ((seqs, size, width), BF16)],
        [((1, width), F32)],
        flops=1.7e9,
    )
    d_mixed_other = swapped(d_mixed)
    ins_a = summed(
        "query_key", index_a, order_a, [mixed_b], [flat(d_proj), flat(d_gates)],
        ((0, 0, 0, 2 * wide), (0, 1, 0, LANES)),
    )
    ins_b = summed(
        "value", index_b, order_b, [mixed_b], [flat(d_proj)], ((0, 0, 2 * wide, out_wide),)
    )
    (grad_input,) = call(
        last_body, "first_norm_back", seqs, [tokens, d_mixed, d_mixed_other, d_resid], [mix_row],
        [((seqs, size, width), F32)],
    )
    result = (resid + (down.astype(F32) + down_other.astype(F32))).astype(BF16)

    shared = jnp.concatenate([d_out_gain.reshape(-1), d_mix_gain.reshape(-1)])
    shared = shared + swapped(shared)
    small = jnp.concatenate(
        [
            dtap_q.reshape(-1), dtap_kv.reshape(-1), d_bias.reshape(-1), shared,
            d_ffn_gain.reshape(-1),
        ]
    ).reshape(-1, LANES)
    for bit in order_a:
        small = small + traded(small, bit)
    small = small.reshape(-1)
    cuts = [0]
    for length in (CONV * wide, CONV * (wide + out_wide), LANES, DV, width, width):
        cuts.append(cuts[-1] + length)
    pieces = [small[a:b] for a, b in zip(cuts[:-1], cuts[1:])]
    taps_kv = pieces[1].reshape(CONV, wide + out_wide)
    grad_gates = ins_a[:, 2 * wide : 2 * wide + 2 * heads].reshape(share, 2, heads)
    grad_down = jnp.concatenate([feed_a[:, units:], feed_b[:, units:]], axis=1)
    return (
        result,
        grad_input,
        ins_a[:, :wide],
        ins_a[:, wide : 2 * wide],
        ins_b,
        grad_g,
        jnp.swapaxes(grad_gates, 0, 1),
        pieces[2][: 2 * heads].reshape(2, heads),
        pieces[0].reshape(CONV, wide),
        taps_kv[:, :wide],
        taps_kv[:, wide:],
        pieces[3],
        jnp.swapaxes(out_t, 0, 1),
        lax.dynamic_slice_in_dim(pieces[4], me * share, share),
        lax.dynamic_slice_in_dim(pieces[5], me * share, share),
        feed_a[:, :units],
        feed_b[:, :units],
        jnp.swapaxes(grad_down, 0, 1),
    )


def solution(mesh):
    return jax.shard_map(
        on_device,
        mesh=mesh,
        in_specs=(
            P(None, "seq", None),
            P(None, "head"),
            P(None, "head"),
            P(None, "head"),
            P(None, "head"),
            P(None, None, "head"),
            P(None, "head"),
            P(None, "head"),
            P(None, "head"),
            P(None, "head"),
            P(),
            P("head", None),
            P(),
            P(),
            P(None, "head"),
            P(None, "head"),
            P("head", None),
            P(None, "seq", None),
        ),
        out_specs=(
            P(None, "seq", None),
            P(None, "seq", None),
            P("seq", "head"),
            P("seq", "head"),
            P("seq", "head"),
            P("seq", "head"),
            P(None, "seq", "head"),
            P(None, "head"),
            P(None, "head"),
            P(None, "head"),
            P(None, "head"),
            P(),
            P("head", "seq"),
            P("seq"),
            P("seq"),
            P("seq", "head"),
            P("seq", "head"),
            P("head", "seq"),
        ),
        check_vma=False,
    )
```

```python
import functools

import jax
import jax.numpy as jnp
from jax import lax
from jax.experimental import pallas as pl
from jax.experimental.pallas import tpu as pltpu
from jax.sharding import PartitionSpec as P

DK = 128
DV = 256
CONV = 4
HALO = 16
LANES = 128
SCALE = DK ** (-0.5)
F32 = jnp.float32
BF16 = jnp.bfloat16
NN = ((1,), (0,))
NT = ((1,), (1,))
TN = ((0,), (0,))
NOTE = 16
VMEM_LIMIT = 48 * 1024 * 1024
SMALL_LIMIT = 20 * 1024 * 1024


def dot(left, right, dims=NN):
    return lax.dot_general(
        left.astype(BF16), right.astype(BF16), (dims, ((), ())), preferred_element_type=F32
    )


def halves(field):
    high = field.astype(BF16)
    return high, (field - high.astype(F32)).astype(BF16)


def dot3(left, right, dims=NN):
    left_high, left_low = halves(left)
    right_high, right_low = halves(right)
    return dot(left_high, right_high, dims) + (
        dot(left_high, right_low, dims) + dot(left_low, right_high, dims)
    )


def ones_dot(ones, field):
    high, low = halves(field)
    lowest = field - high.astype(F32) - low.astype(F32)
    return dot(ones, high) + (dot(ones, low) + dot(ones, lowest))


def rows_cols(size):
    return (
        lax.broadcasted_iota(jnp.int32, (size, size), 0),
        lax.broadcasted_iota(jnp.int32, (size, size), 1),
    )


def log1p_small(value):
    shifted = 1.0 + value
    same = shifted == 1.0
    safe = jnp.where(same, 1.0, shifted - 1.0)
    return jnp.where(same, value, jnp.log(shifted) * (value / safe))


def log_sigmoid(value):
    return jnp.minimum(value, 0.0) - log1p_small(jnp.exp(-jnp.abs(value)))


def sigmoid(value):
    return 1.0 / (1.0 + jnp.exp(-value))


def row_sum(field):
    return jnp.sum(field, axis=-1, keepdims=True)


def inverse_unit(lowers, rows, cols):
    size = lowers[0].shape[0]
    same = (rows // 16) == (cols // 16)
    eye = (rows == cols).astype(F32)
    powers = [jnp.where(same, -lower, 0.0) for lower in lowers]
    inverses = [eye + power for power in powers]
    for _ in range(3):
        powers = [dot3(power, power) for power in powers]
        inverses = [inv + dot3(inv, power) for inv, power in zip(inverses, powers)]
    block = 16
    while block * 2 <= size:
        inside = ((rows // (2 * block)) == (cols // (2 * block))) & (
            (rows // block) != (cols // block)
        )
        parts = [
            dot3(jnp.where(inside, lower, 0.0), inv) for lower, inv in zip(lowers, inverses)
        ]
        inverses = [inv - dot3(inv, part) for inv, part in zip(inverses, parts)]
        block *= 2
    return inverses


def conv_pre(extended, taps):
    total = taps[CONV - 1 : CONV] * extended
    for offset in range(CONV - 1):
        total = total + taps[offset : offset + 1] * pltpu.roll(extended, CONV - 1 - offset, 0)
    return total[HALO:]


def silu(value):
    return value * sigmoid(value)


def silu_slope(value):
    gate = sigmoid(value)
    return gate * (1.0 + value * (1.0 - gate))


def unit(field):
    inverse = lax.rsqrt(row_sum(field * field) + 1e-06)
    return field * inverse, inverse


def first_body(
    heads, x_ref, gain_ref, wq_ref, wk_ref, wv_ref, wg_ref, wgates_ref, bias_ref, cq_ref, ck_ref,
    cv_ref, proj_ref, pg_ref, gates_ref, sums_ref, inv_ref, mapk_ref, fresh_ref,
    score_ref, reach_ref, local_ref, decay_ref, piece_ref, low_ref, map_ref, maplow_ref, log_ref,
    turned_ref,
):
    x = x_ref[0].astype(F32)
    mixed = x * lax.rsqrt(jnp.mean(x * x, axis=-1, keepdims=True) + 1e-06) * gain_ref[...]
    mixed = mixed.astype(BF16)
    main = mixed[HALO:]
    turned_ref[...] = jnp.transpose(main)
    proj_q = dot(mixed, wq_ref[...]).astype(BF16)
    proj_k = dot(mixed, wk_ref[...]).astype(BF16)
    proj_v = dot(mixed, wv_ref[...]).astype(BF16)
    wide = heads * DK
    proj_ref[0, :, :wide] = proj_q
    proj_ref[0, :, wide : 2 * wide] = proj_k
    proj_ref[0, :, 2 * wide :] = proj_v
    pg_ref[0] = dot(main, wg_ref[...])
    gates = dot(main, wgates_ref[...]) + bias_ref[...]
    gates_ref[0] = gates
    size = main.shape[0]
    rows, cols = rows_cols(size)
    lower = rows >= cols
    strict = rows > cols
    sums = ones_dot(lower.astype(BF16), log_sigmoid(gates))
    sums_ref[0] = sums
    sums_t = jnp.transpose(sums)
    conv_q = silu(conv_pre(proj_q.astype(F32), cq_ref[...]))
    conv_k = silu(conv_pre(proj_k.astype(F32), ck_ref[...]))
    conv_v = silu(conv_pre(proj_v.astype(F32), cv_ref[...]))
    each = range(heads)
    queries = [unit(conv_q[:, h * DK : (h + 1) * DK])[0] * SCALE for h in each]
    keys = [unit(conv_k[:, h * DK : (h + 1) * DK])[0] for h in each]
    values = [conv_v[:, h * DV : (h + 1) * DV] for h in each]
    beta = [sigmoid(gates[:, h : h + 1]) for h in each]
    total = [sums[:, heads + h : heads + h + 1] for h in each]
    decay = [
        jnp.where(
            lower, jnp.exp(jnp.minimum(total[h] - sums_t[heads + h : heads + h + 1, :], 0.0)), 0.0
        )
        for h in each
    ]
    scaled = [beta[h] * keys[h] for h in each]
    lowers = [jnp.where(strict, dot3(keys[h], scaled[h], NT) * decay[h], 0.0) for h in each]
    inverses = inverse_unit(lowers, rows, cols)
    growth = [jnp.exp(total[h]) for h in each]
    last = [total[h][size - 1 : size] for h in each]
    tail = [jnp.exp(last[h] - total[h]) * scaled[h] for h in each]
    mapk = [dot3(inverses[h], growth[h] * keys[h]) for h in each]
    fresh = [dot3(inverses[h], values[h]) for h in each]
    scores = [dot3(queries[h], scaled[h], NT) * decay[h] for h in each]
    moved = [-dot3(tail[h], mapk[h], TN) for h in each]
    shift = [dot3(tail[h], fresh[h], TN) for h in each]
    reach = [growth[h] * queries[h] - dot3(scores[h], mapk[h]) for h in each]
    local = [dot3(scores[h], fresh[h]) for h in each]
    for h in each:
        piece_ref[0, h, :, :DK] = moved[h]
        piece_ref[0, h, :, DK:] = shift[h]
        map_ref[0, h] = moved[h]
        note = log_rows(last[h])
        log_ref[0, h] = jnp.broadcast_to(last[h], (8, LANES))
        maplow_ref[0, h, :DK] = moved[h].astype(BF16)
        maplow_ref[0, h, DK:] = note
        low_ref[0, h, :DK, :DK] = moved[h].astype(BF16)
        low_ref[0, h, :DK, DK:] = shift[h].astype(BF16)
        low_ref[0, h, DK:] = jnp.concatenate([note] * (1 + DV // DK), axis=1)
        inv_ref[0, h] = inverses[h]
        mapk_ref[0, h] = mapk[h]
        fresh_ref[0, h] = fresh[h]
        score_ref[0, h] = scores[h]
        reach_ref[0, h] = reach[h]
        local_ref[0, h] = local[h]
        decay_ref[0, h] = decay[h]


def log_rows(log):
    log = jnp.broadcast_to(log, (1, LANES))
    high = log.astype(BF16).astype(F32)
    middle = (log - high).astype(BF16).astype(F32)
    rest = log - high - middle
    place = lax.broadcasted_iota(jnp.int32, (NOTE, LANES), 0)
    zero = jnp.zeros((NOTE, LANES), F32)
    rows = jnp.where(place == 0, high, jnp.where(place == 1, middle, jnp.where(place == 2, rest, zero)))
    return rows.astype(BF16)


def log_of(rows):
    return jnp.sum(rows.astype(F32), axis=0, keepdims=True)


def join_body(pairs, last, piece_ref, log_ref, got_ref, out_ref, newlog_ref, low_ref, *far_ref):
    wide = 1 + DV // DK
    for p in range(pairs):
        own = piece_ref[p]
        got_low = got_ref[p, :DK]
        got = got_low.astype(F32)
        own_log = log_ref[p, :1]
        got_log = log_of(got_ref[p, DK:, :LANES])
        mine = jnp.concatenate([jnp.exp(own_log)] * wide, axis=1)
        high, low = halves(own[:, :DK])
        moved = dot(high, got_low) + dot(low, got_low) + mine * got
        map_part = moved[:, :DK] + jnp.exp(got_log) * own[:, :DK]
        shift_part = moved[:, DK:] + own[:, DK:]
        new_log = own_log + got_log
        out_ref[p, :, :DK] = map_part
        out_ref[p, :, DK:] = shift_part
        newlog_ref[p] = jnp.broadcast_to(new_log, (8, LANES))
        low_ref[p, :DK, :DK] = map_part.astype(BF16)
        low_ref[p, :DK, DK:] = shift_part.astype(BF16)
        low_ref[p, DK:] = jnp.concatenate([log_rows(new_log)] * wide, axis=1)
        if last:
            far_ref[0][p] = shift_part.astype(BF16)


def map_body(pairs, own_ref, log_ref, got_ref, out_ref, newlog_ref, low_ref):
    for p in range(pairs):
        own = own_ref[p]
        got_low = got_ref[p, :DK]
        own_log = log_ref[p, :1]
        got_log = log_of(got_ref[p, DK:])
        high, low = halves(own)
        out = dot(got_low, high) + dot(got_low, low)
        out = out + jnp.exp(got_log) * own + jnp.exp(own_log) * got_low.astype(F32)
        new_log = own_log + got_log
        out_ref[p] = out
        newlog_ref[p] = jnp.broadcast_to(new_log, (8, LANES))
        low_ref[p, :DK] = out.astype(BF16)
        low_ref[p, DK:] = log_rows(new_log)


def entry_body(pairs, near_ref, far_ref, out_ref):
    for p in range(pairs):
        far = far_ref[p]
        scale = jnp.exp(log_of(near_ref[p, DK:, DK:]))
        moved = dot(near_ref[p, :DK, :DK], far) + scale * far.astype(F32)
        out_ref[p] = moved + near_ref[p, :DK, DK:].astype(F32)


def back_body(pairs, map_ref, log_ref, own_ref, got_ref, out_ref, low_ref):
    for p in range(pairs):
        got = got_ref[p]
        high, low = halves(map_ref[p])
        scale = jnp.concatenate([jnp.exp(log_ref[p, :1])] * (DV // DK), axis=1)
        out = own_ref[p] + dot(high, got, TN) + dot(low, got, TN) + scale * got.astype(F32)
        out_ref[p] = out
        low_ref[p] = out.astype(BF16)


def exit_body(pairs, map_ref, near_ref, far_ref, out_ref):
    for p in range(pairs):
        far = far_ref[p]
        scale = jnp.concatenate([jnp.exp(log_of(map_ref[p, DK:]))] * (DV // DK), axis=1)
        moved = dot(map_ref[p, :DK], far, TN) + scale * far.astype(F32)
        out_ref[p] = near_ref[p].astype(F32) + moved


def mixer_out_body(
    heads, state_ref, fresh_ref, mapk_ref, reach_ref, local_ref, pg_ref, gain_ref, wout_ref,
    made_ref, output_ref, gated_ref, attn_ref,
):
    for h in range(heads):
        state = state_ref[0, h]
        made_ref[0, h] = fresh_ref[0, h] - dot3(mapk_ref[0, h], state)
        output = local_ref[0, h] + dot3(reach_ref[0, h], state)
        output_ref[0, :, h * DV : (h + 1) * DV] = output
        scale = lax.rsqrt(jnp.mean(output * output, axis=-1, keepdims=True) + 1e-05)
        gate = pg_ref[0, :, h * DV : (h + 1) * DV]
        gated_ref[0, :, h * DV : (h + 1) * DV] = (
            output * scale * gain_ref[...] * silu(gate)
        ).astype(BF16)
    attn_ref[0] = dot(gated_ref[0], wout_ref[...]).astype(BF16)


def feed_body(
    x_ref, mine_ref, other_ref, cot_ref, gain_ref, wgate_ref, wup_ref, wdown_ref, resid_ref,
    hidden_a_ref, hidden_b_ref, dgate_ref, dup_ref, down_ref, dnorm_ref, normed_ref, cot_turned_ref,
):
    cut = hidden_a_ref.shape[2]
    attn = mine_ref[0].astype(F32) + other_ref[0].astype(F32)
    resid = x_ref[0].astype(F32) + attn
    resid_ref[0] = resid
    normed = resid * lax.rsqrt(jnp.mean(resid * resid, axis=-1, keepdims=True) + 1e-06)
    normed = (normed * gain_ref[...]).astype(BF16)
    normed_ref[...] = jnp.transpose(normed)
    cot_turned_ref[...] = jnp.transpose(cot_ref[0])
    gate = dot(normed, wgate_ref[...])
    up = dot(normed, wup_ref[...])
    d_hidden = dot(cot_ref[0], wdown_ref[...], NT)
    sig = sigmoid(gate)
    active = gate * sig
    hidden = (active * up).astype(BF16)
    hidden_a_ref[0] = hidden[:, :cut]
    hidden_b_ref[0] = hidden[:, cut:]
    d_gate = (d_hidden * up * (sig + active * (1.0 - sig))).astype(BF16)
    d_up = (d_hidden * active).astype(BF16)
    dgate_ref[0] = d_gate
    dup_ref[0] = d_up
    down_ref[0] = dot(hidden, wdown_ref[...]).astype(BF16)
    dnorm_ref[0] = (dot(d_gate, wgate_ref[...], NT) + dot(d_up, wup_ref[...], NT)).astype(BF16)


def mixer_back_body(
    heads, resid_ref, mine_ref, other_ref, cot_ref, output_ref, pg_ref, reach_ref, gain_ref,
    wout_ref, ogain_ref, dresid_ref, dout_ref, dpg_ref, back_ref, low_ref, dattn_ref, dgain_ref,
    dogain_ref,
):
    step = pl.program_id(0)
    resid = resid_ref[0]
    inverse = lax.rsqrt(jnp.mean(resid * resid, axis=-1, keepdims=True) + 1e-06)
    unit_resid = resid * inverse
    d_normed = mine_ref[0].astype(F32) + other_ref[0].astype(F32)
    d_gain = jnp.sum(d_normed * unit_resid, axis=0, keepdims=True)
    d_unit = d_normed * gain_ref[...]
    d_resid = inverse * (
        d_unit - unit_resid * jnp.mean(d_unit * unit_resid, axis=-1, keepdims=True)
    )
    d_resid = d_resid + cot_ref[0].astype(F32)
    dresid_ref[0] = d_resid
    d_attn = d_resid.astype(BF16)
    dattn_ref[...] = jnp.transpose(d_attn)
    d_gated = dot(d_attn, wout_ref[...], NT)
    d_ogain = jnp.zeros((1, DV), F32)
    for h in range(heads):
        part = slice(h * DV, (h + 1) * DV)
        output = output_ref[0, :, part]
        inverse = lax.rsqrt(jnp.mean(output * output, axis=-1, keepdims=True) + 1e-05)
        unit_out = output * inverse
        gate = pg_ref[0, :, part]
        grad = d_gated[:, part]
        active = silu(gate)
        d_ogain = d_ogain + jnp.sum(grad * unit_out * active, axis=0, keepdims=True)
        dpg_ref[0, :, part] = (grad * unit_out * ogain_ref[...] * silu_slope(gate)).astype(BF16)
        d_unit = grad * ogain_ref[...] * active
        d_out = inverse * (d_unit - unit_out * jnp.mean(d_unit * unit_out, axis=-1, keepdims=True))
        dout_ref[0, :, part] = d_out
        back = dot3(reach_ref[0, h], d_out, TN)
        back_ref[0, h] = back
        low_ref[0, h] = back.astype(BF16)

    @pl.when(step == 0)
    def _():
        dgain_ref[...] = d_gain
        dogain_ref[...] = d_ogain

    @pl.when(step > 0)
    def _():
        dgain_ref[...] += d_gain
        dogain_ref[...] += d_ogain


def conv_back(grad, extended, taps, pre):
    d_pre = grad * silu_slope(pre)
    padded = jnp.concatenate([jnp.zeros((HALO, d_pre.shape[1]), F32), d_pre], axis=0)
    length = padded.shape[0]
    d_ext = taps[CONV - 1 : CONV] * padded
    d_taps = []
    for offset in range(CONV):
        back = CONV - 1 - offset
        if back:
            d_ext = d_ext + taps[offset : offset + 1] * pltpu.roll(padded, length - back, 0)
            shifted = pltpu.roll(extended, back, 0)
        else:
            shifted = extended
        d_taps.append(jnp.sum(padded * shifted, axis=0, keepdims=True))
    return d_ext, jnp.concatenate(d_taps, axis=0)


def early_body(
    heads, proj_ref, gates_ref, sums_ref, dout_ref, state_ref, made_ref, inv_ref, score_ref,
    decay_ref, cq_ref, ck_ref, xone_ref, xmap_ref, dkey_ref, dcol_ref, dext_ref, dtap_ref,
):
    step = pl.program_id(0)
    wide = heads * DK
    ext_q = proj_ref[0, :, :wide].astype(F32)
    ext_k = proj_ref[0, :, wide : 2 * wide].astype(F32)
    pre_q = conv_pre(ext_q, cq_ref[...])
    conv_q = silu(pre_q)
    conv_k = silu(conv_pre(ext_k, ck_ref[...]))
    gates = gates_ref[0]
    sums = sums_ref[0]
    size = gates.shape[0]
    each = range(heads)
    units = [unit(conv_q[:, h * DK : (h + 1) * DK]) for h in each]
    queries = [units[h][0] * SCALE for h in each]
    keys = [unit(conv_k[:, h * DK : (h + 1) * DK])[0] for h in each]
    beta = [sigmoid(gates[:, h : h + 1]) for h in each]
    total = [sums[:, heads + h : heads + h + 1] for h in each]
    growth = [jnp.exp(total[h]) for h in each]
    tail = [jnp.exp(total[h][size - 1 : size] - total[h]) * beta[h] * keys[h] for h in each]
    d_out = [dout_ref[0, :, h * DV : (h + 1) * DV] for h in each]
    d_made = [dot3(score_ref[0, h], d_out[h], TN) for h in each]
    d_score = [dot3(d_out[h], made_ref[0, h], NT) * decay_ref[0, h] for h in each]
    d_query = [
        dot3(d_score[h], beta[h] * keys[h]) + dot3(growth[h] * d_out[h], state_ref[0, h], NT)
        for h in each
    ]
    d_key = [dot3(d_score[h], queries[h], TN) for h in each]
    x_one = [dot3(inv_ref[0, h], d_made[h], TN) for h in each]
    x_map = [dot3(inv_ref[0, h], tail[h], TN) for h in each]
    lanes = lax.broadcasted_iota(jnp.int32, (size, LANES), 1)
    cols = jnp.zeros((size, LANES), F32)
    grads = []
    for h in each:
        xone_ref[0, h] = x_one[h]
        xmap_ref[0, h] = x_map[h]
        dkey_ref[0, h] = beta[h] * d_key[h]
        key_sum = row_sum(d_key[h] * keys[h])
        cols = cols + jnp.where(lanes == h, key_sum, 0.0)
        d_total = row_sum(d_query[h] * queries[h]) - beta[h] * key_sum
        cols = cols + jnp.where(lanes == heads + h, d_total, 0.0)
        unit_q, inverse = units[h]
        d_unit = d_query[h] * SCALE
        grads.append(inverse * (d_unit - unit_q * row_sum(d_unit * unit_q)))
    dcol_ref[0] = cols
    d_ext, d_taps = conv_back(jnp.concatenate(grads, axis=1), ext_q, cq_ref[...], pre_q)
    dext_ref[0] = d_ext

    @pl.when(step == 0)
    def _():
        dtap_ref[...] = d_taps

    @pl.when(step > 0)
    def _():
        dtap_ref[...] += d_taps


def late_body(
    heads, proj_ref, gates_ref, sums_ref, dend_ref, state_ref, made_ref, decay_ref, xone_ref,
    xmap_ref, dkey_ref, dcol_ref, dextq_ref, ck_ref, cv_ref, dext_ref, dgates_ref, dtap_ref, dbias_ref,
):
    step = pl.program_id(0)
    wide = heads * DK
    ext_k = proj_ref[0, :, wide : 2 * wide].astype(F32)
    ext_v = proj_ref[0, :, 2 * wide :].astype(F32)
    pre_k = conv_pre(ext_k, ck_ref[...])
    pre_v = conv_pre(ext_v, cv_ref[...])
    conv_k = silu(pre_k)
    gates = gates_ref[0]
    sums = sums_ref[0]
    size = gates.shape[0]
    rows, cols = rows_cols(size)
    strict = rows > cols
    each = range(heads)
    units = [unit(conv_k[:, h * DK : (h + 1) * DK]) for h in each]
    keys = [units[h][0] for h in each]
    beta = [sigmoid(gates[:, h : h + 1]) for h in each]
    total = [sums[:, heads + h : heads + h + 1] for h in each]
    growth = [jnp.exp(total[h]) for h in each]
    left = [jnp.exp(total[h][size - 1 : size] - total[h]) for h in each]
    d_end = [dend_ref[0, h] for h in each]
    made = [made_ref[0, h] for h in each]
    state = [state_ref[0, h] for h in each]
    d_rhs = [xone_ref[0, h] + dot3(xmap_ref[0, h], d_end[h]) for h in each]
    d_tail = [dot3(made[h], d_end[h], NT) for h in each]
    d_lower = [
        jnp.where(strict, -dot3(d_rhs[h], made[h], NT) * decay_ref[0, h], 0.0) for h in each
    ]
    d_plain = [
        dot3(d_lower[h], beta[h] * keys[h]) - dot3(growth[h] * d_rhs[h], state[h], NT) for h in each
    ]
    d_turned = [dot3(d_lower[h], keys[h], TN) for h in each]
    lanes = lax.broadcasted_iota(jnp.int32, (size, LANES), 1)
    places = lax.broadcasted_iota(jnp.int32, (size, 1), 0)
    d_col = dcol_ref[0]
    grads_k = []
    for h in each:
        turned = row_sum(d_turned[h] * keys[h])
        tails = row_sum(d_tail[h] * keys[h])
        tail_weight = left[h] * beta[h]
        d_key = d_plain[h] + beta[h] * d_turned[h] + tail_weight * d_tail[h] + dkey_ref[0, h]
        d_total = row_sum(d_plain[h] * keys[h]) - beta[h] * turned - tail_weight * tails
        ended = jnp.sum(tail_weight * tails, axis=0, keepdims=True)
        whole = jnp.sum(row_sum(d_end[h] * state[h]), axis=0, keepdims=True)
        ended = ended + growth[h][size - 1 : size] * whole
        d_total = d_total + jnp.where(places == size - 1, ended, 0.0)
        d_col = d_col + jnp.where(lanes == h, turned + left[h] * tails, 0.0)
        d_col = d_col + jnp.where(lanes == heads + h, d_total, 0.0)
        unit_k, inverse = units[h]
        grads_k.append(inverse * (d_key - unit_k * row_sum(d_key * unit_k)))
    upper = (rows <= cols).astype(BF16)
    d_decay = ones_dot(upper, d_col)
    rate = sigmoid(gates)
    d_gates = jnp.where(
        lanes < heads, d_col * rate * (1.0 - rate), d_decay / (1.0 + jnp.exp(gates))
    )
    d_gates = jnp.where(lanes < 2 * heads, d_gates, 0.0)
    dgates_ref[0] = d_gates.astype(BF16)
    d_bias = jnp.sum(d_gates, axis=0, keepdims=True)
    dext_k, dtaps_k = conv_back(jnp.concatenate(grads_k, axis=1), ext_k, ck_ref[...], pre_k)
    dext_v, dtaps_v = conv_back(jnp.concatenate(d_rhs, axis=1), ext_v, cv_ref[...], pre_v)
    dext_ref[0, :, :wide] = dextq_ref[0]
    dext_ref[0, :, wide : 2 * wide] = dext_k
    dext_ref[0, :, 2 * wide :] = dext_v

    @pl.when(step == 0)
    def _():
        dtap_ref[:, :wide] = dtaps_k
        dtap_ref[:, wide:] = dtaps_v
        dbias_ref[...] = d_bias

    @pl.when(step > 0)
    def _():
        dtap_ref[:, :wide] += dtaps_k
        dtap_ref[:, wide:] += dtaps_v
        dbias_ref[...] += d_bias


def input_back_body(
    dext_ref, edge_ref, dpg_ref, dgates_ref, x_ref, wq_ref, wk_ref, wv_ref, wg_ref, wgates_ref,
    dproj_ref, dmixed_ref, dgain_ref,
):
    step = pl.program_id(0)
    wide = wq_ref.shape[1]
    own = dext_ref[0, HALO:]
    size = own.shape[0]
    d_proj = jnp.concatenate([own[: size - HALO], own[size - HALO :] + edge_ref[0]], axis=0)
    d_proj = d_proj.astype(BF16)
    dproj_ref[0] = d_proj
    d_mixed = dot(d_proj[:, :wide], wq_ref[...], NT)
    d_mixed = d_mixed + dot(d_proj[:, wide : 2 * wide], wk_ref[...], NT)
    d_mixed = d_mixed + dot(d_proj[:, 2 * wide :], wv_ref[...], NT)
    d_mixed = d_mixed + dot(dpg_ref[0], wg_ref[...], NT)
    d_mixed = d_mixed + dot(dgates_ref[0], wgates_ref[...], NT)
    dmixed_ref[0] = d_mixed.astype(BF16)
    x = x_ref[0].astype(F32)
    unit_x = x * lax.rsqrt(jnp.mean(x * x, axis=-1, keepdims=True) + 1e-06)
    d_gain = jnp.sum(d_mixed * unit_x, axis=0, keepdims=True)

    @pl.when(step == 0)
    def _():
        dgain_ref[...] = d_gain

    @pl.when(step > 0)
    def _():
        dgain_ref[...] += d_gain


def last_body(
    x_ref, mine_ref, other_ref, dresid_ref, resid_ref, down_ref, downother_ref, gain_ref, grad_ref,
    result_ref,
):
    x = x_ref[0].astype(F32)
    inverse = lax.rsqrt(jnp.mean(x * x, axis=-1, keepdims=True) + 1e-06)
    unit_x = x * inverse
    d_mixed = mine_ref[0].astype(F32) + other_ref[0].astype(F32)
    d_unit = d_mixed * gain_ref[...]
    back = inverse * (d_unit - unit_x * jnp.mean(d_unit * unit_x, axis=-1, keepdims=True))
    grad_ref[0] = dresid_ref[0] + back
    down = down_ref[0].astype(F32) + downother_ref[0].astype(F32)
    result_ref[0] = (resid_ref[0] + down).astype(BF16)


def held_rows(left_refs, index_ref, first, blocks, held):
    share = left_refs[0].shape[1]
    for number, left_ref in enumerate(left_refs):
        for place in range(blocks):
            held[number, place * share : (place + 1) * share] = left_ref[index_ref[first + place]]


def send_body(terms, first, blocks, lefts, index_ref, *refs):
    out_ref, held = refs[-2:]
    held_rows(refs[:lefts], index_ref, first, blocks, held)
    at = 0
    for left, right, width in terms:
        out_ref[:, at : at + width] = dot(held[left], refs[lefts + right][...]).astype(BF16)
        at += width


def keep_body(terms, blocks, parts, lefts, index_ref, *refs):
    rights = len(terms)
    got_ref = refs[lefts + rights]
    keep_ref, held = refs[lefts + rights + 1], refs[-1]
    send_refs = refs[lefts + rights + 2 : -1]
    held_rows(refs[:lefts], index_ref, 0, blocks, held)
    rows = keep_ref.shape[0]
    at = 0
    for left, right, width in terms:
        total = dot(held[left], refs[lefts + right][...])
        total = total + got_ref[:, at : at + width].astype(F32)
        keep_ref[:, at : at + width] = total[:rows]
        for part in range(1, parts):
            send_refs[part - 1][:, at : at + width] = total[part * rows : (part + 1) * rows].astype(BF16)
        at += width


def add_body(parts, gots, keep_ref, *refs):
    total = keep_ref[...]
    for got_ref in refs[:gots]:
        total = total + got_ref[...].astype(F32)
    out_ref = refs[gots]
    rows = out_ref.shape[0]
    out_ref[...] = total[:rows]
    for part in range(1, parts):
        refs[gots + part][...] = total[part * rows : (part + 1) * rows].astype(BF16)


def sum_body(count, *refs):
    total = refs[0][...]
    for ref in refs[1:count]:
        total = total + ref[...]
    refs[count][...] = total


def by_seq(shape):
    rest = len(shape) - 1
    return pl.BlockSpec((1,) + tuple(shape[1:]), lambda s: (s,) + (0,) * rest)


def whole(shape):
    rest = len(shape)
    return pl.BlockSpec(tuple(shape), lambda s: (0,) * rest)


def without(body, position, count):
    def shorter(*refs):
        return body(*refs[:position], *refs[position + count :])

    return shorter if count else body


def call(body, name, seqs, parts, shared, outs, sums=(), turned=(), after=(), flops=0):
    operands = list(parts) + list(shared)
    listed = list(outs) + list(turned) + list(sums)
    out_shape = [jax.ShapeDtypeStruct(shape, kind) for shape, kind in listed]
    moved = sum(a.size * a.dtype.itemsize for a in operands + out_shape)
    return pl.pallas_call(
        without(body, len(operands), len(after)),
        grid=(seqs,),
        in_specs=[by_seq(a.shape) for a in parts]
        + [whole(a.shape) for a in shared]
        + [pl.BlockSpec(memory_space=pl.ANY)] * len(after),
        out_specs=[by_seq(shape) for shape, _ in outs]
        + [pl.BlockSpec((shape[0], shape[1] // seqs), lambda s: (0, s)) for shape, _ in turned]
        + [whole(shape) for shape, _ in sums],
        out_shape=out_shape,
        compiler_params=pltpu.CompilerParams(vmem_limit_bytes=VMEM_LIMIT),
        cost_estimate=pl.CostEstimate(flops=int(flops), bytes_accessed=int(moved), transcendentals=0),
        name=name,
    )(*operands, *after)


def small_call(body, name, arrays, outs, after=(), scalars=(), scratch=(), flops=2e8):
    out_shape = [jax.ShapeDtypeStruct(shape, kind) for shape, kind in outs]
    moved = sum(a.size * a.dtype.itemsize for a in list(arrays) + out_shape)
    return pl.pallas_call(
        without(body, len(scalars) + len(arrays), len(after)),
        in_specs=[pl.BlockSpec(memory_space=pltpu.SMEM)] * len(scalars)
        + [pl.BlockSpec(memory_space=pltpu.VMEM)] * len(arrays)
        + [pl.BlockSpec(memory_space=pl.ANY)] * len(after),
        out_specs=[pl.BlockSpec(memory_space=pltpu.VMEM)] * len(outs),
        out_shape=out_shape,
        scratch_shapes=list(scratch),
        compiler_params=pltpu.CompilerParams(vmem_limit_bytes=SMALL_LIMIT),
        cost_estimate=pl.CostEstimate(flops=int(flops), bytes_accessed=int(moved), transcendentals=0),
        name=name,
    )(*scalars, *arrays, *after)


class Halved:
    def __init__(self, name, order, me, lefts, rights, terms):
        self.name, self.lefts, self.rights, self.terms = (name, lefts, rights, terms)
        self.steps = [order[:1], order[1:2]] + [order[i : i + 2] for i in range(2, len(order), 2)]
        self.index = block_index(order, me)
        self.count = 1 << len(order)
        _, self.share, self.tokens = lefts[0].shape
        self.columns = sum(width for _, _, width in terms)
        self.done = 0

    def trade(self, sends):
        bits = self.steps[self.done]
        self.done += 1
        self.gots = []
        for part, send in enumerate(sends, 1):
            moved = sum(
                ((part >> (len(bits) - 1 - place)) & 1) << bit for place, bit in enumerate(bits)
            )
            self.gots.append(traded(send, moved))

    def multiplied(self, body, suffix, extra, outs, after):
        blocks = self.count // 2
        return small_call(
            body, self.name + suffix, list(self.lefts) + list(self.rights) + extra, outs, after,
            scalars=[self.index],
            scratch=[pltpu.VMEM((len(self.lefts), blocks * self.share, self.tokens), BF16)],
            flops=2 * blocks * self.share * self.tokens * self.columns,
        )

    def outs(self, rows):
        parts = 1 << len(self.steps[self.done])
        return parts, [((rows // parts, self.columns), F32)] + [
            ((rows // parts, self.columns), BF16)
        ] * (parts - 1)

    def send(self, *after):
        blocks = self.count // 2
        body = functools.partial(send_body, self.terms, blocks, blocks, len(self.lefts))
        rows = blocks * self.share
        sends = self.multiplied(body, "_send", [], [((rows, self.columns), BF16)], after)
        self.trade(sends)
        return sends[0]

    def keep(self, *after):
        blocks = self.count // 2
        parts, outs = self.outs(blocks * self.share)
        body = functools.partial(keep_body, self.terms, blocks, parts, len(self.lefts))
        self.kept, *sends = self.multiplied(body, "_keep", self.gots, outs, after)
        self.trade(sends)
        return self.kept

    def add(self, *after):
        parts, outs = self.outs(self.kept.shape[0])
        body = functools.partial(add_body, parts, len(self.gots))
        self.kept, *sends = small_call(
            body, self.name + "_add", [self.kept] + self.gots, outs, after, flops=1e6
        )
        self.trade(sends)
        return self.kept

    def left(self):
        return len(self.steps) - self.done

    def total(self):
        return sum((got.astype(F32) for got in self.gots), self.kept)


def halving_order(count, first):
    bits = list(range(count.bit_length() - 1))
    return bits[first : first + 1] + bits[:first] + bits[first + 1 :]


def block_index(order, me):
    count = 1 << len(order)
    moved = [
        sum(((place >> (len(order) - 1 - step)) & 1) << bit for step, bit in enumerate(order))
        for place in range(count)
    ]
    return jnp.bitwise_xor(jnp.array(moved, jnp.int32), me)


def traded(block, moved):
    count = lax.axis_size("seq")
    return lax.ppermute(block, "seq", [(i, i ^ moved) for i in range(count)])


def passed_along(block, axis, distance):
    devices = range(lax.axis_size(axis))
    route = [(i - distance, i) for i in devices if i - distance in devices]
    return lax.ppermute(block, axis, route)


def swapped(block):
    count = lax.axis_size("head")
    return lax.ppermute(block, "head", [(i, i ^ 1) for i in range(count)])


def on_device(
    tokens, w_query, w_key, w_value, w_outgate, w_gates, gate_bias, conv_query, conv_key,
    conv_value, out_gain, w_out, mix_gain, ffn_gain, w_gate, w_up, w_down, cotangent,
):
    seqs, size, width = tokens.shape
    heads = gate_bias.shape[1]
    pairs = seqs * heads
    units = w_gate.shape[1]
    count, me = lax.axis_size("seq"), lax.axis_index("seq")
    wide = heads * DK
    out_wide = heads * DV
    proj_wide = 2 * wide + out_wide

    halo = passed_along(tokens[:, size - HALO :], "seq", 1)
    x_ext = jnp.concatenate([halo, tokens], axis=1)
    gates_w = jnp.swapaxes(w_gates, 0, 1).reshape(width, 2 * heads)
    gates_w = jnp.pad(gates_w, ((0, 0), (0, LANES - 2 * heads)))
    bias = jnp.pad(gate_bias.reshape(1, 2 * heads), ((0, 0), (0, LANES - 2 * heads)))
    mix_row = mix_gain.reshape(1, width)
    ffn_row = ffn_gain.reshape(1, width)
    out_row = out_gain.reshape(1, DV)
    square = (seqs, heads, size, size)
    by_key = (seqs, heads, size, DK)
    by_value = (seqs, heads, size, DV)
    tokens_here = seqs * size
    order_a, order_b = halving_order(count, 0), halving_order(count, 1)
    half_units = (units // 2 + LANES - 1) // LANES * LANES
    turned_shape = (width, tokens_here)
    share = width // count

    def in_blocks(turned):
        return turned.reshape(count, share, tokens_here)

    def flat(field):
        return field.reshape(tokens_here, field.shape[2])

    (
        proj, proj_g, gates, sums, inv, mapk, fresh, score, reach, local, decay, piece, low,
        back_map, back_low, log, mixed_t,
    ) = call(
        functools.partial(first_body, heads), "project_and_local", seqs, [x_ext],
        [mix_row, w_query, w_key, w_value, w_outgate, gates_w, bias, conv_query, conv_key, conv_value],
        [
            ((seqs, size + HALO, proj_wide), BF16),
            ((seqs, size, out_wide), F32), ((seqs, size, LANES), F32), ((seqs, size, LANES), F32),
            (square, F32), (by_key, F32), (by_value, F32), (square, F32), (by_key, F32),
            (by_value, F32), (square, F32), ((seqs, heads, DK, DK + DV), F32),
            ((seqs, heads, DK + NOTE, DK + DV), BF16), ((seqs, heads, DK, DK), F32),
            ((seqs, heads, DK + NOTE, DK), BF16), ((seqs, heads, 8, LANES), F32),
        ],
        turned=[(turned_shape, BF16)],
        flops=1e10,
    )

    piece = piece.reshape(pairs, DK, DK + DV)
    low = low.reshape(pairs, DK + NOTE, DK + DV)
    log = log.reshape(pairs, 8, LANES)
    back_maps = [back_map.reshape(pairs, DK, DK)]
    back_low = back_low.reshape(pairs, DK + NOTE, DK)
    back_logs = [log]
    state_shape = (pairs, DK, DV)
    dists = []
    reach_by = 1
    while reach_by * 2 < count:
        dists.append(reach_by)
        reach_by *= 2
    for level, d in enumerate(dists):
        got = passed_along(low, "seq", d)
        got_back = passed_along(back_low, "seq", -d)
        last = level + 1 == len(dists)
        outs = [(piece.shape, F32), (log.shape, F32), (low.shape, BF16)]
        if last:
            outs.append((state_shape, BF16))
        piece, log, low, *far = small_call(
            functools.partial(join_body, pairs, last), "join", [piece, log, got], outs,
            after=[back_low] if level else [],
        )
        new_map, new_log, back_low = small_call(
            functools.partial(map_body, pairs), "join_maps", [back_maps[-1], back_logs[-1], got_back],
            [(back_maps[0].shape, F32), (log.shape, F32), (back_low.shape, BF16)],
        )
        back_maps.append(new_map)
        back_logs.append(new_log)
    near = passed_along(low, "seq", 1)
    far = passed_along(far[0], "seq", 1 + reach_by)
    near_map = passed_along(back_low, "seq", -1)
    (state,) = small_call(
        functools.partial(entry_body, pairs), "entry", [near, far], [(state_shape, F32)],
        after=[back_low],
    )
    state = state.reshape(seqs, heads, DK, DV)

    made, output, gated, attn = call(
        functools.partial(mixer_out_body, heads), "mixer_out", seqs,
        [state, fresh, mapk, reach, local, proj_g], [out_row, w_out],
        [
            (by_value, F32), ((seqs, size, out_wide), F32), ((seqs, size, out_wide), BF16),
            ((seqs, size, width), BF16),
        ],
        flops=1.5e9,
    )
    attn_other = swapped(attn)

    resid, hidden_a, hidden_b, d_gate, d_up, down, d_norm, normed_t, cot_t = call(
        feed_body, "feed_forward", seqs, [tokens, attn, attn_other, cotangent],
        [ffn_row, w_gate, w_up, w_down],
        [
            ((seqs, size, width), F32), ((seqs, size, half_units), BF16),
            ((seqs, size, units - half_units), BF16), ((seqs, size, units), BF16),
            ((seqs, size, units), BF16), ((seqs, size, width), BF16), ((seqs, size, width), BF16),
        ],
        turned=[(turned_shape, BF16), (turned_shape, BF16)],
        flops=1.2e10,
    )
    d_norm_other = swapped(d_norm)
    down_other = swapped(down)

    normed_b, cot_b, mixed_b = in_blocks(normed_t), in_blocks(cot_t), in_blocks(mixed_t)
    gates_a = Halved("gate", order_a, me, [normed_b], [flat(d_gate)], ((0, 0, units),))
    gates_b = Halved("up", order_b, me, [normed_b], [flat(d_up)], ((0, 0, units),))
    done = gates_a.send()

    d_resid, d_out, d_pg, back, low, d_attn_t, d_ffn_gain, d_out_gain = call(
        functools.partial(mixer_back_body, heads), "mixer_back", seqs,
        [resid, d_norm, d_norm_other, cotangent, output, proj_g, reach],
        [ffn_row, w_out, out_row],
        [
            ((seqs, size, width), F32), ((seqs, size, out_wide), F32),
            ((seqs, size, out_wide), BF16), ((seqs, heads, DK, DV), F32),
            ((seqs, heads, DK, DV), BF16),
        ],
        [((1, width), F32), ((1, DV), F32)],
        turned=[(turned_shape, BF16)],
        after=[done],
        flops=1.5e9,
    )

    outs_a = Halved(
        "down_out", order_a, me, [cot_b, in_blocks(d_attn_t)], [flat(hidden_a), flat(gated)],
        ((0, 0, half_units), (1, 1, out_wide)),
    )
    outs_b = Halved(
        "down_outgate", order_b, me, [cot_b, mixed_b], [flat(hidden_b), flat(d_pg)],
        ((0, 0, units - half_units), (1, 1, out_wide)),
    )
    back = back.reshape(state_shape)
    low = low.reshape(state_shape)

    def early(done):
        return call(
            functools.partial(early_body, heads), "delta_back_early", seqs,
            [proj, gates, sums, d_out, state, made, inv, score, decay], [conv_query, conv_key],
            [
                (by_value, F32), (by_key, F32), (by_key, F32), ((seqs, size, LANES), F32),
                ((seqs, size + HALO, wide), F32),
            ],
            [((CONV, wide), F32)],
            after=[done],
            flops=3e9,
        )

    done = gates_b.send(low)
    done = outs_a.send(done)
    waits = [
        lambda done: outs_b.send(done), None, lambda done: gates_b.keep(gates_a.keep(done)),
    ]
    early_outs = None
    for level, d in enumerate(dists):
        got = passed_along(low, "seq", -d)
        if level < len(waits) and waits[level] is not None:
            done = waits[level](done)
        elif early_outs is None:
            early_outs = early(done)
            done = early_outs[3]
        back, low = small_call(
            functools.partial(back_body, pairs), "join_back",
            [back_maps[level], back_logs[level], back, got], [(state_shape, F32), (state_shape, BF16)],
            after=[done],
        )
        done = low
    near = passed_along(low, "seq", -1)
    far = passed_along(low, "seq", -1 - reach_by)
    done = outs_b.keep(outs_a.keep(done))
    x_one, x_map, d_key, d_col, dext_q, dtap_q = early_outs
    (d_end,) = small_call(
        functools.partial(exit_body, pairs), "exit", [near_map, near, far], [(state_shape, F32)],
        after=[done],
    )
    d_end = d_end.reshape(seqs, heads, DK, DV)
    d_ext, d_gates, dtap_kv, d_bias = call(
        functools.partial(late_body, heads), "delta_back_late", seqs,
        [
            proj, gates, sums, d_end, state, made, decay, x_one, x_map, d_key, d_col, dext_q,
        ],
        [conv_key, conv_value],
        [((seqs, size + HALO, proj_wide), F32), ((seqs, size, LANES), BF16)],
        [((CONV, wide + out_wide), F32), ((1, LANES), F32)],
        flops=3e9,
    )
    edges = passed_along(d_ext[:, :HALO], "seq", -1)
    done = gates_b.add(gates_a.add(d_bias))
    d_proj, d_mixed, d_mix_gain = call(
        input_back_body, "input_back", seqs, [d_ext, edges, d_pg, d_gates, tokens],
        [w_query, w_key, w_value, w_outgate, gates_w],
        [((seqs, size, proj_wide), BF16), ((seqs, size, width), BF16)],
        [((1, width), F32)],
        after=[done],
        flops=1.7e9,
    )
    d_mixed_other = swapped(d_mixed)
    shared = jnp.concatenate([d_out_gain.reshape(-1), d_mix_gain.reshape(-1)]).reshape(-1, LANES)
    shared_other = swapped(shared)
    rows_all = flat(d_proj)
    ins_a = Halved(
        "query_key", order_a, me, [mixed_b], [rows_all[:, : 2 * wide], flat(d_gates)],
        ((0, 0, 2 * wide), (0, 1, LANES)),
    )
    ins_b = Halved("value", order_b, me, [mixed_b], [rows_all[:, 2 * wide :]], ((0, 0, out_wide),))
    done = ins_b.send(ins_a.send(d_mix_gain))
    grad_input, result = call(
        last_body, "first_norm_back", seqs,
        [tokens, d_mixed, d_mixed_other, d_resid, resid, down, down_other], [mix_row],
        [((seqs, size, width), F32), ((seqs, size, width), BF16)],
        after=[done],
    )

    small = jnp.concatenate(
        [
            dtap_q.reshape(-1), dtap_kv.reshape(-1), d_bias.reshape(-1), d_ffn_gain.reshape(-1),
        ]
    ).reshape(-1, LANES)
    small = jnp.concatenate([small, shared + shared_other], axis=0)
    done = result
    steps = [
        lambda done: ins_b.keep(ins_a.keep(outs_b.add(outs_a.add(done)))),
        lambda done: ins_b.add(ins_a.add(done)),
    ]
    for bits in [order_a[:2]] + ins_a.steps[2:]:
        others = [
            traded(small, sum(((part >> place) & 1) << bit for place, bit in enumerate(bits)))
            for part in range(1, 1 << len(bits))
        ]
        if steps:
            done = steps.pop(0)(done)
        (small,) = small_call(
            functools.partial(sum_body, 1 + len(others)), "small_sum", [small] + others,
            [(small.shape, F32)], after=[done],
        )
        done = small
    groups = [gates_a, gates_b, outs_a, outs_b, ins_a, ins_b]
    for group in groups:
        while group.left():
            done = group.add(done)
    feed_gate, feed_up, out_down_a, out_down_b, ins_a, ins_b = [group.total() for group in groups]
    small = small.reshape(-1)
    cuts = [0]
    for length in (CONV * wide, CONV * (wide + out_wide), LANES, width, DV, width):
        cuts.append(cuts[-1] + length)
    pieces = [small[a:b] for a, b in zip(cuts[:-1], cuts[1:])]
    taps_kv = pieces[1].reshape(CONV, wide + out_wide)
    grad_gates = ins_a[:, 2 * wide : 2 * wide + 2 * heads].reshape(share, 2, heads)
    grad_down = jnp.concatenate([out_down_a[:, :half_units], out_down_b[:, :-out_wide]], axis=1)
    return (
        result,
        grad_input,
        ins_a[:, :wide],
        ins_a[:, wide : 2 * wide],
        ins_b,
        out_down_b[:, -out_wide:],
        jnp.swapaxes(grad_gates, 0, 1),
        pieces[2][: 2 * heads].reshape(2, heads),
        pieces[0].reshape(CONV, wide),
        taps_kv[:, :wide],
        taps_kv[:, wide:],
        pieces[4],
        jnp.swapaxes(out_down_a[:, half_units:], 0, 1),
        lax.dynamic_slice_in_dim(pieces[5], me * share, share),
        lax.dynamic_slice_in_dim(pieces[3], me * share, share),
        feed_gate,
        feed_up,
        jnp.swapaxes(grad_down, 0, 1),
    )


def solution(mesh):
    return jax.shard_map(
        on_device,
        mesh=mesh,
        in_specs=(
            P(None, "seq", None),
            P(None, "head"),
            P(None, "head"),
            P(None, "head"),
            P(None, "head"),
            P(None, None, "head"),
            P(None, "head"),
            P(None, "head"),
            P(None, "head"),
            P(None, "head"),
            P(),
            P("head", None),
            P(),
            P(),
            P(None, "head"),
            P(None, "head"),
            P("head", None),
            P(None, "seq", None),
        ),
        out_specs=(
            P(None, "seq", None),
            P(None, "seq", None),
            P("seq", "head"),
            P("seq", "head"),
            P("seq", "head"),
            P("seq", "head"),
            P(None, "seq", "head"),
            P(None, "head"),
            P(None, "head"),
            P(None, "head"),
            P(None, "head"),
            P(),
            P("head", "seq"),
            P("seq"),
            P("seq"),
            P("seq", "head"),
            P("seq", "head"),
            P("head", "seq"),
        ),
        check_vma=False,
    )
```

```python
import copy
import functools

import jax
import jax.numpy as jnp
from jax import lax
from jax.experimental import pallas as pl
from jax.experimental.pallas import tpu as pltpu
from jax.sharding import PartitionSpec as P

DK = 128
DV = 256
CONV = 4
HALO = 16
LANES = 128
SCALE = DK ** (-0.5)
F32 = jnp.float32
BF16 = jnp.bfloat16
NN = ((1,), (0,))
NT = ((1,), (1,))
TN = ((0,), (0,))
NOTE = 16
VMEM_LIMIT = 48 * 1024 * 1024
SMALL_LIMIT = 20 * 1024 * 1024


def dot(left, right, dims=NN):
    return lax.dot_general(
        left.astype(BF16), right.astype(BF16), (dims, ((), ())), preferred_element_type=F32
    )


def halves(field):
    high = field.astype(BF16)
    return high, (field - high.astype(F32)).astype(BF16)


def dot3(left, right, dims=NN):
    left_high, left_low = halves(left)
    right_high, right_low = halves(right)
    return dot(left_high, right_high, dims) + (
        dot(left_high, right_low, dims) + dot(left_low, right_high, dims)
    )


def ones_dot(ones, field):
    high, low = halves(field)
    lowest = field - high.astype(F32) - low.astype(F32)
    return dot(ones, high) + (dot(ones, low) + dot(ones, lowest))


def rows_cols(size):
    return (
        lax.broadcasted_iota(jnp.int32, (size, size), 0),
        lax.broadcasted_iota(jnp.int32, (size, size), 1),
    )


def log1p_small(value):
    shifted = 1.0 + value
    same = shifted == 1.0
    safe = jnp.where(same, 1.0, shifted - 1.0)
    return jnp.where(same, value, jnp.log(shifted) * (value / safe))


def log_sigmoid(value):
    return jnp.minimum(value, 0.0) - log1p_small(jnp.exp(-jnp.abs(value)))


def sigmoid(value):
    return 1.0 / (1.0 + jnp.exp(-value))


def row_sum(field):
    return jnp.sum(field, axis=-1, keepdims=True)


def inverse_unit(lowers, rows, cols):
    size = lowers[0].shape[0]
    same = (rows // 16) == (cols // 16)
    eye = (rows == cols).astype(F32)
    powers = [jnp.where(same, -lower, 0.0) for lower in lowers]
    inverses = [eye + power for power in powers]
    for _ in range(3):
        powers = [dot3(power, power) for power in powers]
        inverses = [inv + dot3(inv, power) for inv, power in zip(inverses, powers)]
    block = 16
    while block * 2 <= size:
        inside = ((rows // (2 * block)) == (cols // (2 * block))) & (
            (rows // block) != (cols // block)
        )
        parts = [
            dot3(jnp.where(inside, lower, 0.0), inv) for lower, inv in zip(lowers, inverses)
        ]
        inverses = [inv - dot3(inv, part) for inv, part in zip(inverses, parts)]
        block *= 2
    return inverses


def conv_pre(extended, taps):
    total = taps[CONV - 1 : CONV] * extended
    for offset in range(CONV - 1):
        total = total + taps[offset : offset + 1] * pltpu.roll(extended, CONV - 1 - offset, 0)
    return total[HALO:]


def silu(value):
    return value * sigmoid(value)


def silu_slope(value):
    gate = sigmoid(value)
    return gate * (1.0 + value * (1.0 - gate))


def unit(field):
    inverse = lax.rsqrt(row_sum(field * field) + 1e-06)
    return field * inverse, inverse


def first_body(
    heads, x_ref, gain_ref, wq_ref, wk_ref, wv_ref, wg_ref, wgates_ref, bias_ref, cq_ref, ck_ref,
    cv_ref, proj_ref, pg_ref, gates_ref, sums_ref, inv_ref, mapk_ref, fresh_ref,
    score_ref, reach_ref, local_ref, decay_ref, piece_ref, low_ref, maplow_ref, log_ref, turned_ref,
):
    x = x_ref[0].astype(F32)
    mixed = x * lax.rsqrt(jnp.mean(x * x, axis=-1, keepdims=True) + 1e-06) * gain_ref[...]
    mixed = mixed.astype(BF16)
    main = mixed[HALO:]
    turned_ref[...] = jnp.transpose(main)
    proj_q = dot(mixed, wq_ref[...]).astype(BF16)
    proj_k = dot(mixed, wk_ref[...]).astype(BF16)
    proj_v = dot(mixed, wv_ref[...]).astype(BF16)
    wide = heads * DK
    proj_ref[0, :, :wide] = proj_q
    proj_ref[0, :, wide : 2 * wide] = proj_k
    proj_ref[0, :, 2 * wide :] = proj_v
    pg_ref[0] = dot(main, wg_ref[...])
    gates = dot(main, wgates_ref[...]) + bias_ref[...]
    gates_ref[0] = gates
    size = main.shape[0]
    rows, cols = rows_cols(size)
    lower = rows >= cols
    strict = rows > cols
    sums = ones_dot(lower.astype(BF16), log_sigmoid(gates))
    sums_ref[0] = sums
    sums_t = jnp.transpose(sums)
    conv_q = silu(conv_pre(proj_q.astype(F32), cq_ref[...]))
    conv_k = silu(conv_pre(proj_k.astype(F32), ck_ref[...]))
    conv_v = silu(conv_pre(proj_v.astype(F32), cv_ref[...]))
    each = range(heads)
    queries = [unit(conv_q[:, h * DK : (h + 1) * DK])[0] * SCALE for h in each]
    keys = [unit(conv_k[:, h * DK : (h + 1) * DK])[0] for h in each]
    values = [conv_v[:, h * DV : (h + 1) * DV] for h in each]
    beta = [sigmoid(gates[:, h : h + 1]) for h in each]
    total = [sums[:, heads + h : heads + h + 1] for h in each]
    decay = [
        jnp.where(
            lower, jnp.exp(jnp.minimum(total[h] - sums_t[heads + h : heads + h + 1, :], 0.0)), 0.0
        )
        for h in each
    ]
    scaled = [beta[h] * keys[h] for h in each]
    lowers = [jnp.where(strict, dot3(keys[h], scaled[h], NT) * decay[h], 0.0) for h in each]
    inverses = inverse_unit(lowers, rows, cols)
    growth = [jnp.exp(total[h]) for h in each]
    last = [total[h][size - 1 : size] for h in each]
    tail = [jnp.exp(last[h] - total[h]) * scaled[h] for h in each]
    mapk = [dot3(inverses[h], growth[h] * keys[h]) for h in each]
    fresh = [dot3(inverses[h], values[h]) for h in each]
    scores = [dot(queries[h], scaled[h], NT) * decay[h] for h in each]
    moved = [-dot3(tail[h], mapk[h], TN) for h in each]
    shift = [dot3(tail[h], fresh[h], TN) for h in each]
    reach = [growth[h] * queries[h] - dot(scores[h], mapk[h]) for h in each]
    local = [dot(scores[h], fresh[h]) for h in each]
    for h in each:
        piece_ref[0, h, :, :DK] = moved[h]
        piece_ref[0, h, :, DK:] = shift[h]
        note = log_rows(last[h])
        log_ref[0, h] = jnp.broadcast_to(last[h], (8, LANES))
        maplow_ref[0, h, :DK] = moved[h].astype(BF16)
        maplow_ref[0, h, DK:] = note
        low_ref[0, h, :DK, :DK] = moved[h].astype(BF16)
        low_ref[0, h, :DK, DK:] = shift[h].astype(BF16)
        low_ref[0, h, DK:] = jnp.concatenate([note] * (1 + DV // DK), axis=1)
        inv_ref[0, h] = inverses[h]
        mapk_ref[0, h] = mapk[h]
        fresh_ref[0, h] = fresh[h]
        score_ref[0, h] = scores[h]
        reach_ref[0, h] = reach[h]
        local_ref[0, h] = local[h]
        decay_ref[0, h] = decay[h]


def log_rows(log):
    log = jnp.broadcast_to(log, (1, LANES))
    high = log.astype(BF16).astype(F32)
    middle = (log - high).astype(BF16).astype(F32)
    rest = log - high - middle
    place = lax.broadcasted_iota(jnp.int32, (NOTE, LANES), 0)
    zero = jnp.zeros((NOTE, LANES), F32)
    rows = jnp.where(place == 0, high, jnp.where(place == 1, middle, jnp.where(place == 2, rest, zero)))
    return rows.astype(BF16)


def log_of(rows):
    return jnp.sum(rows.astype(F32), axis=0, keepdims=True)


def join_body(
    pairs, last, piece_ref, log_ref, got_ref, out_ref, newlog_ref, low_ref, maplow_ref, *far_ref
):
    wide = 1 + DV // DK
    for p in range(pairs):
        own = piece_ref[p]
        got_low = got_ref[p, :DK]
        got = got_low.astype(F32)
        own_log = log_ref[p, :1]
        got_log = log_of(got_ref[p, DK:, :LANES])
        mine = jnp.concatenate([jnp.exp(own_log)] * wide, axis=1)
        high, low = halves(own[:, :DK])
        moved = dot(high, got_low) + dot(low, got_low) + mine * got
        map_part = moved[:, :DK] + jnp.exp(got_log) * own[:, :DK]
        shift_part = moved[:, DK:] + own[:, DK:]
        new_log = own_log + got_log
        out_ref[p, :, :DK] = map_part
        out_ref[p, :, DK:] = shift_part
        newlog_ref[p] = jnp.broadcast_to(new_log, (8, LANES))
        low_ref[p, :DK, :DK] = map_part.astype(BF16)
        low_ref[p, :DK, DK:] = shift_part.astype(BF16)
        note = log_rows(new_log)
        low_ref[p, DK:] = jnp.concatenate([note] * wide, axis=1)
        maplow_ref[p, :DK] = map_part.astype(BF16)
        maplow_ref[p, DK:] = note
        if last:
            far_ref[0][p] = shift_part.astype(BF16)


def entry_body(pairs, near_ref, far_ref, out_ref):
    for p in range(pairs):
        far = far_ref[p]
        scale = jnp.exp(log_of(near_ref[p, DK:, DK:]))
        moved = dot(near_ref[p, :DK, :DK], far) + scale * far.astype(F32)
        out_ref[p] = moved + near_ref[p, :DK, DK:].astype(F32)


def back_body(pairs, map_ref, own_ref, got_ref, out_ref, low_ref):
    for p in range(pairs):
        got = got_ref[p]
        scale = jnp.concatenate([jnp.exp(log_of(map_ref[p, DK:]))] * (DV // DK), axis=1)
        out = own_ref[p] + dot(map_ref[p, :DK], got, TN) + scale * got.astype(F32)
        out_ref[p] = out
        low_ref[p] = out.astype(BF16)


def exit_body(pairs, map_ref, near_ref, far_ref, out_ref):
    for p in range(pairs):
        far = far_ref[p]
        scale = jnp.concatenate([jnp.exp(log_of(map_ref[p, DK:]))] * (DV // DK), axis=1)
        moved = dot(map_ref[p, :DK], far, TN) + scale * far.astype(F32)
        out_ref[p] = near_ref[p].astype(F32) + moved


def mixer_out_body(
    heads, state_ref, fresh_ref, mapk_ref, reach_ref, local_ref, pg_ref, gain_ref, wout_ref,
    made_ref, output_ref, gated_ref, attn_ref,
):
    for h in range(heads):
        state = state_ref[0, h]
        made_ref[0, h] = fresh_ref[0, h] - dot3(mapk_ref[0, h], state)
        output = local_ref[0, h] + dot(reach_ref[0, h], state)
        output_ref[0, :, h * DV : (h + 1) * DV] = output
        scale = lax.rsqrt(jnp.mean(output * output, axis=-1, keepdims=True) + 1e-05)
        gate = pg_ref[0, :, h * DV : (h + 1) * DV]
        gated_ref[0, :, h * DV : (h + 1) * DV] = (
            output * scale * gain_ref[...] * silu(gate)
        ).astype(BF16)
    attn_ref[0] = dot(gated_ref[0], wout_ref[...]).astype(BF16)


def feed_body(
    x_ref, mine_ref, other_ref, cot_ref, gain_ref, wgate_ref, wup_ref, wdown_ref, resid_ref,
    hidden_ref, dgate_ref, dup_ref, down_ref, dnorm_ref, normed_ref, cot_turned_ref,
):
    attn = mine_ref[0].astype(F32) + other_ref[0].astype(F32)
    resid = x_ref[0].astype(F32) + attn
    resid_ref[0] = resid
    normed = resid * lax.rsqrt(jnp.mean(resid * resid, axis=-1, keepdims=True) + 1e-06)
    normed = (normed * gain_ref[...]).astype(BF16)
    normed_ref[...] = jnp.transpose(normed)
    cot_turned_ref[...] = jnp.transpose(cot_ref[0])
    gate = dot(normed, wgate_ref[...])
    up = dot(normed, wup_ref[...])
    d_hidden = dot(cot_ref[0], wdown_ref[...], NT)
    sig = sigmoid(gate)
    active = gate * sig
    hidden = (active * up).astype(BF16)
    hidden_ref[0] = hidden
    d_gate = (d_hidden * up * (sig + active * (1.0 - sig))).astype(BF16)
    d_up = (d_hidden * active).astype(BF16)
    dgate_ref[0] = d_gate
    dup_ref[0] = d_up
    down_ref[0] = dot(hidden, wdown_ref[...]).astype(BF16)
    dnorm_ref[0] = (dot(d_gate, wgate_ref[...], NT) + dot(d_up, wup_ref[...], NT)).astype(BF16)


def mixer_back_body(
    heads, resid_ref, mine_ref, other_ref, cot_ref, output_ref, pg_ref, reach_ref, gain_ref,
    wout_ref, ogain_ref, dresid_ref, dout_ref, dpg_ref, back_ref, low_ref, dattn_ref, dgain_ref,
    dogain_ref,
):
    step = pl.program_id(0)
    resid = resid_ref[0]
    inverse = lax.rsqrt(jnp.mean(resid * resid, axis=-1, keepdims=True) + 1e-06)
    unit_resid = resid * inverse
    d_normed = mine_ref[0].astype(F32) + other_ref[0].astype(F32)
    d_gain = jnp.sum(d_normed * unit_resid, axis=0, keepdims=True)
    d_unit = d_normed * gain_ref[...]
    d_resid = inverse * (
        d_unit - unit_resid * jnp.mean(d_unit * unit_resid, axis=-1, keepdims=True)
    )
    d_resid = d_resid + cot_ref[0].astype(F32)
    dresid_ref[0] = d_resid
    d_attn = d_resid.astype(BF16)
    dattn_ref[...] = jnp.transpose(d_attn)
    d_gated = dot(d_attn, wout_ref[...], NT)
    d_ogain = jnp.zeros((1, DV), F32)
    for h in range(heads):
        part = slice(h * DV, (h + 1) * DV)
        output = output_ref[0, :, part]
        inverse = lax.rsqrt(jnp.mean(output * output, axis=-1, keepdims=True) + 1e-05)
        unit_out = output * inverse
        gate = pg_ref[0, :, part]
        grad = d_gated[:, part]
        active = silu(gate)
        d_ogain = d_ogain + jnp.sum(grad * unit_out * active, axis=0, keepdims=True)
        dpg_ref[0, :, part] = (grad * unit_out * ogain_ref[...] * silu_slope(gate)).astype(BF16)
        d_unit = grad * ogain_ref[...] * active
        d_out = inverse * (d_unit - unit_out * jnp.mean(d_unit * unit_out, axis=-1, keepdims=True))
        dout_ref[0, :, part] = d_out
        back = dot(reach_ref[0, h], d_out, TN)
        back_ref[0, h] = back
        low_ref[0, h] = back.astype(BF16)

    @pl.when(step == 0)
    def _():
        dgain_ref[...] = d_gain
        dogain_ref[...] = d_ogain

    @pl.when(step > 0)
    def _():
        dgain_ref[...] += d_gain
        dogain_ref[...] += d_ogain


def conv_back(grad, extended, taps, pre):
    d_pre = grad * silu_slope(pre)
    padded = jnp.concatenate([jnp.zeros((HALO, d_pre.shape[1]), F32), d_pre], axis=0)
    length = padded.shape[0]
    d_ext = taps[CONV - 1 : CONV] * padded
    d_taps = []
    for offset in range(CONV):
        back = CONV - 1 - offset
        if back:
            d_ext = d_ext + taps[offset : offset + 1] * pltpu.roll(padded, length - back, 0)
            shifted = pltpu.roll(extended, back, 0)
        else:
            shifted = extended
        d_taps.append(jnp.sum(padded * shifted, axis=0, keepdims=True))
    return d_ext, jnp.concatenate(d_taps, axis=0)


def early_body(
    heads, proj_ref, gates_ref, sums_ref, dout_ref, state_ref, made_ref, inv_ref, score_ref,
    decay_ref, cq_ref, ck_ref, xone_ref, xmap_ref, dkey_ref, dcol_ref, dext_ref, dtap_ref,
):
    step = pl.program_id(0)
    wide = heads * DK
    ext_q = proj_ref[0, :, :wide].astype(F32)
    ext_k = proj_ref[0, :, wide : 2 * wide].astype(F32)
    pre_q = conv_pre(ext_q, cq_ref[...])
    conv_q = silu(pre_q)
    conv_k = silu(conv_pre(ext_k, ck_ref[...]))
    gates = gates_ref[0]
    sums = sums_ref[0]
    size = gates.shape[0]
    each = range(heads)
    units = [unit(conv_q[:, h * DK : (h + 1) * DK]) for h in each]
    queries = [units[h][0] * SCALE for h in each]
    keys = [unit(conv_k[:, h * DK : (h + 1) * DK])[0] for h in each]
    beta = [sigmoid(gates[:, h : h + 1]) for h in each]
    total = [sums[:, heads + h : heads + h + 1] for h in each]
    growth = [jnp.exp(total[h]) for h in each]
    tail = [jnp.exp(total[h][size - 1 : size] - total[h]) * beta[h] * keys[h] for h in each]
    d_out = [dout_ref[0, :, h * DV : (h + 1) * DV] for h in each]
    d_made = [dot(score_ref[0, h], d_out[h], TN) for h in each]
    d_score = [dot(d_out[h], made_ref[0, h], NT) * decay_ref[0, h] for h in each]
    d_query = [
        dot3(d_score[h], beta[h] * keys[h]) + dot(growth[h] * d_out[h], state_ref[0, h], NT)
        for h in each
    ]
    d_key = [dot3(d_score[h], queries[h], TN) for h in each]
    x_one = [dot(inv_ref[0, h], d_made[h], TN) for h in each]
    x_map = [dot(inv_ref[0, h], tail[h], TN) for h in each]
    lanes = lax.broadcasted_iota(jnp.int32, (size, LANES), 1)
    cols = jnp.zeros((size, LANES), F32)
    grads = []
    for h in each:
        xone_ref[0, h] = x_one[h]
        xmap_ref[0, h] = x_map[h]
        dkey_ref[0, h] = beta[h] * d_key[h]
        key_sum = row_sum(d_key[h] * keys[h])
        cols = cols + jnp.where(lanes == h, key_sum, 0.0)
        d_total = row_sum(d_query[h] * queries[h]) - beta[h] * key_sum
        cols = cols + jnp.where(lanes == heads + h, d_total, 0.0)
        unit_q, inverse = units[h]
        d_unit = d_query[h] * SCALE
        grads.append(inverse * (d_unit - unit_q * row_sum(d_unit * unit_q)))
    dcol_ref[0] = cols
    d_ext, d_taps = conv_back(jnp.concatenate(grads, axis=1), ext_q, cq_ref[...], pre_q)
    dext_ref[0] = d_ext

    @pl.when(step == 0)
    def _():
        dtap_ref[...] = d_taps

    @pl.when(step > 0)
    def _():
        dtap_ref[...] += d_taps


def late_body(
    heads, proj_ref, gates_ref, sums_ref, dend_ref, state_ref, made_ref, decay_ref, xone_ref,
    xmap_ref, dkey_ref, dcol_ref, dextq_ref, ck_ref, cv_ref, dext_ref, dgates_ref, dtap_ref, dbias_ref,
):
    step = pl.program_id(0)
    wide = heads * DK
    ext_k = proj_ref[0, :, wide : 2 * wide].astype(F32)
    ext_v = proj_ref[0, :, 2 * wide :].astype(F32)
    pre_k = conv_pre(ext_k, ck_ref[...])
    pre_v = conv_pre(ext_v, cv_ref[...])
    conv_k = silu(pre_k)
    gates = gates_ref[0]
    sums = sums_ref[0]
    size = gates.shape[0]
    rows, cols = rows_cols(size)
    strict = rows > cols
    each = range(heads)
    units = [unit(conv_k[:, h * DK : (h + 1) * DK]) for h in each]
    keys = [units[h][0] for h in each]
    beta = [sigmoid(gates[:, h : h + 1]) for h in each]
    total = [sums[:, heads + h : heads + h + 1] for h in each]
    growth = [jnp.exp(total[h]) for h in each]
    left = [jnp.exp(total[h][size - 1 : size] - total[h]) for h in each]
    d_end = [dend_ref[0, h] for h in each]
    made = [made_ref[0, h] for h in each]
    state = [state_ref[0, h] for h in each]
    d_rhs = [xone_ref[0, h] + dot(xmap_ref[0, h], d_end[h]) for h in each]
    d_tail = [dot(made[h], d_end[h], NT) for h in each]
    d_lower = [
        jnp.where(strict, -dot(d_rhs[h], made[h], NT) * decay_ref[0, h], 0.0) for h in each
    ]
    d_plain = [
        dot3(d_lower[h], beta[h] * keys[h]) - dot(growth[h] * d_rhs[h], state[h], NT) for h in each
    ]
    d_turned = [dot3(d_lower[h], keys[h], TN) for h in each]
    lanes = lax.broadcasted_iota(jnp.int32, (size, LANES), 1)
    places = lax.broadcasted_iota(jnp.int32, (size, 1), 0)
    d_col = dcol_ref[0]
    grads_k = []
    for h in each:
        turned = row_sum(d_turned[h] * keys[h])
        tails = row_sum(d_tail[h] * keys[h])
        tail_weight = left[h] * beta[h]
        d_key = d_plain[h] + beta[h] * d_turned[h] + tail_weight * d_tail[h] + dkey_ref[0, h]
        d_total = row_sum(d_plain[h] * keys[h]) - beta[h] * turned - tail_weight * tails
        ended = jnp.sum(tail_weight * tails, axis=0, keepdims=True)
        whole = jnp.sum(row_sum(d_end[h] * state[h]), axis=0, keepdims=True)
        ended = ended + growth[h][size - 1 : size] * whole
        d_total = d_total + jnp.where(places == size - 1, ended, 0.0)
        d_col = d_col + jnp.where(lanes == h, turned + left[h] * tails, 0.0)
        d_col = d_col + jnp.where(lanes == heads + h, d_total, 0.0)
        unit_k, inverse = units[h]
        grads_k.append(inverse * (d_key - unit_k * row_sum(d_key * unit_k)))
    upper = (rows <= cols).astype(BF16)
    d_decay = ones_dot(upper, d_col)
    rate = sigmoid(gates)
    d_gates = jnp.where(
        lanes < heads, d_col * rate * (1.0 - rate), d_decay / (1.0 + jnp.exp(gates))
    )
    d_gates = jnp.where(lanes < 2 * heads, d_gates, 0.0)
    dgates_ref[0] = d_gates.astype(BF16)
    d_bias = jnp.sum(d_gates, axis=0, keepdims=True)
    dext_k, dtaps_k = conv_back(jnp.concatenate(grads_k, axis=1), ext_k, ck_ref[...], pre_k)
    dext_v, dtaps_v = conv_back(jnp.concatenate(d_rhs, axis=1), ext_v, cv_ref[...], pre_v)
    dext_ref[0, :, :wide] = dextq_ref[0]
    dext_ref[0, :, wide : 2 * wide] = dext_k
    dext_ref[0, :, 2 * wide :] = dext_v

    @pl.when(step == 0)
    def _():
        dtap_ref[:, :wide] = dtaps_k
        dtap_ref[:, wide:] = dtaps_v
        dbias_ref[...] = d_bias

    @pl.when(step > 0)
    def _():
        dtap_ref[:, :wide] += dtaps_k
        dtap_ref[:, wide:] += dtaps_v
        dbias_ref[...] += d_bias


def input_back_body(
    dext_ref, edge_ref, dpg_ref, dgates_ref, wq_ref, wk_ref, wv_ref, wg_ref, wgates_ref,
    dqk_ref, dv_ref, dmixed_ref,
):
    wide = wq_ref.shape[1]
    own = dext_ref[0, HALO:]
    size = own.shape[0]
    d_proj = jnp.concatenate([own[: size - HALO], own[size - HALO :] + edge_ref[0]], axis=0)
    d_proj = d_proj.astype(BF16)
    dqk_ref[0] = d_proj[:, : 2 * wide]
    dv_ref[0] = d_proj[:, 2 * wide :]
    d_mixed = dot(d_proj[:, :wide], wq_ref[...], NT)
    d_mixed = d_mixed + dot(d_proj[:, wide : 2 * wide], wk_ref[...], NT)
    d_mixed = d_mixed + dot(d_proj[:, 2 * wide :], wv_ref[...], NT)
    d_mixed = d_mixed + dot(dpg_ref[0], wg_ref[...], NT)
    d_mixed = d_mixed + dot(dgates_ref[0], wgates_ref[...], NT)
    dmixed_ref[0] = d_mixed.astype(BF16)


def last_body(
    x_ref, mine_ref, other_ref, dresid_ref, gain_ref, grad_ref, dgain_ref,
):
    x = x_ref[0].astype(F32)
    inverse = lax.rsqrt(jnp.mean(x * x, axis=-1, keepdims=True) + 1e-06)
    unit_x = x * inverse
    d_mixed = mine_ref[0].astype(F32) + other_ref[0].astype(F32)
    d_unit = d_mixed * gain_ref[...]
    back = inverse * (d_unit - unit_x * jnp.mean(d_unit * unit_x, axis=-1, keepdims=True))
    grad_ref[0] = dresid_ref[0] + back
    d_gain = jnp.sum(d_mixed * unit_x, axis=0, keepdims=True)
    step = pl.program_id(0)

    @pl.when(step == 0)
    def _():
        dgain_ref[...] = d_gain

    @pl.when(step > 0)
    def _():
        dgain_ref[...] += d_gain


def result_body(resid_ref, down_ref, downother_ref, result_ref):
    down = down_ref[0].astype(F32) + downother_ref[0].astype(F32)
    result_ref[0] = (resid_ref[0] + down).astype(BF16)


def held_rows(left_refs, index_ref, first, blocks, held):
    share = left_refs[0].shape[1]
    for number, left_ref in enumerate(left_refs):
        for place in range(blocks):
            held[number, place * share : (place + 1) * share] = left_ref[index_ref[first + place]]


def send_body(terms, first, blocks, lefts, index_ref, *refs):
    out_ref, held = refs[-2:]
    held_rows(refs[:lefts], index_ref, first, blocks, held)
    at = 0
    for left, right, width in terms:
        out_ref[:, at : at + width] = dot(held[left], refs[lefts + right][...]).astype(BF16)
        at += width


def keep_body(terms, blocks, parts, lefts, index_ref, *refs):
    rights = len(terms)
    got_ref = refs[lefts + rights]
    keep_ref, held = refs[lefts + rights + 1], refs[-1]
    send_refs = refs[lefts + rights + 2 : -1]
    held_rows(refs[:lefts], index_ref, 0, blocks, held)
    rows = keep_ref.shape[0]
    at = 0
    for left, right, width in terms:
        total = dot(held[left], refs[lefts + right][...])
        total = total + got_ref[:, at : at + width].astype(F32)
        keep_ref[:, at : at + width] = total[:rows]
        for part in range(1, parts):
            send_refs[part - 1][:, at : at + width] = total[part * rows : (part + 1) * rows].astype(BF16)
        at += width


def add_body(parts, gots, keep_ref, *refs):
    total = keep_ref[...]
    for got_ref in refs[:gots]:
        total = total + got_ref[...].astype(F32)
    out_ref = refs[gots]
    rows = out_ref.shape[0]
    out_ref[...] = total[:rows]
    for part in range(1, parts):
        refs[gots + part][...] = total[part * rows : (part + 1) * rows].astype(BF16)


def joined_body(widths, *refs):
    keep_ref, send_ref = refs[-2:]
    rows = keep_ref.shape[0]
    at = 0
    for number, width in enumerate(widths):
        total = refs[2 * number][...] + refs[2 * number + 1][...].astype(F32)
        keep_ref[:, at : at + width] = total[:rows]
        send_ref[:, at : at + width] = total[rows:].astype(BF16)
        at += width


def total_body(cuts, gots, *refs):
    at = 0
    for ref, width in zip(refs[1 + gots :], cuts):
        total = refs[0][:, at : at + width]
        for got_ref in refs[1 : 1 + gots]:
            total = total + got_ref[:, at : at + width].astype(F32)
        ref[...] = total
        at += width


def pack_body(tapq_ref, tapkv_ref, bias_ref, ffn_ref, mix_ref, ogain_ref, other_ref, out_ref):
    wide = tapq_ref.shape[1]
    out_ref[...] = jnp.zeros_like(out_ref)
    out_ref[:CONV, :wide] = tapq_ref[...]
    out_ref[:CONV, wide:] = tapkv_ref[...]
    out_ref[4:5, :LANES] = bias_ref[...]
    out_ref[5:6] = ffn_ref[...]
    out_ref[6:7] = mix_ref[...]
    out_ref[7:8, :DV] = ogain_ref[...] + other_ref[...]


def sum_body(count, *refs):
    total = refs[0][...]
    for ref in refs[1:count]:
        total = total + ref[...]
    refs[count][...] = total


def by_seq(shape):
    rest = len(shape) - 1
    return pl.BlockSpec((1,) + tuple(shape[1:]), lambda s: (s,) + (0,) * rest)


def whole(shape):
    rest = len(shape)
    return pl.BlockSpec(tuple(shape), lambda s: (0,) * rest)


def without(body, position, count):
    def shorter(*refs):
        return body(*refs[:position], *refs[position + count :])

    return shorter if count else body


def call(body, name, seqs, parts, shared, outs, sums=(), turned=(), after=(), flops=0):
    operands = list(parts) + list(shared)
    listed = list(outs) + list(turned) + list(sums)
    out_shape = [jax.ShapeDtypeStruct(shape, kind) for shape, kind in listed]
    moved = sum(a.size * a.dtype.itemsize for a in operands + out_shape)
    return pl.pallas_call(
        without(body, len(operands), len(after)),
        grid=(seqs,),
        in_specs=[by_seq(a.shape) for a in parts]
        + [whole(a.shape) for a in shared]
        + [pl.BlockSpec(memory_space=pl.ANY)] * len(after),
        out_specs=[by_seq(shape) for shape, _ in outs]
        + [pl.BlockSpec((shape[0], shape[1] // seqs), lambda s: (0, s)) for shape, _ in turned]
        + [whole(shape) for shape, _ in sums],
        out_shape=out_shape,
        compiler_params=pltpu.CompilerParams(vmem_limit_bytes=VMEM_LIMIT),
        cost_estimate=pl.CostEstimate(flops=int(flops), bytes_accessed=int(moved), transcendentals=0),
        name=name,
    )(*operands, *after)


def small_call(body, name, arrays, outs, after=(), scalars=(), scratch=(), flops=2e8):
    out_shape = [jax.ShapeDtypeStruct(shape, kind) for shape, kind in outs]
    moved = sum(a.size * a.dtype.itemsize for a in list(arrays) + out_shape)
    return pl.pallas_call(
        without(body, len(scalars) + len(arrays), len(after)),
        in_specs=[pl.BlockSpec(memory_space=pltpu.SMEM)] * len(scalars)
        + [pl.BlockSpec(memory_space=pltpu.VMEM)] * len(arrays)
        + [pl.BlockSpec(memory_space=pl.ANY)] * len(after),
        out_specs=[pl.BlockSpec(memory_space=pltpu.VMEM)] * len(outs),
        out_shape=out_shape,
        scratch_shapes=list(scratch),
        compiler_params=pltpu.CompilerParams(vmem_limit_bytes=SMALL_LIMIT),
        cost_estimate=pl.CostEstimate(flops=int(flops), bytes_accessed=int(moved), transcendentals=0),
        name=name,
    )(*scalars, *arrays, *after)


class Halved:
    def __init__(self, name, steps, me, lefts, rights, terms):
        self.name, self.lefts, self.rights, self.terms = (name, lefts, rights, terms)
        order = [bit for step in steps for bit in step]
        self.steps = steps
        self.index = block_index(order, me)
        self.count = 1 << len(order)
        _, self.share, self.tokens = lefts[0].shape
        self.columns = sum(width for _, _, width in terms)
        self.done = 0

    def trade(self, sends):
        bits = self.steps[self.done]
        self.done += 1
        self.gots = []
        for part, send in enumerate(sends, 1):
            moved = sum(
                ((part >> (len(bits) - 1 - place)) & 1) << bit for place, bit in enumerate(bits)
            )
            self.gots.append(traded(send, moved))

    def multiplied(self, body, suffix, extra, outs, after):
        blocks = self.count // 2
        return small_call(
            body, self.name + suffix, list(self.lefts) + list(self.rights) + extra, outs, after,
            scalars=[self.index],
            scratch=[pltpu.VMEM((len(self.lefts), blocks * self.share, self.tokens), BF16)],
            flops=2 * blocks * self.share * self.tokens * self.columns,
        )

    def outs(self, rows):
        parts = 1 << len(self.steps[self.done])
        return parts, [((rows // parts, self.columns), F32)] + [
            ((rows // parts, self.columns), BF16)
        ] * (parts - 1)

    def send(self, *after):
        blocks = self.count // 2
        body = functools.partial(send_body, self.terms, blocks, blocks, len(self.lefts))
        rows = blocks * self.share
        sends = self.multiplied(body, "_send", [], [((rows, self.columns), BF16)], after)
        self.trade(sends)
        return sends[0]

    def keep(self, *after):
        blocks = self.count // 2
        parts, outs = self.outs(blocks * self.share)
        body = functools.partial(keep_body, self.terms, blocks, parts, len(self.lefts))
        self.kept, *sends = self.multiplied(body, "_keep", self.gots, outs, after)
        self.trade(sends)
        return self.kept

    def add(self, *after):
        parts, outs = self.outs(self.kept.shape[0])
        body = functools.partial(add_body, parts, len(self.gots))
        self.kept, *sends = small_call(
            body, self.name + "_add", [self.kept] + self.gots, outs, after, flops=1e6
        )
        self.trade(sends)
        return self.kept

    def left(self):
        return len(self.steps) - self.done

    def total(self, cuts, *after):
        rows = self.kept.shape[0]
        outs = [((rows, width), F32) for width in cuts]
        return small_call(
            functools.partial(total_body, tuple(cuts), len(self.gots)), self.name + "_total",
            [self.kept] + self.gots, outs, after, flops=1e6,
        )


def joined(name, groups, *after):
    whole_sum = copy.copy(groups[0])
    whole_sum.name = name
    whole_sum.columns = sum(group.columns for group in groups)
    rows = groups[0].kept.shape[0] // 2
    shape = (rows, whole_sum.columns)
    operands = [array for group in groups for array in [group.kept] + group.gots]
    body = functools.partial(joined_body, [group.columns for group in groups])
    whole_sum.kept, send = small_call(
        body, name, operands, [(shape, F32), (shape, BF16)], after, flops=1e6
    )
    whole_sum.trade([send])
    return whole_sum


def halving_steps(count, first):
    bits = list(range(count.bit_length() - 1))
    return [[bit] for bit in first] + [[bit] for bit in bits if bit not in first]


def block_index(order, me):
    count = 1 << len(order)
    moved = [
        sum(((place >> (len(order) - 1 - step)) & 1) << bit for step, bit in enumerate(order))
        for place in range(count)
    ]
    return jnp.bitwise_xor(jnp.array(moved, jnp.int32), me)


def traded(block, moved):
    count = lax.axis_size("seq")
    return lax.ppermute(block, "seq", [(i, i ^ moved) for i in range(count)])


def passed_along(block, axis, distance):
    devices = range(lax.axis_size(axis))
    route = [(i - distance, i) for i in devices if i - distance in devices]
    return lax.ppermute(block, axis, route)


def swapped(block):
    count = lax.axis_size("head")
    return lax.ppermute(block, "head", [(i, i ^ 1) for i in range(count)])


def on_device(
    tokens, w_query, w_key, w_value, w_outgate, w_gates, gate_bias, conv_query, conv_key,
    conv_value, out_gain, w_out, mix_gain, ffn_gain, w_gate, w_up, w_down, cotangent,
):
    seqs, size, width = tokens.shape
    heads = gate_bias.shape[1]
    pairs = seqs * heads
    units = w_gate.shape[1]
    count, me = lax.axis_size("seq"), lax.axis_index("seq")
    wide = heads * DK
    out_wide = heads * DV
    proj_wide = 2 * wide + out_wide

    halo = passed_along(tokens[:, size - HALO :], "seq", 1)
    x_ext = jnp.concatenate([halo, tokens], axis=1)
    gates_w = jnp.swapaxes(w_gates, 0, 1).reshape(width, 2 * heads)
    gates_w = jnp.pad(gates_w, ((0, 0), (0, LANES - 2 * heads)))
    bias = jnp.pad(gate_bias.reshape(1, 2 * heads), ((0, 0), (0, LANES - 2 * heads)))
    mix_row = mix_gain.reshape(1, width)
    ffn_row = ffn_gain.reshape(1, width)
    out_row = out_gain.reshape(1, DV)
    square = (seqs, heads, size, size)
    by_key = (seqs, heads, size, DK)
    by_value = (seqs, heads, size, DV)
    tokens_here = seqs * size
    steps_x, steps_y = halving_steps(count, (0, 1)), halving_steps(count, (1, 0))
    steps_yzx, steps_zxy = halving_steps(count, (1, 2, 0)), halving_steps(count, (2, 0, 1))
    turned_shape = (width, tokens_here)
    share = width // count

    def in_blocks(turned):
        return turned.reshape(count, share, tokens_here)

    def flat(field):
        return field.reshape(tokens_here, field.shape[2])

    (
        proj, proj_g, gates, sums, inv, mapk, fresh, score, reach, local, decay, piece, low,
        map_low, log, mixed_t,
    ) = call(
        functools.partial(first_body, heads), "project_and_local", seqs, [x_ext],
        [mix_row, w_query, w_key, w_value, w_outgate, gates_w, bias, conv_query, conv_key, conv_value],
        [
            ((seqs, size + HALO, proj_wide), BF16),
            ((seqs, size, out_wide), F32), ((seqs, size, LANES), F32), ((seqs, size, LANES), F32),
            (square, F32), (by_key, F32), (by_value, F32), (square, F32), (by_key, F32),
            (by_value, F32), (square, F32), ((seqs, heads, DK, DK + DV), F32),
            ((seqs, heads, DK + NOTE, DK + DV), BF16),
            ((seqs, heads, DK + NOTE, DK), BF16), ((seqs, heads, 8, LANES), F32),
        ],
        turned=[(turned_shape, BF16)],
        flops=1e10,
    )

    piece = piece.reshape(pairs, DK, DK + DV)
    low = low.reshape(pairs, DK + NOTE, DK + DV)
    log = log.reshape(pairs, 8, LANES)
    maps = [map_low.reshape(pairs, DK + NOTE, DK)]
    state_shape = (pairs, DK, DV)
    dists = []
    reach_by = 1
    while reach_by * 2 < count:
        dists.append(reach_by)
        reach_by *= 2
    for level, d in enumerate(dists):
        got = passed_along(low, "seq", d)
        last = level + 1 == len(dists)
        outs = [(piece.shape, F32), (log.shape, F32), (low.shape, BF16), (maps[0].shape, BF16)]
        if last:
            outs.append((state_shape, BF16))
        piece, log, low, map_low, *far = small_call(
            functools.partial(join_body, pairs, last), "join", [piece, log, got], outs
        )
        maps.append(map_low)
    near = passed_along(low, "seq", 1)
    far = passed_along(far[0], "seq", 1 + reach_by)
    back_maps = [maps[0]]
    for level in range(1, len(dists)):
        back_maps.append(passed_along(maps[level], "seq", 1 - dists[level]))
    near_map = passed_along(maps[-1], "seq", -reach_by)
    (state,) = small_call(
        functools.partial(entry_body, pairs), "entry", [near, far], [(state_shape, F32)]
    )
    state = state.reshape(seqs, heads, DK, DV)

    made, output, gated, attn = call(
        functools.partial(mixer_out_body, heads), "mixer_out", seqs,
        [state, fresh, mapk, reach, local, proj_g], [out_row, w_out],
        [
            (by_value, F32), ((seqs, size, out_wide), F32), ((seqs, size, out_wide), BF16),
            ((seqs, size, width), BF16),
        ],
        after=[near_map] + back_maps[1:],
        flops=1.5e9,
    )
    attn_other = swapped(attn)

    resid, hidden, d_gate, d_up, down, d_norm, normed_t, cot_t = call(
        feed_body, "feed_forward", seqs, [tokens, attn, attn_other, cotangent],
        [ffn_row, w_gate, w_up, w_down],
        [
            ((seqs, size, width), F32), ((seqs, size, units), BF16), ((seqs, size, units), BF16),
            ((seqs, size, units), BF16), ((seqs, size, width), BF16), ((seqs, size, width), BF16),
        ],
        turned=[(turned_shape, BF16), (turned_shape, BF16)],
        flops=1.2e10,
    )
    d_norm_other = swapped(d_norm)
    down_other = swapped(down)

    normed_b, cot_b, mixed_b = in_blocks(normed_t), in_blocks(cot_t), in_blocks(mixed_t)
    gate_sum = Halved("gate", steps_x, me, [normed_b], [flat(d_gate)], ((0, 0, units),))
    up_sum = Halved("up", steps_yzx, me, [normed_b], [flat(d_up)], ((0, 0, units),))
    down_sum = Halved("down", steps_zxy, me, [cot_b], [flat(hidden)], ((0, 0, units),))
    done = down_sum.send(up_sum.send(gate_sum.send()))

    d_resid, d_out, d_pg, back, low, d_attn_t, d_ffn_gain, d_out_gain = call(
        functools.partial(mixer_back_body, heads), "mixer_back", seqs,
        [resid, d_norm, d_norm_other, cotangent, output, proj_g, reach],
        [ffn_row, w_out, out_row],
        [
            ((seqs, size, width), F32), ((seqs, size, out_wide), F32),
            ((seqs, size, out_wide), BF16), ((seqs, heads, DK, DV), F32),
            ((seqs, heads, DK, DV), BF16),
        ],
        [((1, width), F32), ((1, DV), F32)],
        turned=[(turned_shape, BF16)],
        after=[done],
        flops=1.5e9,
    )

    outs_sum = Halved(
        "outs", steps_zxy, me, [in_blocks(d_attn_t), mixed_b], [flat(gated), flat(d_pg)],
        ((0, 0, out_wide), (1, 1, out_wide)),
    )
    back = back.reshape(state_shape)
    low = low.reshape(state_shape)
    x_one, x_map, d_key, d_col, dext_q, dtap_q = call(
        functools.partial(early_body, heads), "delta_back_early", seqs,
        [proj, gates, sums, d_out, state, made, inv, score, decay], [conv_query, conv_key],
        [
            (by_value, F32), (by_key, F32), (by_key, F32), ((seqs, size, LANES), F32),
            ((seqs, size + HALO, wide), F32),
        ],
        [((CONV, wide), F32)],
        flops=3e9,
    )
    (result,) = call(
        result_body, "result", seqs, [resid, down, down_other], [],
        [((seqs, size, width), BF16)], after=[d_col],
    )
    done = result
    for level, d in enumerate(dists):
        got = passed_along(low, "seq", -d)
        if level == 1:
            done = down_sum.keep(up_sum.keep(gate_sum.keep(done)))
        back, low = small_call(
            functools.partial(back_body, pairs), "join_back", [back_maps[level], back, got],
            [(state_shape, F32), (state_shape, BF16)], after=[done],
        )
        done = low
    near = passed_along(low, "seq", -1)
    far = passed_along(low, "seq", -1 - reach_by)
    done = down_sum.add(up_sum.add(gate_sum.add(done)))
    (d_end,) = small_call(
        functools.partial(exit_body, pairs), "exit", [near_map, near, far], [(state_shape, F32)],
        after=[done],
    )
    done = outs_sum.send(d_end)
    d_end = d_end.reshape(seqs, heads, DK, DV)
    d_ext, d_gates, dtap_kv, d_bias = call(
        functools.partial(late_body, heads), "delta_back_late", seqs,
        [
            proj, gates, sums, d_end, state, made, decay, x_one, x_map, d_key, d_col, dext_q,
        ],
        [conv_key, conv_value],
        [((seqs, size + HALO, proj_wide), F32), ((seqs, size, LANES), BF16)],
        [((CONV, wide + out_wide), F32), ((1, LANES), F32)],
        after=[done],
        flops=3e9,
    )
    edges = passed_along(d_ext[:, :HALO], "seq", -1)
    feed_sum = joined("feed_last", [gate_sum, up_sum, down_sum], d_bias)
    done = feed_sum.kept
    d_qk, d_v, d_mixed = call(
        input_back_body, "input_back", seqs, [d_ext, edges, d_pg, d_gates],
        [w_query, w_key, w_value, w_outgate, gates_w],
        [
            ((seqs, size, 2 * wide), BF16), ((seqs, size, out_wide), BF16),
            ((seqs, size, width), BF16),
        ],
        after=[done],
        flops=1.7e9,
    )
    d_mixed_other = swapped(d_mixed)
    query_sum = Halved(
        "query_key", steps_x, me, [mixed_b], [flat(d_qk), flat(d_gates)],
        ((0, 0, 2 * wide), (0, 1, LANES)),
    )
    value_sum = Halved("value", steps_y, me, [mixed_b], [flat(d_v)], ((0, 0, out_wide),))
    done = outs_sum.keep(value_sum.send(query_sum.send(d_mixed)))
    grad_input, d_mix_gain = call(
        last_body, "first_norm_back", seqs, [tokens, d_mixed, d_mixed_other, d_resid], [mix_row],
        [((seqs, size, width), F32)], [((1, width), F32)], after=[done],
    )

    (small,) = small_call(
        pack_body, "pack",
        [dtap_q, dtap_kv, d_bias, d_ffn_gain, d_mix_gain, d_out_gain, swapped(d_out_gain)],
        [((8, width), F32)], flops=1e4,
    )

    def finish(group, cuts, done):
        while group.left():
            done = group.add(done)
        return group.total(cuts, done)

    def small_step(bit, done):
        return small_call(
            functools.partial(sum_body, 2), "small_sum", [small, traded(small, 1 << bit)],
            [(small.shape, F32)], after=[done], flops=1e4,
        )[0]

    bits = [step[0] for step in steps_x]
    done = value_sum.keep(query_sum.keep(small))
    grad_gate, grad_up, grad_down = finish(feed_sum, [units] * 3, done)
    done = outs_sum.add(grad_gate)
    done = small = small_step(bits.pop(0), done)
    ins_sum = joined("ins_join", [query_sum, value_sum], done)
    done = small = small_step(bits.pop(0), ins_sum.kept)
    ins_sum = joined("ins_last", [ins_sum, outs_sum], done)
    done = small = small_step(bits.pop(0), ins_sum.kept)
    grad_query, grad_key, grad_gates, grad_value, grad_out, grad_outgate = finish(
        ins_sum, [wide, wide, LANES, out_wide, out_wide, out_wide], done
    )
    done = grad_query
    while bits:
        done = small = small_step(bits.pop(0), done)
    grad_gates = grad_gates[:, : 2 * heads].reshape(share, 2, heads)

    def mine_of(row):
        return lax.dynamic_slice(small, (row, me * share), (1, share)).reshape(share)

    return (
        result,
        grad_input,
        grad_query,
        grad_key,
        grad_value,
        grad_outgate,
        jnp.swapaxes(grad_gates, 0, 1),
        small[4, : 2 * heads].reshape(2, heads),
        small[:CONV, :wide],
        small[:CONV, wide : 2 * wide],
        small[:CONV, 2 * wide : proj_wide],
        small[7, :DV],
        jnp.swapaxes(grad_out, 0, 1),
        mine_of(6),
        mine_of(5),
        grad_gate,
        grad_up,
        jnp.swapaxes(grad_down, 0, 1),
    )


def solution(mesh):
    return jax.shard_map(
        on_device,
        mesh=mesh,
        in_specs=(
            P(None, "seq", None),
            P(None, "head"),
            P(None, "head"),
            P(None, "head"),
            P(None, "head"),
            P(None, None, "head"),
            P(None, "head"),
            P(None, "head"),
            P(None, "head"),
            P(None, "head"),
            P(),
            P("head", None),
            P(),
            P(),
            P(None, "head"),
            P(None, "head"),
            P("head", None),
            P(None, "seq", None),
        ),
        out_specs=(
            P(None, "seq", None),
            P(None, "seq", None),
            P("seq", "head"),
            P("seq", "head"),
            P("seq", "head"),
            P("seq", "head"),
            P(None, "seq", "head"),
            P(None, "head"),
            P(None, "head"),
            P(None, "head"),
            P(None, "head"),
            P(),
            P("head", "seq"),
            P("seq"),
            P("seq"),
            P("seq", "head"),
            P("seq", "head"),
            P("head", "seq"),
        ),
        check_vma=False,
    )
```

```python
import copy
import functools

import jax
import jax.numpy as jnp
from jax import lax
from jax.experimental import pallas as pl
from jax.experimental.pallas import tpu as pltpu
from jax.sharding import PartitionSpec as P

DK = 128
DV = 256
CONV = 4
HALO = 16
LANES = 128
SCALE = DK ** (-0.5)
F32 = jnp.float32
BF16 = jnp.bfloat16
NN = ((1,), (0,))
NT = ((1,), (1,))
TN = ((0,), (0,))
NOTE = 16
VMEM_LIMIT = 60 * 1024 * 1024
SMALL_LIMIT = 20 * 1024 * 1024


def dot(left, right, dims=NN):
    return lax.dot_general(
        left.astype(BF16), right.astype(BF16), (dims, ((), ())), preferred_element_type=F32
    )


def halves(field):
    high = field.astype(BF16)
    return high, (field - high.astype(F32)).astype(BF16)


def dot3(left, right, dims=NN):
    left_high, left_low = halves(left)
    right_high, right_low = halves(right)
    return dot(left_high, right_high, dims) + (
        dot(left_high, right_low, dims) + dot(left_low, right_high, dims)
    )


def ones_dot(ones, field):
    high, low = halves(field)
    lowest = field - high.astype(F32) - low.astype(F32)
    return dot(ones, high) + (dot(ones, low) + dot(ones, lowest))


def rows_cols(size):
    return (
        lax.broadcasted_iota(jnp.int32, (size, size), 0),
        lax.broadcasted_iota(jnp.int32, (size, size), 1),
    )


def log1p_small(value):
    shifted = 1.0 + value
    same = shifted == 1.0
    safe = jnp.where(same, 1.0, shifted - 1.0)
    return jnp.where(same, value, jnp.log(shifted) * (value / safe))


def log_sigmoid(value):
    return jnp.minimum(value, 0.0) - log1p_small(jnp.exp(-jnp.abs(value)))


def sigmoid(value):
    return 1.0 / (1.0 + jnp.exp(-value))


def row_sum(field):
    return jnp.sum(field, axis=-1, keepdims=True)


def inverse_unit(lowers, rows, cols):
    size = lowers[0].shape[0]
    same = (rows // 16) == (cols // 16)
    eye = (rows == cols).astype(F32)
    powers = [jnp.where(same, -lower, 0.0) for lower in lowers]
    inverses = [eye + power for power in powers]
    for _ in range(3):
        powers = [dot(power, power) for power in powers]
        inverses = [inv + dot(inv, power) for inv, power in zip(inverses, powers)]
    block = 16
    while block * 2 <= size:
        inside = ((rows // (2 * block)) == (cols // (2 * block))) & (
            (rows // block) != (cols // block)
        )
        parts = [dot(jnp.where(inside, lower, 0.0), inv) for lower, inv in zip(lowers, inverses)]
        inverses = [inv - dot(inv, part) for inv, part in zip(inverses, parts)]
        block *= 2
    errors = [eye - inv - dot3(lower, inv) for lower, inv in zip(lowers, inverses)]
    return [inv + dot(inv, error) for inv, error in zip(inverses, errors)]


def conv_pre(extended, taps):
    total = taps[CONV - 1 : CONV] * extended
    for offset in range(CONV - 1):
        total = total + taps[offset : offset + 1] * pltpu.roll(extended, CONV - 1 - offset, 0)
    return total[HALO:]


def silu(value):
    return value * sigmoid(value)


def silu_slope(value):
    gate = sigmoid(value)
    return gate * (1.0 + value * (1.0 - gate))


def unit(field):
    inverse = lax.rsqrt(row_sum(field * field) + 1e-06)
    return field * inverse, inverse


def first_body(
    heads, halo_ref, x_ref, gain_ref, wq_ref, wk_ref, wv_ref, wg_ref, wgates_ref, bias_ref, cq_ref, ck_ref,
    cv_ref, proj_ref, pg_ref, gates_ref, sums_ref, inv_ref, mapk_ref, fresh_ref,
    score_ref, reach_ref, local_ref, decay_ref, piece_ref, low_ref, maplow_ref, log_ref, mixhalo_ref, turned_ref,
):
    x = jnp.concatenate([halo_ref[0], x_ref[0]], axis=0).astype(F32)
    mixed = x * lax.rsqrt(jnp.mean(x * x, axis=-1, keepdims=True) + 1e-06) * gain_ref[...]
    mixed = mixed.astype(BF16)
    main = mixed[HALO:]
    mixhalo_ref[0] = mixed[:HALO]
    turned_ref[...] = jnp.transpose(main)
    proj_q = dot(mixed, wq_ref[...]).astype(BF16)
    proj_k = dot(mixed, wk_ref[...]).astype(BF16)
    proj_v = dot(mixed, wv_ref[...]).astype(BF16)
    wide = heads * DK
    proj_ref[0, :, :wide] = proj_q
    proj_ref[0, :, wide : 2 * wide] = proj_k
    proj_ref[0, :, 2 * wide :] = proj_v
    pg_ref[0] = dot(main, wg_ref[...])
    gates = dot(main, wgates_ref[...]) + bias_ref[...]
    gates_ref[0] = gates
    size = main.shape[0]
    rows, cols = rows_cols(size)
    lower = rows >= cols
    strict = rows > cols
    sums = ones_dot(lower.astype(BF16), log_sigmoid(gates))
    sums_ref[0] = sums
    sums_t = jnp.transpose(sums)
    conv_q = silu(conv_pre(proj_q.astype(F32), cq_ref[...]))
    conv_k = silu(conv_pre(proj_k.astype(F32), ck_ref[...]))
    conv_v = silu(conv_pre(proj_v.astype(F32), cv_ref[...]))
    each = range(heads)
    queries = [unit(conv_q[:, h * DK : (h + 1) * DK])[0] * SCALE for h in each]
    keys = [unit(conv_k[:, h * DK : (h + 1) * DK])[0] for h in each]
    values = [conv_v[:, h * DV : (h + 1) * DV] for h in each]
    beta = [sigmoid(gates[:, h : h + 1]) for h in each]
    total = [sums[:, heads + h : heads + h + 1] for h in each]
    decay = [
        jnp.where(
            lower, jnp.exp(jnp.minimum(total[h] - sums_t[heads + h : heads + h + 1, :], 0.0)), 0.0
        )
        for h in each
    ]
    scaled = [beta[h] * keys[h] for h in each]
    lowers = [jnp.where(strict, dot3(keys[h], scaled[h], NT) * decay[h], 0.0) for h in each]
    inverses = inverse_unit(lowers, rows, cols)
    growth = [jnp.exp(total[h]) for h in each]
    last = [total[h][size - 1 : size] for h in each]
    tail = [jnp.exp(last[h] - total[h]) * scaled[h] for h in each]
    mapk = [dot3(inverses[h], growth[h] * keys[h]) for h in each]
    fresh = [dot3(inverses[h], values[h]) for h in each]
    scores = [dot(queries[h], scaled[h], NT) * decay[h] for h in each]
    moved = [-dot3(tail[h], mapk[h], TN) for h in each]
    shift = [dot3(tail[h], fresh[h], TN) for h in each]
    reach = [growth[h] * queries[h] - dot(scores[h], mapk[h]) for h in each]
    local = [dot(scores[h], fresh[h]) for h in each]
    for h in each:
        piece_ref[0, h, :, :DK] = moved[h]
        piece_ref[0, h, :, DK:] = shift[h]
        note = log_rows(last[h])
        log_ref[0, h] = jnp.broadcast_to(last[h], (8, LANES))
        maplow_ref[0, h, :DK] = moved[h].astype(BF16)
        maplow_ref[0, h, DK:] = note
        low_ref[0, h, :DK, :DK] = moved[h].astype(BF16)
        low_ref[0, h, :DK, DK:] = shift[h].astype(BF16)
        low_ref[0, h, DK:] = jnp.concatenate([note] * (1 + DV // DK), axis=1)
        inv_ref[0, h] = inverses[h]
        mapk_ref[0, h] = mapk[h]
        fresh_ref[0, h] = fresh[h]
        score_ref[0, h] = scores[h]
        reach_ref[0, h] = reach[h]
        local_ref[0, h] = local[h]
        decay_ref[0, h] = decay[h]


def log_rows(log):
    log = jnp.broadcast_to(log, (1, LANES))
    high = log.astype(BF16).astype(F32)
    middle = (log - high).astype(BF16).astype(F32)
    rest = log - high - middle
    place = lax.broadcasted_iota(jnp.int32, (NOTE, LANES), 0)
    zero = jnp.zeros((NOTE, LANES), F32)
    rows = jnp.where(place == 0, high, jnp.where(place == 1, middle, jnp.where(place == 2, rest, zero)))
    return rows.astype(BF16)


def log_of(rows):
    return jnp.sum(rows.astype(F32), axis=0, keepdims=True)


def join_body(
    pairs, last, piece_ref, log_ref, got_ref, out_ref, newlog_ref, low_ref, maplow_ref, *far_ref
):
    wide = 1 + DV // DK
    for p in range(pairs):
        own = piece_ref[p]
        got_low = got_ref[p, :DK]
        got = got_low.astype(F32)
        own_log = log_ref[p, :1]
        got_log = log_of(got_ref[p, DK:, :LANES])
        mine = jnp.concatenate([jnp.exp(own_log)] * wide, axis=1)
        high, low = halves(own[:, :DK])
        moved = dot(high, got_low) + dot(low, got_low) + mine * got
        map_part = moved[:, :DK] + jnp.exp(got_log) * own[:, :DK]
        shift_part = moved[:, DK:] + own[:, DK:]
        new_log = own_log + got_log
        out_ref[p, :, :DK] = map_part
        out_ref[p, :, DK:] = shift_part
        newlog_ref[p] = jnp.broadcast_to(new_log, (8, LANES))
        low_ref[p, :DK, :DK] = map_part.astype(BF16)
        low_ref[p, :DK, DK:] = shift_part.astype(BF16)
        note = log_rows(new_log)
        low_ref[p, DK:] = jnp.concatenate([note] * wide, axis=1)
        maplow_ref[p, :DK] = map_part.astype(BF16)
        maplow_ref[p, DK:] = note
        if last:
            far_ref[0][p] = shift_part.astype(BF16)


def entry_body(pairs, near_ref, far_ref, out_ref):
    for p in range(pairs):
        far = far_ref[p]
        scale = jnp.exp(log_of(near_ref[p, DK:, DK:]))
        moved = dot(near_ref[p, :DK, :DK], far) + scale * far.astype(F32)
        out_ref[p] = moved + near_ref[p, :DK, DK:].astype(F32)


def back_body(pairs, map_ref, own_ref, got_ref, out_ref, low_ref):
    for p in range(pairs):
        got = got_ref[p]
        scale = jnp.concatenate([jnp.exp(log_of(map_ref[p, DK:]))] * (DV // DK), axis=1)
        out = own_ref[p] + dot(map_ref[p, :DK], got, TN) + scale * got.astype(F32)
        out_ref[p] = out
        low_ref[p] = out.astype(BF16)


def exit_body(pairs, map_ref, near_ref, far_ref, out_ref):
    for p in range(pairs):
        far = far_ref[p]
        scale = jnp.concatenate([jnp.exp(log_of(map_ref[p, DK:]))] * (DV // DK), axis=1)
        moved = dot(map_ref[p, :DK], far, TN) + scale * far.astype(F32)
        out_ref[p] = near_ref[p].astype(F32) + moved


def mixer_out_body(
    heads, state_ref, fresh_ref, mapk_ref, reach_ref, local_ref, pg_ref, gain_ref, wout_ref,
    made_ref, output_ref, gated_ref, attn_ref,
):
    for h in range(heads):
        state = state_ref[0, h]
        made_ref[0, h] = fresh_ref[0, h] - dot3(mapk_ref[0, h], state)
        output = local_ref[0, h] + dot(reach_ref[0, h], state)
        output_ref[0, :, h * DV : (h + 1) * DV] = output
        scale = lax.rsqrt(jnp.mean(output * output, axis=-1, keepdims=True) + 1e-05)
        gate = pg_ref[0, :, h * DV : (h + 1) * DV]
        gated_ref[0, :, h * DV : (h + 1) * DV] = (
            output * scale * gain_ref[...] * silu(gate)
        ).astype(BF16)
    attn_ref[0] = dot(gated_ref[0], wout_ref[...]).astype(BF16)


def feed_body(
    x_ref, mine_ref, other_ref, cot_ref, gain_ref, wgate_ref, wup_ref, wdown_ref, resid_ref,
    hidden_ref, dgate_ref, dup_ref, down_ref, dnorm_ref, normed_ref, cot_turned_ref,
):
    attn = mine_ref[0].astype(F32) + other_ref[0].astype(F32)
    resid = x_ref[0].astype(F32) + attn
    resid_ref[0] = resid
    normed = resid * lax.rsqrt(jnp.mean(resid * resid, axis=-1, keepdims=True) + 1e-06)
    normed = (normed * gain_ref[...]).astype(BF16)
    normed_ref[...] = jnp.transpose(normed)
    cot_turned_ref[...] = jnp.transpose(cot_ref[0])
    gate = dot(normed, wgate_ref[...])
    up = dot(normed, wup_ref[...])
    d_hidden = dot(cot_ref[0], wdown_ref[...], NT)
    sig = sigmoid(gate)
    active = gate * sig
    hidden = (active * up).astype(BF16)
    hidden_ref[0] = hidden
    d_gate = (d_hidden * up * (sig + active * (1.0 - sig))).astype(BF16)
    d_up = (d_hidden * active).astype(BF16)
    dgate_ref[0] = d_gate
    dup_ref[0] = d_up
    down_ref[0] = dot(hidden, wdown_ref[...]).astype(BF16)
    dnorm_ref[0] = (dot(d_gate, wgate_ref[...], NT) + dot(d_up, wup_ref[...], NT)).astype(BF16)


def mixer_back_body(
    heads, resid_ref, mine_ref, other_ref, cot_ref, output_ref, pg_ref, reach_ref, gain_ref,
    wout_ref, ogain_ref, dresid_ref, dout_ref, dpg_ref, back_ref, low_ref, dattn_ref, dgain_ref,
    dogain_ref,
):
    step = pl.program_id(0)
    resid = resid_ref[0]
    inverse = lax.rsqrt(jnp.mean(resid * resid, axis=-1, keepdims=True) + 1e-06)
    unit_resid = resid * inverse
    d_normed = mine_ref[0].astype(F32) + other_ref[0].astype(F32)
    d_gain = jnp.sum(d_normed * unit_resid, axis=0, keepdims=True)
    d_unit = d_normed * gain_ref[...]
    d_resid = inverse * (
        d_unit - unit_resid * jnp.mean(d_unit * unit_resid, axis=-1, keepdims=True)
    )
    d_resid = d_resid + cot_ref[0].astype(F32)
    dresid_ref[0] = d_resid
    d_attn = d_resid.astype(BF16)
    dattn_ref[...] = jnp.transpose(d_attn)
    d_gated = dot(d_attn, wout_ref[...], NT)
    d_ogain = jnp.zeros((1, DV), F32)
    for h in range(heads):
        part = slice(h * DV, (h + 1) * DV)
        output = output_ref[0, :, part]
        inverse = lax.rsqrt(jnp.mean(output * output, axis=-1, keepdims=True) + 1e-05)
        unit_out = output * inverse
        gate = pg_ref[0, :, part]
        grad = d_gated[:, part]
        active = silu(gate)
        d_ogain = d_ogain + jnp.sum(grad * unit_out * active, axis=0, keepdims=True)
        dpg_ref[0, :, part] = (grad * unit_out * ogain_ref[...] * silu_slope(gate)).astype(BF16)
        d_unit = grad * ogain_ref[...] * active
        d_out = inverse * (d_unit - unit_out * jnp.mean(d_unit * unit_out, axis=-1, keepdims=True))
        dout_ref[0, :, part] = d_out
        back = dot(reach_ref[0, h], d_out, TN)
        back_ref[0, h] = back
        low_ref[0, h] = back.astype(BF16)

    @pl.when(step == 0)
    def _():
        dgain_ref[...] = d_gain
        dogain_ref[...] = d_ogain

    @pl.when(step > 0)
    def _():
        dgain_ref[...] += d_gain
        dogain_ref[...] += d_ogain


def conv_back(grad, extended, taps, pre):
    d_pre = grad * silu_slope(pre)
    padded = jnp.concatenate([jnp.zeros((HALO, d_pre.shape[1]), F32), d_pre], axis=0)
    length = padded.shape[0]
    d_ext = taps[CONV - 1 : CONV] * padded
    d_taps = []
    for offset in range(CONV):
        back = CONV - 1 - offset
        if back:
            d_ext = d_ext + taps[offset : offset + 1] * pltpu.roll(padded, length - back, 0)
            shifted = pltpu.roll(extended, back, 0)
        else:
            shifted = extended
        d_taps.append(jnp.sum(padded * shifted, axis=0, keepdims=True))
    return d_ext, jnp.concatenate(d_taps, axis=0)


def early_body(
    heads, proj_ref, gates_ref, sums_ref, dout_ref, state_ref, made_ref, inv_ref, score_ref,
    decay_ref, cq_ref, ck_ref, xone_ref, xmap_ref, dkey_ref, dcol_ref, dext_ref, dtap_ref,
):
    step = pl.program_id(0)
    wide = heads * DK
    ext_q = proj_ref[0, :, :wide].astype(F32)
    ext_k = proj_ref[0, :, wide : 2 * wide].astype(F32)
    pre_q = conv_pre(ext_q, cq_ref[...])
    conv_q = silu(pre_q)
    conv_k = silu(conv_pre(ext_k, ck_ref[...]))
    gates = gates_ref[0]
    sums = sums_ref[0]
    size = gates.shape[0]
    each = range(heads)
    units = [unit(conv_q[:, h * DK : (h + 1) * DK]) for h in each]
    queries = [units[h][0] * SCALE for h in each]
    keys = [unit(conv_k[:, h * DK : (h + 1) * DK])[0] for h in each]
    beta = [sigmoid(gates[:, h : h + 1]) for h in each]
    total = [sums[:, heads + h : heads + h + 1] for h in each]
    growth = [jnp.exp(total[h]) for h in each]
    tail = [jnp.exp(total[h][size - 1 : size] - total[h]) * beta[h] * keys[h] for h in each]
    d_out = [dout_ref[0, :, h * DV : (h + 1) * DV] for h in each]
    d_made = [dot(score_ref[0, h], d_out[h], TN) for h in each]
    d_score = [dot(d_out[h], made_ref[0, h], NT) * decay_ref[0, h] for h in each]
    d_query = [
        dot3(d_score[h], beta[h] * keys[h]) + dot(growth[h] * d_out[h], state_ref[0, h], NT)
        for h in each
    ]
    d_key = [dot3(d_score[h], queries[h], TN) for h in each]
    x_one = [dot(inv_ref[0, h], d_made[h], TN) for h in each]
    x_map = [dot(inv_ref[0, h], tail[h], TN) for h in each]
    lanes = lax.broadcasted_iota(jnp.int32, (size, LANES), 1)
    cols = jnp.zeros((size, LANES), F32)
    grads = []
    for h in each:
        xone_ref[0, h] = x_one[h]
        xmap_ref[0, h] = x_map[h]
        dkey_ref[0, h] = beta[h] * d_key[h]
        key_sum = row_sum(d_key[h] * keys[h])
        cols = cols + jnp.where(lanes == h, key_sum, 0.0)
        d_total = row_sum(d_query[h] * queries[h]) - beta[h] * key_sum
        cols = cols + jnp.where(lanes == heads + h, d_total, 0.0)
        unit_q, inverse = units[h]
        d_unit = d_query[h] * SCALE
        grads.append(inverse * (d_unit - unit_q * row_sum(d_unit * unit_q)))
    dcol_ref[0] = cols
    d_ext, d_taps = conv_back(jnp.concatenate(grads, axis=1), ext_q, cq_ref[...], pre_q)
    dext_ref[0] = d_ext

    @pl.when(step == 0)
    def _():
        dtap_ref[...] = d_taps

    @pl.when(step > 0)
    def _():
        dtap_ref[...] += d_taps


def late_body(
    heads, proj_ref, gates_ref, sums_ref, dend_ref, state_ref, made_ref, decay_ref, xone_ref,
    xmap_ref, dkey_ref, dcol_ref, dextq_ref, ck_ref, cv_ref, dext_ref, dgates_ref, dtap_ref, dbias_ref,
):
    step = pl.program_id(0)
    wide = heads * DK
    ext_k = proj_ref[0, :, wide : 2 * wide].astype(F32)
    ext_v = proj_ref[0, :, 2 * wide :].astype(F32)
    pre_k = conv_pre(ext_k, ck_ref[...])
    pre_v = conv_pre(ext_v, cv_ref[...])
    conv_k = silu(pre_k)
    gates = gates_ref[0]
    sums = sums_ref[0]
    size = gates.shape[0]
    rows, cols = rows_cols(size)
    strict = rows > cols
    each = range(heads)
    units = [unit(conv_k[:, h * DK : (h + 1) * DK]) for h in each]
    keys = [units[h][0] for h in each]
    beta = [sigmoid(gates[:, h : h + 1]) for h in each]
    total = [sums[:, heads + h : heads + h + 1] for h in each]
    growth = [jnp.exp(total[h]) for h in each]
    left = [jnp.exp(total[h][size - 1 : size] - total[h]) for h in each]
    d_end = [dend_ref[0, h] for h in each]
    made = [made_ref[0, h] for h in each]
    state = [state_ref[0, h] for h in each]
    d_rhs = [xone_ref[0, h] + dot(xmap_ref[0, h], d_end[h]) for h in each]
    d_tail = [dot(made[h], d_end[h], NT) for h in each]
    d_lower = [
        jnp.where(strict, -dot(d_rhs[h], made[h], NT) * decay_ref[0, h], 0.0) for h in each
    ]
    d_plain = [
        dot3(d_lower[h], beta[h] * keys[h]) - dot(growth[h] * d_rhs[h], state[h], NT) for h in each
    ]
    d_turned = [dot3(d_lower[h], keys[h], TN) for h in each]
    lanes = lax.broadcasted_iota(jnp.int32, (size, LANES), 1)
    places = lax.broadcasted_iota(jnp.int32, (size, 1), 0)
    d_col = dcol_ref[0]
    grads_k = []
    for h in each:
        turned = row_sum(d_turned[h] * keys[h])
        tails = row_sum(d_tail[h] * keys[h])
        tail_weight = left[h] * beta[h]
        d_key = d_plain[h] + beta[h] * d_turned[h] + tail_weight * d_tail[h] + dkey_ref[0, h]
        d_total = row_sum(d_plain[h] * keys[h]) - beta[h] * turned - tail_weight * tails
        ended = jnp.sum(tail_weight * tails, axis=0, keepdims=True)
        whole = jnp.sum(row_sum(d_end[h] * state[h]), axis=0, keepdims=True)
        ended = ended + growth[h][size - 1 : size] * whole
        d_total = d_total + jnp.where(places == size - 1, ended, 0.0)
        d_col = d_col + jnp.where(lanes == h, turned + left[h] * tails, 0.0)
        d_col = d_col + jnp.where(lanes == heads + h, d_total, 0.0)
        unit_k, inverse = units[h]
        grads_k.append(inverse * (d_key - unit_k * row_sum(d_key * unit_k)))
    upper = (rows <= cols).astype(BF16)
    d_decay = ones_dot(upper, d_col)
    rate = sigmoid(gates)
    d_gates = jnp.where(
        lanes < heads, d_col * rate * (1.0 - rate), d_decay / (1.0 + jnp.exp(gates))
    )
    d_gates = jnp.where(lanes < 2 * heads, d_gates, 0.0)
    dgates_ref[0] = d_gates.astype(BF16)
    d_bias = jnp.sum(d_gates, axis=0, keepdims=True)
    dext_k, dtaps_k = conv_back(jnp.concatenate(grads_k, axis=1), ext_k, ck_ref[...], pre_k)
    dext_v, dtaps_v = conv_back(jnp.concatenate(d_rhs, axis=1), ext_v, cv_ref[...], pre_v)
    dext_ref[0, :, :wide] = dextq_ref[0]
    dext_ref[0, :, wide : 2 * wide] = dext_k
    dext_ref[0, :, 2 * wide :] = dext_v

    @pl.when(step == 0)
    def _():
        dtap_ref[:, :wide] = dtaps_k
        dtap_ref[:, wide:] = dtaps_v
        dbias_ref[...] = d_bias

    @pl.when(step > 0)
    def _():
        dtap_ref[:, :wide] += dtaps_k
        dtap_ref[:, wide:] += dtaps_v
        dbias_ref[...] += d_bias


def input_back_body(
    dext_ref, dpg_ref, dgates_ref, wq_ref, wk_ref, wv_ref, wg_ref, wgates_ref, dqk_ref, dv_ref,
    dqkhalo_ref, dvhalo_ref, dmixed_ref, dhalo_ref,
):
    wide = wq_ref.shape[1]
    d_proj = dext_ref[0].astype(BF16)
    dqk_ref[0] = d_proj[HALO:, : 2 * wide]
    dv_ref[0] = d_proj[HALO:, 2 * wide :]
    dqkhalo_ref[0] = d_proj[:HALO, : 2 * wide]
    dvhalo_ref[0] = d_proj[:HALO, 2 * wide :]
    d_mixed = dot(d_proj[:, :wide], wq_ref[...], NT)
    d_mixed = d_mixed + dot(d_proj[:, wide : 2 * wide], wk_ref[...], NT)
    d_mixed = d_mixed + dot(d_proj[:, 2 * wide :], wv_ref[...], NT)
    dhalo_ref[0] = d_mixed[:HALO].astype(BF16)
    main = d_mixed[HALO:] + dot(dpg_ref[0], wg_ref[...], NT)
    main = main + dot(dgates_ref[0], wgates_ref[...], NT)
    dmixed_ref[0] = main.astype(BF16)


def last_body(
    x_ref, mine_ref, other_ref, halo_ref, halo_other_ref, dresid_ref, gain_ref, grad_ref, dgain_ref,
):
    x = x_ref[0].astype(F32)
    inverse = lax.rsqrt(jnp.mean(x * x, axis=-1, keepdims=True) + 1e-06)
    unit_x = x * inverse
    d_mixed = mine_ref[0].astype(F32) + other_ref[0].astype(F32)
    halo = halo_ref[0].astype(F32) + halo_other_ref[0].astype(F32)
    size = d_mixed.shape[0]
    d_mixed = jnp.concatenate([d_mixed[: size - HALO], d_mixed[size - HALO :] + halo], axis=0)
    d_unit = d_mixed * gain_ref[...]
    back = inverse * (d_unit - unit_x * jnp.mean(d_unit * unit_x, axis=-1, keepdims=True))
    grad_ref[0] = dresid_ref[0] + back
    d_gain = jnp.sum(d_mixed * unit_x, axis=0, keepdims=True)
    step = pl.program_id(0)

    @pl.when(step == 0)
    def _():
        dgain_ref[...] = d_gain

    @pl.when(step > 0)
    def _():
        dgain_ref[...] += d_gain


def result_body(resid_ref, down_ref, downother_ref, result_ref):
    down = down_ref[0].astype(F32) + downother_ref[0].astype(F32)
    result_ref[0] = (resid_ref[0] + down).astype(BF16)


def held_rows(left_refs, index_ref, first, blocks, held):
    share = left_refs[0].shape[1]
    for left_ref, held_ref in zip(left_refs, held):
        for place in range(blocks):
            held_ref[place * share : (place + 1) * share] = left_ref[index_ref[first + place]]


def send_body(terms, first, blocks, lefts, rights, index_ref, *refs):
    out_ref, held = refs[lefts + rights], refs[lefts + rights + 1 :]
    held_rows(refs[:lefts], index_ref, first, blocks, held)
    at = 0
    for factors, width in terms:
        total = sum(dot(held[left][...], refs[lefts + right][...]) for left, right in factors)
        out_ref[:, at : at + width] = total.astype(BF16)
        at += width


def keep_body(terms, blocks, parts, lefts, rights, index_ref, *refs):
    got_ref, keep_ref = refs[lefts + rights], refs[lefts + rights + 1]
    send_refs = refs[lefts + rights + 2 : lefts + rights + 1 + parts]
    held = refs[lefts + rights + 1 + parts :]
    held_rows(refs[:lefts], index_ref, 0, blocks, held)
    rows = keep_ref.shape[0]
    at = 0
    for factors, width in terms:
        total = got_ref[:, at : at + width].astype(F32)
        for left, right in factors:
            total = total + dot(held[left][...], refs[lefts + right][...])
        keep_ref[:, at : at + width] = total[:rows]
        for part in range(1, parts):
            send_refs[part - 1][:, at : at + width] = total[part * rows : (part + 1) * rows].astype(BF16)
        at += width


def add_body(parts, gots, keep_ref, *refs):
    total = keep_ref[...]
    for got_ref in refs[:gots]:
        total = total + got_ref[...].astype(F32)
    out_ref = refs[gots]
    rows = out_ref.shape[0]
    out_ref[...] = total[:rows]
    for part in range(1, parts):
        refs[gots + part][...] = total[part * rows : (part + 1) * rows].astype(BF16)


def joined_body(widths, *refs):
    keep_ref, send_ref = refs[-2:]
    rows = keep_ref.shape[0]
    at = 0
    for number, width in enumerate(widths):
        total = refs[2 * number][...] + refs[2 * number + 1][...].astype(F32)
        keep_ref[:, at : at + width] = total[:rows]
        send_ref[:, at : at + width] = total[rows:].astype(BF16)
        at += width


def total_body(cuts, gots, *refs):
    at = 0
    for ref, width in zip(refs[1 + gots :], cuts):
        total = refs[0][:, at : at + width]
        for got_ref in refs[1 : 1 + gots]:
            total = total + got_ref[:, at : at + width].astype(F32)
        ref[...] = total
        at += width


def pack_body(tapq_ref, tapkv_ref, bias_ref, ffn_ref, mix_ref, ogain_ref, other_ref, out_ref):
    wide = tapq_ref.shape[1]
    out_ref[...] = jnp.zeros_like(out_ref)
    out_ref[:CONV, :wide] = tapq_ref[...]
    out_ref[:CONV, wide:] = tapkv_ref[...]
    out_ref[4:5, :LANES] = bias_ref[...]
    out_ref[5:6] = ffn_ref[...]
    out_ref[6:7] = mix_ref[...]
    out_ref[7:8, :DV] = ogain_ref[...] + other_ref[...]


def unpack_body(heads, count, start_ref, *refs):
    total = refs[0][...]
    for ref in refs[1:count]:
        total = total + ref[...]
    tapq_ref, tapk_ref, tapv_ref, bias_ref, ogain_ref, gains_ref = refs[count:]
    wide = tapq_ref.shape[1]
    share = gains_ref.shape[1]
    tapq_ref[...] = total[:CONV, :wide]
    tapk_ref[...] = total[:CONV, wide : 2 * wide]
    tapv_ref[...] = total[:CONV, 2 * wide :]
    for row in range(2):
        bias_ref[row : row + 1] = total[4:5, row * heads : (row + 1) * heads]
    ogain_ref[...] = total[7:8, : ogain_ref.shape[1]]
    width = total.shape[1]
    turned = pltpu.roll(total, lax.rem(width - start_ref[0], width), 1)
    gains_ref[...] = turned[5:7, :share]


def sum_body(count, *refs):
    total = refs[0][...]
    for ref in refs[1:count]:
        total = total + ref[...]
    refs[count][...] = total


def by_seq(shape):
    rest = len(shape) - 1
    return pl.BlockSpec((1,) + tuple(shape[1:]), lambda s: (s,) + (0,) * rest)


def whole(shape):
    rest = len(shape)
    return pl.BlockSpec(tuple(shape), lambda s: (0,) * rest)


def without(body, position, count):
    def shorter(*refs):
        return body(*refs[:position], *refs[position + count :])

    return shorter if count else body


def call(body, name, seqs, parts, shared, outs, sums=(), turned=(), after=(), flops=0):
    operands = list(parts) + list(shared)
    listed = list(outs) + list(turned) + list(sums)
    out_shape = [jax.ShapeDtypeStruct(shape, kind) for shape, kind in listed]
    moved = sum(a.size * a.dtype.itemsize for a in operands + out_shape)
    return pl.pallas_call(
        without(body, len(operands), len(after)),
        grid=(seqs,),
        in_specs=[by_seq(a.shape) for a in parts]
        + [whole(a.shape) for a in shared]
        + [pl.BlockSpec(memory_space=pl.ANY)] * len(after),
        out_specs=[by_seq(shape) for shape, _ in outs]
        + [pl.BlockSpec((shape[0], shape[1] // seqs), lambda s: (0, s)) for shape, _ in turned]
        + [whole(shape) for shape, _ in sums],
        out_shape=out_shape,
        compiler_params=pltpu.CompilerParams(vmem_limit_bytes=VMEM_LIMIT),
        cost_estimate=pl.CostEstimate(flops=int(flops), bytes_accessed=int(moved), transcendentals=0),
        name=name,
    )(*operands, *after)


def small_call(body, name, arrays, outs, after=(), scalars=(), scratch=(), flops=2e8):
    out_shape = [jax.ShapeDtypeStruct(shape, kind) for shape, kind in outs]
    moved = sum(a.size * a.dtype.itemsize for a in list(arrays) + out_shape)
    return pl.pallas_call(
        without(body, len(scalars) + len(arrays), len(after)),
        in_specs=[pl.BlockSpec(memory_space=pltpu.SMEM)] * len(scalars)
        + [pl.BlockSpec(memory_space=pltpu.VMEM)] * len(arrays)
        + [pl.BlockSpec(memory_space=pl.ANY)] * len(after),
        out_specs=[pl.BlockSpec(memory_space=pltpu.VMEM)] * len(outs),
        out_shape=out_shape,
        scratch_shapes=list(scratch),
        compiler_params=pltpu.CompilerParams(vmem_limit_bytes=SMALL_LIMIT),
        cost_estimate=pl.CostEstimate(flops=int(flops), bytes_accessed=int(moved), transcendentals=0),
        name=name,
    )(*scalars, *arrays, *after)


class Halved:
    def __init__(self, name, steps, me, lefts, rights, terms):
        self.name, self.lefts, self.rights, self.terms = (name, lefts, rights, terms)
        order = [bit for step in steps for bit in step]
        self.steps = steps
        self.index = block_index(order, me)
        self.count = 1 << len(order)
        self.share, self.tokens = lefts[0].shape[1:]
        self.columns = sum(width for _, width in terms)
        self.done = 0

    def trade(self, sends):
        bits = self.steps[self.done]
        self.done += 1
        self.gots = []
        for part, send in enumerate(sends, 1):
            moved = sum(
                ((part >> (len(bits) - 1 - place)) & 1) << bit for place, bit in enumerate(bits)
            )
            self.gots.append(traded(send, moved))

    def multiplied(self, body, suffix, extra, outs, after):
        blocks = self.count // 2
        return small_call(
            body, self.name + suffix, list(self.lefts) + list(self.rights) + extra, outs, after,
            scalars=[self.index],
            scratch=[pltpu.VMEM((blocks * self.share, left.shape[2]), BF16) for left in self.lefts],
            flops=2 * blocks * self.share * self.tokens * self.columns,
        )

    def outs(self, rows):
        parts = 1 << len(self.steps[self.done])
        return parts, [((rows // parts, self.columns), F32)] + [
            ((rows // parts, self.columns), BF16)
        ] * (parts - 1)

    def send(self, *after):
        blocks = self.count // 2
        body = functools.partial(
            send_body, self.terms, blocks, blocks, len(self.lefts), len(self.rights)
        )
        rows = blocks * self.share
        sends = self.multiplied(body, "_send", [], [((rows, self.columns), BF16)], after)
        self.trade(sends)
        return sends[0]

    def keep(self, *after):
        blocks = self.count // 2
        parts, outs = self.outs(blocks * self.share)
        body = functools.partial(
            keep_body, self.terms, blocks, parts, len(self.lefts), len(self.rights)
        )
        self.kept, *sends = self.multiplied(body, "_keep", self.gots, outs, after)
        self.trade(sends)
        return self.kept

    def add(self, *after):
        parts, outs = self.outs(self.kept.shape[0])
        body = functools.partial(add_body, parts, len(self.gots))
        self.kept, *sends = small_call(
            body, self.name + "_add", [self.kept] + self.gots, outs, after, flops=1e6
        )
        self.trade(sends)
        return self.kept

    def left(self):
        return len(self.steps) - self.done

    def total(self, cuts, *after):
        rows = self.kept.shape[0]
        outs = [((rows, width), F32) for width in cuts]
        return small_call(
            functools.partial(total_body, tuple(cuts), len(self.gots)), self.name + "_total",
            [self.kept] + self.gots, outs, after, flops=1e6,
        )


def joined(name, groups, *after):
    whole_sum = copy.copy(groups[0])
    whole_sum.name = name
    whole_sum.columns = sum(group.columns for group in groups)
    rows = groups[0].kept.shape[0] // 2
    shape = (rows, whole_sum.columns)
    operands = [array for group in groups for array in [group.kept] + group.gots]
    body = functools.partial(joined_body, [group.columns for group in groups])
    whole_sum.kept, send = small_call(
        body, name, operands, [(shape, F32), (shape, BF16)], after, flops=1e6
    )
    whole_sum.trade([send])
    return whole_sum


def halving_steps(count, first):
    bits = list(range(count.bit_length() - 1))
    return [[bit] for bit in first] + [[bit] for bit in bits if bit not in first]


def block_index(order, me):
    count = 1 << len(order)
    moved = [
        sum(((place >> (len(order) - 1 - step)) & 1) << bit for step, bit in enumerate(order))
        for place in range(count)
    ]
    return jnp.bitwise_xor(jnp.array(moved, jnp.int32), me)


def traded(block, moved):
    count = lax.axis_size("seq")
    return lax.ppermute(block, "seq", [(i, i ^ moved) for i in range(count)])


def passed_along(block, axis, distance):
    devices = range(lax.axis_size(axis))
    route = [(i - distance, i) for i in devices if i - distance in devices]
    return lax.ppermute(block, axis, route)


def swapped(block):
    count = lax.axis_size("head")
    return lax.ppermute(block, "head", [(i, i ^ 1) for i in range(count)])


def on_device(
    tokens, w_query, w_key, w_value, w_outgate, w_gates, gate_bias, conv_query, conv_key,
    conv_value, out_gain, w_out, mix_gain, ffn_gain, w_gate, w_up, w_down, cotangent,
):
    seqs, size, width = tokens.shape
    heads = gate_bias.shape[1]
    pairs = seqs * heads
    units = w_gate.shape[1]
    count, me = lax.axis_size("seq"), lax.axis_index("seq")
    wide = heads * DK
    out_wide = heads * DV
    proj_wide = 2 * wide + out_wide

    halo = passed_along(tokens[:, size - HALO :], "seq", 1)
    gates_w = jnp.swapaxes(w_gates, 0, 1).reshape(width, 2 * heads)
    gates_w = jnp.pad(gates_w, ((0, 0), (0, LANES - 2 * heads)))
    bias = jnp.pad(gate_bias.reshape(1, 2 * heads), ((0, 0), (0, LANES - 2 * heads)))
    mix_row = mix_gain.reshape(1, width)
    ffn_row = ffn_gain.reshape(1, width)
    out_row = out_gain.reshape(1, DV)
    square = (seqs, heads, size, size)
    by_key = (seqs, heads, size, DK)
    by_value = (seqs, heads, size, DV)
    tokens_here = seqs * size
    steps_x, steps_y = halving_steps(count, (0, 1)), halving_steps(count, (1, 0))
    steps_yzx, steps_zxy = halving_steps(count, (1, 2, 0)), halving_steps(count, (2, 0, 1))
    turned_shape = (width, tokens_here)
    share = width // count

    def in_blocks(turned):
        return turned.reshape(count, share, tokens_here)

    def flat(field):
        return field.reshape(tokens_here, field.shape[2])

    (
        proj, proj_g, gates, sums, inv, mapk, fresh, score, reach, local, decay, piece, low,
        map_low, log, mixed_halo, mixed_t,
    ) = call(
        functools.partial(first_body, heads), "project_and_local", seqs, [halo, tokens],
        [mix_row, w_query, w_key, w_value, w_outgate, gates_w, bias, conv_query, conv_key, conv_value],
        [
            ((seqs, size + HALO, proj_wide), BF16),
            ((seqs, size, out_wide), F32), ((seqs, size, LANES), F32), ((seqs, size, LANES), F32),
            (square, F32), (by_key, F32), (by_value, F32), (square, F32), (by_key, F32),
            (by_value, F32), (square, F32), ((seqs, heads, DK, DK + DV), F32),
            ((seqs, heads, DK + NOTE, DK + DV), BF16),
            ((seqs, heads, DK + NOTE, DK), BF16), ((seqs, heads, 8, LANES), F32),
            ((seqs, HALO, width), BF16),
        ],
        turned=[(turned_shape, BF16)],
        flops=1e10,
    )

    piece = piece.reshape(pairs, DK, DK + DV)
    low = low.reshape(pairs, DK + NOTE, DK + DV)
    log = log.reshape(pairs, 8, LANES)
    maps = [map_low.reshape(pairs, DK + NOTE, DK)]
    state_shape = (pairs, DK, DV)
    dists = []
    reach_by = 1
    while reach_by * 2 < count:
        dists.append(reach_by)
        reach_by *= 2
    for level, d in enumerate(dists):
        got = passed_along(low, "seq", d)
        last = level + 1 == len(dists)
        outs = [(piece.shape, F32), (log.shape, F32), (low.shape, BF16), (maps[0].shape, BF16)]
        if last:
            outs.append((state_shape, BF16))
        piece, log, low, map_low, *far = small_call(
            functools.partial(join_body, pairs, last), "join", [piece, log, got], outs
        )
        maps.append(map_low)
    near = passed_along(low, "seq", 1)
    far = passed_along(far[0], "seq", 1 + reach_by)
    back_maps = [maps[0]]
    for level in range(1, len(dists)):
        back_maps.append(passed_along(maps[level], "seq", 1 - dists[level]))
    near_map = passed_along(maps[-1], "seq", -reach_by)
    (state,) = small_call(
        functools.partial(entry_body, pairs), "entry", [near, far], [(state_shape, F32)]
    )
    state = state.reshape(seqs, heads, DK, DV)

    made, output, gated, attn = call(
        functools.partial(mixer_out_body, heads), "mixer_out", seqs,
        [state, fresh, mapk, reach, local, proj_g], [out_row, w_out],
        [
            (by_value, F32), ((seqs, size, out_wide), F32), ((seqs, size, out_wide), BF16),
            ((seqs, size, width), BF16),
        ],
        after=[near_map] + back_maps[1:],
        flops=1.5e9,
    )
    attn_other = swapped(attn)

    resid, hidden, d_gate, d_up, down, d_norm, normed_t, cot_t = call(
        feed_body, "feed_forward", seqs, [tokens, attn, attn_other, cotangent],
        [ffn_row, w_gate, w_up, w_down],
        [
            ((seqs, size, width), F32), ((seqs, size, units), BF16), ((seqs, size, units), BF16),
            ((seqs, size, units), BF16), ((seqs, size, width), BF16), ((seqs, size, width), BF16),
        ],
        turned=[(turned_shape, BF16), (turned_shape, BF16)],
        flops=1.2e10,
    )
    d_norm_other = swapped(d_norm)
    down_other = swapped(down)

    normed_b, cot_b, mixed_b = in_blocks(normed_t), in_blocks(cot_t), in_blocks(mixed_t)
    gate_sum = Halved("gate", steps_x, me, [normed_b], [flat(d_gate)], ((((0, 0),), units),))
    up_sum = Halved("up", steps_yzx, me, [normed_b], [flat(d_up)], ((((0, 0),), units),))
    down_sum = Halved("down", steps_zxy, me, [cot_b], [flat(hidden)], ((((0, 0),), units),))
    done = down_sum.send(up_sum.send(gate_sum.send()))

    d_resid, d_out, d_pg, back, low, d_attn_t, d_ffn_gain, d_out_gain = call(
        functools.partial(mixer_back_body, heads), "mixer_back", seqs,
        [resid, d_norm, d_norm_other, cotangent, output, proj_g, reach],
        [ffn_row, w_out, out_row],
        [
            ((seqs, size, width), F32), ((seqs, size, out_wide), F32),
            ((seqs, size, out_wide), BF16), ((seqs, heads, DK, DV), F32),
            ((seqs, heads, DK, DV), BF16),
        ],
        [((1, width), F32), ((1, DV), F32)],
        turned=[(turned_shape, BF16)],
        after=[done],
        flops=1.5e9,
    )

    outs_sum = Halved(
        "outs", steps_zxy, me, [in_blocks(d_attn_t), mixed_b], [flat(gated), flat(d_pg)],
        ((((0, 0),), out_wide), (((1, 1),), out_wide)),
    )
    back = back.reshape(state_shape)
    low = low.reshape(state_shape)
    x_one, x_map, d_key, d_col, dext_q, dtap_q = call(
        functools.partial(early_body, heads), "delta_back_early", seqs,
        [proj, gates, sums, d_out, state, made, inv, score, decay], [conv_query, conv_key],
        [
            (by_value, F32), (by_key, F32), (by_key, F32), ((seqs, size, LANES), F32),
            ((seqs, size + HALO, wide), F32),
        ],
        [((CONV, wide), F32)],
        flops=3e9,
    )
    (result,) = call(
        result_body, "result", seqs, [resid, down, down_other], [],
        [((seqs, size, width), BF16)], after=[d_col],
    )
    done = result
    for level, d in enumerate(dists):
        got = passed_along(low, "seq", -d)
        if level == 1:
            done = down_sum.keep(up_sum.keep(gate_sum.keep(done)))
        back, low = small_call(
            functools.partial(back_body, pairs), "join_back", [back_maps[level], back, got],
            [(state_shape, F32), (state_shape, BF16)], after=[done],
        )
        done = low
    near = passed_along(low, "seq", -1)
    far = passed_along(low, "seq", -1 - reach_by)
    done = down_sum.add(up_sum.add(gate_sum.add(done)))
    (d_end,) = small_call(
        functools.partial(exit_body, pairs), "exit", [near_map, near, far], [(state_shape, F32)],
        after=[done],
    )
    d_end = d_end.reshape(seqs, heads, DK, DV)
    d_ext, d_gates, dtap_kv, d_bias = call(
        functools.partial(late_body, heads), "delta_back_late", seqs,
        [
            proj, gates, sums, d_end, state, made, decay, x_one, x_map, d_key, d_col, dext_q,
        ],
        [conv_key, conv_value],
        [((seqs, size + HALO, proj_wide), F32), ((seqs, size, LANES), BF16)],
        [((CONV, wide + out_wide), F32), ((1, LANES), F32)],
        flops=3e9,
    )
    done = outs_sum.send(d_bias)
    feed_sum = joined("feed_last", [gate_sum, up_sum, down_sum], done)
    done = feed_sum.kept
    d_qk, d_v, d_qk_halo, d_v_halo, d_mixed, d_halo = call(
        input_back_body, "input_back", seqs, [d_ext, d_pg, d_gates],
        [w_query, w_key, w_value, w_outgate, gates_w],
        [
            ((seqs, size, 2 * wide), BF16), ((seqs, size, out_wide), BF16),
            ((seqs, HALO, 2 * wide), BF16), ((seqs, HALO, out_wide), BF16),
            ((seqs, size, width), BF16), ((seqs, HALO, width), BF16),
        ],
        after=[done],
        flops=1.7e9,
    )
    d_mixed_other = swapped(d_mixed)
    halo_rows = seqs * HALO
    halo_b = jnp.swapaxes(mixed_halo.reshape(halo_rows, width), 0, 1).reshape(count, share, halo_rows)
    query_sum = Halved(
        "query_key", steps_x, me, [mixed_b, halo_b],
        [flat(d_qk), d_qk_halo.reshape(halo_rows, 2 * wide), flat(d_gates)],
        ((((0, 0), (1, 1)), 2 * wide), (((0, 2),), LANES)),
    )
    value_sum = Halved(
        "value", steps_y, me, [mixed_b, halo_b],
        [flat(d_v), d_v_halo.reshape(halo_rows, out_wide)], ((((0, 0), (1, 1)), out_wide),),
    )
    done = value_sum.send(query_sum.send(d_mixed))
    done = value_sum.keep(query_sum.keep(outs_sum.keep(done)))
    halo_grad = passed_along(d_halo, "seq", -1)
    halo_other = swapped(halo_grad)
    grad_input, d_mix_gain = call(
        last_body, "first_norm_back", seqs,
        [tokens, d_mixed, d_mixed_other, halo_grad, halo_other, d_resid], [mix_row],
        [((seqs, size, width), F32)], [((1, width), F32)], after=[done],
    )

    (small,) = small_call(
        pack_body, "pack",
        [dtap_q, dtap_kv, d_bias, d_ffn_gain, d_mix_gain, d_out_gain, swapped(d_out_gain)],
        [((8, width), F32)], flops=1e4,
    )

    def finish(group, cuts, done):
        while group.left():
            done = group.add(done)
        return group.total(cuts, done)

    def small_others(bits):
        return [
            traded(small, sum(((part >> place) & 1) << bit for place, bit in enumerate(bits)))
            for part in range(1, 1 << len(bits))
        ]

    def small_step(bits, done):
        others = small_others(bits)
        return small_call(
            functools.partial(sum_body, 1 + len(others)), "small_sum", [small] + others,
            [(small.shape, F32)], after=[done], flops=1e4,
        )[0]

    bits = [[0], [1]] + [[b for step in steps_x[at : at + 2] for b in step] for at in range(2, len(steps_x), 2)]
    done = small = small_step(bits.pop(0), small)
    ins_sum = joined("ins_join", [query_sum, value_sum], done)
    done = outs_sum.add(ins_sum.kept)
    grad_gate, grad_up, grad_down = finish(feed_sum, [units] * 3, done)
    done = small = small_step(bits.pop(0), grad_gate)
    ins_sum = joined("ins_last", [ins_sum, outs_sum], done)
    while len(bits) > 1:
        small = small_step(bits.pop(0), ins_sum.kept)
    others = small_others(bits.pop(0))
    tap_shape = (CONV, wide)
    taps_q, taps_k, taps_v, grad_bias, gain_out, gains = small_call(
        functools.partial(unpack_body, heads, 1 + len(others)), "unpack", [small] + others,
        [
            (tap_shape, F32), (tap_shape, F32), ((CONV, out_wide), F32), ((2, heads), F32),
            ((1, DV), F32), ((2, share), F32),
        ],
        after=[ins_sum.kept], scalars=[(me * share).astype(jnp.int32).reshape(1)], flops=1e4,
    )
    grad_query, grad_key, grad_gates, grad_value, grad_out, grad_outgate = finish(
        ins_sum, [wide, wide, LANES, out_wide, out_wide, out_wide], gains
    )
    grad_gates = grad_gates[:, : 2 * heads].reshape(share, 2, heads)

    return (
        result,
        grad_input,
        grad_query,
        grad_key,
        grad_value,
        grad_outgate,
        jnp.swapaxes(grad_gates, 0, 1),
        grad_bias,
        taps_q,
        taps_k,
        taps_v,
        gain_out.reshape(DV),
        jnp.swapaxes(grad_out, 0, 1),
        gains[1],
        gains[0],
        grad_gate,
        grad_up,
        jnp.swapaxes(grad_down, 0, 1),
    )


def solution(mesh):
    return jax.shard_map(
        on_device,
        mesh=mesh,
        in_specs=(
            P(None, "seq", None),
            P(None, "head"),
            P(None, "head"),
            P(None, "head"),
            P(None, "head"),
            P(None, None, "head"),
            P(None, "head"),
            P(None, "head"),
            P(None, "head"),
            P(None, "head"),
            P(),
            P("head", None),
            P(),
            P(),
            P(None, "head"),
            P(None, "head"),
            P("head", None),
            P(None, "seq", None),
        ),
        out_specs=(
            P(None, "seq", None),
            P(None, "seq", None),
            P("seq", "head"),
            P("seq", "head"),
            P("seq", "head"),
            P("seq", "head"),
            P(None, "seq", "head"),
            P(None, "head"),
            P(None, "head"),
            P(None, "head"),
            P(None, "head"),
            P(),
            P("head", "seq"),
            P("seq"),
            P("seq"),
            P("seq", "head"),
            P("seq", "head"),
            P("head", "seq"),
        ),
        check_vma=False,
    )
```

```python
import copy
import functools

import jax
import jax.numpy as jnp
from jax import lax
from jax.experimental import pallas as pl
from jax.experimental.pallas import tpu as pltpu
from jax.sharding import PartitionSpec as P

DK = 128
DV = 256
CONV = 4
HALO = 16
LANES = 128
SCALE = DK ** (-0.5)
F32 = jnp.float32
BF16 = jnp.bfloat16
NN = ((1,), (0,))
NT = ((1,), (1,))
TN = ((0,), (0,))
NOTE = 16
VMEM_LIMIT = 48 * 1024 * 1024
WHOLE_LIMIT = 60 * 1024 * 1024
SMALL_LIMIT = 20 * 1024 * 1024


def dot(left, right, dims=NN):
    return lax.dot_general(
        left.astype(BF16), right.astype(BF16), (dims, ((), ())), preferred_element_type=F32
    )


def halves(field):
    high = field.astype(BF16)
    return high, (field - high.astype(F32)).astype(BF16)


def dot3(left, right, dims=NN):
    left_high, left_low = halves(left)
    right_high, right_low = halves(right)
    return dot(left_high, right_high, dims) + (
        dot(left_high, right_low, dims) + dot(left_low, right_high, dims)
    )


def ones_dot(ones, field):
    high, low = halves(field)
    lowest = field - high.astype(F32) - low.astype(F32)
    return dot(ones, high) + (dot(ones, low) + dot(ones, lowest))


def rows_cols(size):
    return (
        lax.broadcasted_iota(jnp.int32, (size, size), 0),
        lax.broadcasted_iota(jnp.int32, (size, size), 1),
    )


def log1p_small(value):
    shifted = 1.0 + value
    same = shifted == 1.0
    safe = jnp.where(same, 1.0, shifted - 1.0)
    return jnp.where(same, value, jnp.log(shifted) * (value / safe))


def log_sigmoid(value):
    return jnp.minimum(value, 0.0) - log1p_small(jnp.exp(-jnp.abs(value)))


def sigmoid(value):
    return 1.0 / (1.0 + jnp.exp(-value))


def row_sum(field):
    return jnp.sum(field, axis=-1, keepdims=True)


def inverse_unit(lowers, rows, cols):
    size = lowers[0].shape[0]
    same = (rows // 16) == (cols // 16)
    eye = (rows == cols).astype(F32)
    powers = [jnp.where(same, -lower, 0.0) for lower in lowers]
    inverses = [eye + power for power in powers]
    for _ in range(3):
        powers = [dot(power, power) for power in powers]
        inverses = [inv + dot(inv, power) for inv, power in zip(inverses, powers)]
    block = 16
    while block * 2 <= size:
        inside = ((rows // (2 * block)) == (cols // (2 * block))) & (
            (rows // block) != (cols // block)
        )
        parts = [dot(jnp.where(inside, lower, 0.0), inv) for lower, inv in zip(lowers, inverses)]
        inverses = [inv - dot(inv, part) for inv, part in zip(inverses, parts)]
        block *= 2
    errors = [eye - inv - dot3(lower, inv) for lower, inv in zip(lowers, inverses)]
    return [inv + dot(inv, error) for inv, error in zip(inverses, errors)]


def conv_pre(extended, taps):
    total = taps[CONV - 1 : CONV] * extended
    for offset in range(CONV - 1):
        total = total + taps[offset : offset + 1] * pltpu.roll(extended, CONV - 1 - offset, 0)
    return total[HALO:]


def silu(value):
    return value * sigmoid(value)


def silu_slope(value):
    gate = sigmoid(value)
    return gate * (1.0 + value * (1.0 - gate))


def unit(field):
    inverse = lax.rsqrt(row_sum(field * field) + 1e-06)
    return field * inverse, inverse


def first_body(
    heads, halo_ref, x_ref, gain_ref, wq_ref, wk_ref, wv_ref, wg_ref, wgates_ref, bias_ref, cq_ref, ck_ref,
    cv_ref, proj_ref, pg_ref, gates_ref, sums_ref, inv_ref, mapk_ref, fresh_ref,
    score_ref, reach_ref, local_ref, decay_ref, piece_ref, low_ref, maplow_ref, log_ref, mixhalo_ref, turned_ref,
):
    x = jnp.concatenate([halo_ref[0], x_ref[0]], axis=0).astype(F32)
    mixed = x * lax.rsqrt(jnp.mean(x * x, axis=-1, keepdims=True) + 1e-06) * gain_ref[...]
    mixed = mixed.astype(BF16)
    main = mixed[HALO:]
    mixhalo_ref[0] = mixed[:HALO]
    turned_ref[...] = jnp.transpose(main)
    proj_q = dot(mixed, wq_ref[...]).astype(BF16)
    proj_k = dot(mixed, wk_ref[...]).astype(BF16)
    proj_v = dot(mixed, wv_ref[...]).astype(BF16)
    wide = heads * DK
    proj_ref[0, :, :wide] = proj_q
    proj_ref[0, :, wide : 2 * wide] = proj_k
    proj_ref[0, :, 2 * wide :] = proj_v
    pg_ref[0] = dot(main, wg_ref[...])
    gates = dot(main, wgates_ref[...]) + bias_ref[...]
    gates_ref[0] = gates
    size = main.shape[0]
    rows, cols = rows_cols(size)
    lower = rows >= cols
    strict = rows > cols
    sums = ones_dot(lower.astype(BF16), log_sigmoid(gates))
    sums_ref[0] = sums
    sums_t = jnp.transpose(sums)
    conv_q = silu(conv_pre(proj_q.astype(F32), cq_ref[...]))
    conv_k = silu(conv_pre(proj_k.astype(F32), ck_ref[...]))
    conv_v = silu(conv_pre(proj_v.astype(F32), cv_ref[...]))
    each = range(heads)
    queries = [unit(conv_q[:, h * DK : (h + 1) * DK])[0] * SCALE for h in each]
    keys = [unit(conv_k[:, h * DK : (h + 1) * DK])[0] for h in each]
    values = [conv_v[:, h * DV : (h + 1) * DV] for h in each]
    beta = [sigmoid(gates[:, h : h + 1]) for h in each]
    total = [sums[:, heads + h : heads + h + 1] for h in each]
    decay = [
        jnp.where(
            lower, jnp.exp(jnp.minimum(total[h] - sums_t[heads + h : heads + h + 1, :], 0.0)), 0.0
        )
        for h in each
    ]
    scaled = [beta[h] * keys[h] for h in each]
    lowers = [jnp.where(strict, dot3(keys[h], scaled[h], NT) * decay[h], 0.0) for h in each]
    inverses = inverse_unit(lowers, rows, cols)
    growth = [jnp.exp(total[h]) for h in each]
    last = [total[h][size - 1 : size] for h in each]
    tail = [jnp.exp(last[h] - total[h]) * scaled[h] for h in each]
    mapk = [dot3(inverses[h], growth[h] * keys[h]) for h in each]
    fresh = [dot3(inverses[h], values[h]) for h in each]
    scores = [dot(queries[h], scaled[h], NT) * decay[h] for h in each]
    moved = [-dot3(tail[h], mapk[h], TN) for h in each]
    shift = [dot3(tail[h], fresh[h], TN) for h in each]
    reach = [growth[h] * queries[h] - dot(scores[h], mapk[h]) for h in each]
    local = [dot(scores[h], fresh[h]) for h in each]
    for h in each:
        piece_ref[0, h, :, :DK] = moved[h]
        piece_ref[0, h, :, DK:] = shift[h]
        note = log_rows(last[h])
        log_ref[0, h] = jnp.broadcast_to(last[h], (8, LANES))
        maplow_ref[0, h, :DK] = moved[h].astype(BF16)
        maplow_ref[0, h, DK:] = note
        low_ref[0, h, :DK, :DK] = moved[h].astype(BF16)
        low_ref[0, h, :DK, DK:] = shift[h].astype(BF16)
        low_ref[0, h, DK:] = jnp.concatenate([note] * (1 + DV // DK), axis=1)
        inv_ref[0, h] = inverses[h]
        mapk_ref[0, h] = mapk[h]
        fresh_ref[0, h] = fresh[h]
        score_ref[0, h] = scores[h]
        reach_ref[0, h] = reach[h]
        local_ref[0, h] = local[h]
        decay_ref[0, h] = decay[h]


def log_rows(log):
    log = jnp.broadcast_to(log, (1, LANES))
    high = log.astype(BF16).astype(F32)
    middle = (log - high).astype(BF16).astype(F32)
    rest = log - high - middle
    place = lax.broadcasted_iota(jnp.int32, (NOTE, LANES), 0)
    zero = jnp.zeros((NOTE, LANES), F32)
    rows = jnp.where(place == 0, high, jnp.where(place == 1, middle, jnp.where(place == 2, rest, zero)))
    return rows.astype(BF16)


def log_of(rows):
    return jnp.sum(rows.astype(F32), axis=0, keepdims=True)


def join_body(
    pairs, last, piece_ref, log_ref, got_ref, out_ref, newlog_ref, low_ref, maplow_ref, *far_ref
):
    wide = 1 + DV // DK
    for p in range(pairs):
        own = piece_ref[p]
        got_low = got_ref[p, :DK]
        got = got_low.astype(F32)
        own_log = log_ref[p, :1]
        got_log = log_of(got_ref[p, DK:, :LANES])
        mine = jnp.concatenate([jnp.exp(own_log)] * wide, axis=1)
        high, low = halves(own[:, :DK])
        moved = dot(high, got_low) + dot(low, got_low) + mine * got
        map_part = moved[:, :DK] + jnp.exp(got_log) * own[:, :DK]
        shift_part = moved[:, DK:] + own[:, DK:]
        new_log = own_log + got_log
        out_ref[p, :, :DK] = map_part
        out_ref[p, :, DK:] = shift_part
        newlog_ref[p] = jnp.broadcast_to(new_log, (8, LANES))
        low_ref[p, :DK, :DK] = map_part.astype(BF16)
        low_ref[p, :DK, DK:] = shift_part.astype(BF16)
        note = log_rows(new_log)
        low_ref[p, DK:] = jnp.concatenate([note] * wide, axis=1)
        maplow_ref[p, :DK] = map_part.astype(BF16)
        maplow_ref[p, DK:] = note
        if last:
            far_ref[0][p] = shift_part.astype(BF16)


def entry_body(pairs, near_ref, far_ref, out_ref):
    for p in range(pairs):
        far = far_ref[p]
        scale = jnp.exp(log_of(near_ref[p, DK:, DK:]))
        moved = dot(near_ref[p, :DK, :DK], far) + scale * far.astype(F32)
        out_ref[p] = moved + near_ref[p, :DK, DK:].astype(F32)


def back_body(pairs, map_ref, own_ref, got_ref, out_ref, low_ref):
    for p in range(pairs):
        got = got_ref[p]
        scale = jnp.concatenate([jnp.exp(log_of(map_ref[p, DK:]))] * (DV // DK), axis=1)
        out = own_ref[p] + dot(map_ref[p, :DK], got, TN) + scale * got.astype(F32)
        out_ref[p] = out
        low_ref[p] = out.astype(BF16)


def exit_body(pairs, map_ref, near_ref, far_ref, out_ref):
    for p in range(pairs):
        far = far_ref[p]
        scale = jnp.concatenate([jnp.exp(log_of(map_ref[p, DK:]))] * (DV // DK), axis=1)
        moved = dot(map_ref[p, :DK], far, TN) + scale * far.astype(F32)
        out_ref[p] = near_ref[p].astype(F32) + moved


def mixer_out_body(
    heads, state_ref, fresh_ref, mapk_ref, reach_ref, local_ref, pg_ref, gain_ref, wout_ref,
    made_ref, output_ref, gated_ref, attn_ref,
):
    for h in range(heads):
        state = state_ref[0, h]
        made_ref[0, h] = fresh_ref[0, h] - dot3(mapk_ref[0, h], state)
        output = local_ref[0, h] + dot(reach_ref[0, h], state)
        output_ref[0, :, h * DV : (h + 1) * DV] = output
        scale = lax.rsqrt(jnp.mean(output * output, axis=-1, keepdims=True) + 1e-05)
        gate = pg_ref[0, :, h * DV : (h + 1) * DV]
        gated_ref[0, :, h * DV : (h + 1) * DV] = (
            output * scale * gain_ref[...] * silu(gate)
        ).astype(BF16)
    attn_ref[0] = dot(gated_ref[0], wout_ref[...]).astype(BF16)


def feed_body(
    x_ref, mine_ref, other_ref, cot_ref, gain_ref, wgate_ref, wup_ref, wdown_ref, resid_ref,
    hidden_ref, dgate_ref, dup_ref, down_ref, dnorm_ref, normed_ref, cot_turned_ref,
):
    attn = mine_ref[0].astype(F32) + other_ref[0].astype(F32)
    resid = x_ref[0].astype(F32) + attn
    resid_ref[0] = resid
    normed = resid * lax.rsqrt(jnp.mean(resid * resid, axis=-1, keepdims=True) + 1e-06)
    normed = (normed * gain_ref[...]).astype(BF16)
    normed_ref[...] = jnp.transpose(normed)
    cot_turned_ref[...] = jnp.transpose(cot_ref[0])
    gate = dot(normed, wgate_ref[...])
    up = dot(normed, wup_ref[...])
    d_hidden = dot(cot_ref[0], wdown_ref[...], NT)
    sig = sigmoid(gate)
    active = gate * sig
    hidden = (active * up).astype(BF16)
    hidden_ref[0] = hidden
    d_gate = (d_hidden * up * (sig + active * (1.0 - sig))).astype(BF16)
    d_up = (d_hidden * active).astype(BF16)
    dgate_ref[0] = d_gate
    dup_ref[0] = d_up
    down_ref[0] = dot(hidden, wdown_ref[...]).astype(BF16)
    dnorm_ref[0] = (dot(d_gate, wgate_ref[...], NT) + dot(d_up, wup_ref[...], NT)).astype(BF16)


def mixer_back_body(
    heads, resid_ref, mine_ref, other_ref, cot_ref, output_ref, pg_ref, reach_ref, gain_ref,
    wout_ref, ogain_ref, dresid_ref, dout_ref, dpg_ref, back_ref, low_ref, dattn_ref, dgain_ref,
    dogain_ref,
):
    step = pl.program_id(0)
    resid = resid_ref[0]
    inverse = lax.rsqrt(jnp.mean(resid * resid, axis=-1, keepdims=True) + 1e-06)
    unit_resid = resid * inverse
    d_normed = mine_ref[0].astype(F32) + other_ref[0].astype(F32)
    d_gain = jnp.sum(d_normed * unit_resid, axis=0, keepdims=True)
    d_unit = d_normed * gain_ref[...]
    d_resid = inverse * (
        d_unit - unit_resid * jnp.mean(d_unit * unit_resid, axis=-1, keepdims=True)
    )
    d_resid = d_resid + cot_ref[0].astype(F32)
    dresid_ref[0] = d_resid
    d_attn = d_resid.astype(BF16)
    dattn_ref[...] = jnp.transpose(d_attn)
    d_gated = dot(d_attn, wout_ref[...], NT)
    d_ogain = jnp.zeros((1, DV), F32)
    for h in range(heads):
        part = slice(h * DV, (h + 1) * DV)
        output = output_ref[0, :, part]
        inverse = lax.rsqrt(jnp.mean(output * output, axis=-1, keepdims=True) + 1e-05)
        unit_out = output * inverse
        gate = pg_ref[0, :, part]
        grad = d_gated[:, part]
        active = silu(gate)
        d_ogain = d_ogain + jnp.sum(grad * unit_out * active, axis=0, keepdims=True)
        dpg_ref[0, :, part] = (grad * unit_out * ogain_ref[...] * silu_slope(gate)).astype(BF16)
        d_unit = grad * ogain_ref[...] * active
        d_out = inverse * (d_unit - unit_out * jnp.mean(d_unit * unit_out, axis=-1, keepdims=True))
        dout_ref[0, :, part] = d_out
        back = dot(reach_ref[0, h], d_out, TN)
        back_ref[0, h] = back
        low_ref[0, h] = back.astype(BF16)

    @pl.when(step == 0)
    def _():
        dgain_ref[...] = d_gain
        dogain_ref[...] = d_ogain

    @pl.when(step > 0)
    def _():
        dgain_ref[...] += d_gain
        dogain_ref[...] += d_ogain


def conv_back(grad, extended, taps, pre):
    d_pre = grad * silu_slope(pre)
    padded = jnp.concatenate([jnp.zeros((HALO, d_pre.shape[1]), F32), d_pre], axis=0)
    length = padded.shape[0]
    d_ext = taps[CONV - 1 : CONV] * padded
    d_taps = []
    for offset in range(CONV):
        back = CONV - 1 - offset
        if back:
            d_ext = d_ext + taps[offset : offset + 1] * pltpu.roll(padded, length - back, 0)
            shifted = pltpu.roll(extended, back, 0)
        else:
            shifted = extended
        d_taps.append(jnp.sum(padded * shifted, axis=0, keepdims=True))
    return d_ext, jnp.concatenate(d_taps, axis=0)


def early_body(
    heads, proj_ref, gates_ref, sums_ref, dout_ref, state_ref, made_ref, inv_ref, score_ref,
    decay_ref, cq_ref, ck_ref, xone_ref, xmap_ref, dkey_ref, dcol_ref, dext_ref, dtap_ref,
):
    step = pl.program_id(0)
    wide = heads * DK
    ext_q = proj_ref[0, :, :wide].astype(F32)
    ext_k = proj_ref[0, :, wide : 2 * wide].astype(F32)
    pre_q = conv_pre(ext_q, cq_ref[...])
    conv_q = silu(pre_q)
    conv_k = silu(conv_pre(ext_k, ck_ref[...]))
    gates = gates_ref[0]
    sums = sums_ref[0]
    size = gates.shape[0]
    each = range(heads)
    units = [unit(conv_q[:, h * DK : (h + 1) * DK]) for h in each]
    queries = [units[h][0] * SCALE for h in each]
    keys = [unit(conv_k[:, h * DK : (h + 1) * DK])[0] for h in each]
    beta = [sigmoid(gates[:, h : h + 1]) for h in each]
    total = [sums[:, heads + h : heads + h + 1] for h in each]
    growth = [jnp.exp(total[h]) for h in each]
    tail = [jnp.exp(total[h][size - 1 : size] - total[h]) * beta[h] * keys[h] for h in each]
    d_out = [dout_ref[0, :, h * DV : (h + 1) * DV] for h in each]
    d_made = [dot(score_ref[0, h], d_out[h], TN) for h in each]
    d_score = [dot(d_out[h], made_ref[0, h], NT) * decay_ref[0, h] for h in each]
    d_query = [
        dot3(d_score[h], beta[h] * keys[h]) + dot(growth[h] * d_out[h], state_ref[0, h], NT)
        for h in each
    ]
    d_key = [dot3(d_score[h], queries[h], TN) for h in each]
    x_one = [dot(inv_ref[0, h], d_made[h], TN) for h in each]
    x_map = [dot(inv_ref[0, h], tail[h], TN) for h in each]
    lanes = lax.broadcasted_iota(jnp.int32, (size, LANES), 1)
    cols = jnp.zeros((size, LANES), F32)
    grads = []
    for h in each:
        xone_ref[0, h] = x_one[h]
        xmap_ref[0, h] = x_map[h]
        dkey_ref[0, h] = beta[h] * d_key[h]
        key_sum = row_sum(d_key[h] * keys[h])
        cols = cols + jnp.where(lanes == h, key_sum, 0.0)
        d_total = row_sum(d_query[h] * queries[h]) - beta[h] * key_sum
        cols = cols + jnp.where(lanes == heads + h, d_total, 0.0)
        unit_q, inverse = units[h]
        d_unit = d_query[h] * SCALE
        grads.append(inverse * (d_unit - unit_q * row_sum(d_unit * unit_q)))
    dcol_ref[0] = cols
    d_ext, d_taps = conv_back(jnp.concatenate(grads, axis=1), ext_q, cq_ref[...], pre_q)
    dext_ref[0] = d_ext

    @pl.when(step == 0)
    def _():
        dtap_ref[...] = d_taps

    @pl.when(step > 0)
    def _():
        dtap_ref[...] += d_taps


def late_body(
    heads, proj_ref, gates_ref, sums_ref, dend_ref, state_ref, made_ref, decay_ref, xone_ref,
    xmap_ref, dkey_ref, dcol_ref, dextq_ref, ck_ref, cv_ref, dext_ref, dgates_ref, dtap_ref, dbias_ref,
):
    step = pl.program_id(0)
    wide = heads * DK
    ext_k = proj_ref[0, :, wide : 2 * wide].astype(F32)
    ext_v = proj_ref[0, :, 2 * wide :].astype(F32)
    pre_k = conv_pre(ext_k, ck_ref[...])
    pre_v = conv_pre(ext_v, cv_ref[...])
    conv_k = silu(pre_k)
    gates = gates_ref[0]
    sums = sums_ref[0]
    size = gates.shape[0]
    rows, cols = rows_cols(size)
    strict = rows > cols
    each = range(heads)
    units = [unit(conv_k[:, h * DK : (h + 1) * DK]) for h in each]
    keys = [units[h][0] for h in each]
    beta = [sigmoid(gates[:, h : h + 1]) for h in each]
    total = [sums[:, heads + h : heads + h + 1] for h in each]
    growth = [jnp.exp(total[h]) for h in each]
    left = [jnp.exp(total[h][size - 1 : size] - total[h]) for h in each]
    d_end = [dend_ref[0, h] for h in each]
    made = [made_ref[0, h] for h in each]
    state = [state_ref[0, h] for h in each]
    d_rhs = [xone_ref[0, h] + dot(xmap_ref[0, h], d_end[h]) for h in each]
    d_tail = [dot(made[h], d_end[h], NT) for h in each]
    d_lower = [
        jnp.where(strict, -dot(d_rhs[h], made[h], NT) * decay_ref[0, h], 0.0) for h in each
    ]
    d_plain = [
        dot3(d_lower[h], beta[h] * keys[h]) - dot(growth[h] * d_rhs[h], state[h], NT) for h in each
    ]
    d_turned = [dot3(d_lower[h], keys[h], TN) for h in each]
    lanes = lax.broadcasted_iota(jnp.int32, (size, LANES), 1)
    places = lax.broadcasted_iota(jnp.int32, (size, 1), 0)
    d_col = dcol_ref[0]
    grads_k = []
    for h in each:
        turned = row_sum(d_turned[h] * keys[h])
        tails = row_sum(d_tail[h] * keys[h])
        tail_weight = left[h] * beta[h]
        d_key = d_plain[h] + beta[h] * d_turned[h] + tail_weight * d_tail[h] + dkey_ref[0, h]
        d_total = row_sum(d_plain[h] * keys[h]) - beta[h] * turned - tail_weight * tails
        ended = jnp.sum(tail_weight * tails, axis=0, keepdims=True)
        whole = jnp.sum(row_sum(d_end[h] * state[h]), axis=0, keepdims=True)
        ended = ended + growth[h][size - 1 : size] * whole
        d_total = d_total + jnp.where(places == size - 1, ended, 0.0)
        d_col = d_col + jnp.where(lanes == h, turned + left[h] * tails, 0.0)
        d_col = d_col + jnp.where(lanes == heads + h, d_total, 0.0)
        unit_k, inverse = units[h]
        grads_k.append(inverse * (d_key - unit_k * row_sum(d_key * unit_k)))
    upper = (rows <= cols).astype(BF16)
    d_decay = ones_dot(upper, d_col)
    rate = sigmoid(gates)
    d_gates = jnp.where(
        lanes < heads, d_col * rate * (1.0 - rate), d_decay / (1.0 + jnp.exp(gates))
    )
    d_gates = jnp.where(lanes < 2 * heads, d_gates, 0.0)
    dgates_ref[0] = d_gates.astype(BF16)
    d_bias = jnp.sum(d_gates, axis=0, keepdims=True)
    dext_k, dtaps_k = conv_back(jnp.concatenate(grads_k, axis=1), ext_k, ck_ref[...], pre_k)
    dext_v, dtaps_v = conv_back(jnp.concatenate(d_rhs, axis=1), ext_v, cv_ref[...], pre_v)
    dext_ref[0, :, :wide] = dextq_ref[0]
    dext_ref[0, :, wide : 2 * wide] = dext_k
    dext_ref[0, :, 2 * wide :] = dext_v

    @pl.when(step == 0)
    def _():
        dtap_ref[:, :wide] = dtaps_k
        dtap_ref[:, wide:] = dtaps_v
        dbias_ref[...] = d_bias

    @pl.when(step > 0)
    def _():
        dtap_ref[:, :wide] += dtaps_k
        dtap_ref[:, wide:] += dtaps_v
        dbias_ref[...] += d_bias


def input_back_body(
    dext_ref, dpg_ref, dgates_ref, wq_ref, wk_ref, wv_ref, wg_ref, wgates_ref, dqk_ref, dv_ref,
    dqkhalo_ref, dvhalo_ref, dmixed_ref, dhalo_ref,
):
    wide = wq_ref.shape[1]
    d_proj = dext_ref[0].astype(BF16)
    dqk_ref[0] = d_proj[HALO:, : 2 * wide]
    dv_ref[0] = d_proj[HALO:, 2 * wide :]
    dqkhalo_ref[0] = d_proj[:HALO, : 2 * wide]
    dvhalo_ref[0] = d_proj[:HALO, 2 * wide :]
    d_mixed = dot(d_proj[:, :wide], wq_ref[...], NT)
    d_mixed = d_mixed + dot(d_proj[:, wide : 2 * wide], wk_ref[...], NT)
    d_mixed = d_mixed + dot(d_proj[:, 2 * wide :], wv_ref[...], NT)
    dhalo_ref[0] = d_mixed[:HALO].astype(BF16)
    main = d_mixed[HALO:] + dot(dpg_ref[0], wg_ref[...], NT)
    main = main + dot(dgates_ref[0], wgates_ref[...], NT)
    dmixed_ref[0] = main.astype(BF16)


def last_body(
    x_ref, mine_ref, other_ref, halo_ref, halo_other_ref, dresid_ref, gain_ref, grad_ref, dgain_ref,
):
    x = x_ref[0].astype(F32)
    inverse = lax.rsqrt(jnp.mean(x * x, axis=-1, keepdims=True) + 1e-06)
    unit_x = x * inverse
    d_mixed = mine_ref[0].astype(F32) + other_ref[0].astype(F32)
    halo = halo_ref[0].astype(F32) + halo_other_ref[0].astype(F32)
    size = d_mixed.shape[0]
    d_mixed = jnp.concatenate([d_mixed[: size - HALO], d_mixed[size - HALO :] + halo], axis=0)
    d_unit = d_mixed * gain_ref[...]
    back = inverse * (d_unit - unit_x * jnp.mean(d_unit * unit_x, axis=-1, keepdims=True))
    grad_ref[0] = dresid_ref[0] + back
    d_gain = jnp.sum(d_mixed * unit_x, axis=0, keepdims=True)
    step = pl.program_id(0)

    @pl.when(step == 0)
    def _():
        dgain_ref[...] = d_gain

    @pl.when(step > 0)
    def _():
        dgain_ref[...] += d_gain


def result_body(resid_ref, down_ref, downother_ref, result_ref):
    down = down_ref[0].astype(F32) + downother_ref[0].astype(F32)
    result_ref[0] = (resid_ref[0] + down).astype(BF16)


def held_rows(left_refs, index_ref, first, blocks, held):
    share = left_refs[0].shape[1]
    for left_ref, held_ref in zip(left_refs, held):
        for place in range(blocks):
            held_ref[place * share : (place + 1) * share] = left_ref[index_ref[first + place]]


def send_body(terms, first, blocks, lefts, rights, index_ref, *refs):
    out_ref, held = refs[lefts + rights], refs[lefts + rights + 1 :]
    held_rows(refs[:lefts], index_ref, first, blocks, held)
    at = 0
    for factors, width in terms:
        total = sum(dot(held[left][...], refs[lefts + right][...]) for left, right in factors)
        out_ref[:, at : at + width] = total.astype(BF16)
        at += width


def keep_body(terms, blocks, parts, lefts, rights, index_ref, *refs):
    got_ref, keep_ref = refs[lefts + rights], refs[lefts + rights + 1]
    send_refs = refs[lefts + rights + 2 : lefts + rights + 1 + parts]
    held = refs[lefts + rights + 1 + parts :]
    held_rows(refs[:lefts], index_ref, 0, blocks, held)
    rows = keep_ref.shape[0]
    at = 0
    for factors, width in terms:
        total = got_ref[:, at : at + width].astype(F32)
        for left, right in factors:
            total = total + dot(held[left][...], refs[lefts + right][...])
        keep_ref[:, at : at + width] = total[:rows]
        for part in range(1, parts):
            send_refs[part - 1][:, at : at + width] = total[part * rows : (part + 1) * rows].astype(BF16)
        at += width


def add_body(parts, gots, keep_ref, *refs):
    total = keep_ref[...]
    for got_ref in refs[:gots]:
        total = total + got_ref[...].astype(F32)
    out_ref = refs[gots]
    rows = out_ref.shape[0]
    out_ref[...] = total[:rows]
    for part in range(1, parts):
        refs[gots + part][...] = total[part * rows : (part + 1) * rows].astype(BF16)


def joined_body(widths, *refs):
    keep_ref, send_ref = refs[-2:]
    rows = keep_ref.shape[0]
    at = 0
    for number, width in enumerate(widths):
        total = refs[2 * number][...] + refs[2 * number + 1][...].astype(F32)
        keep_ref[:, at : at + width] = total[:rows]
        send_ref[:, at : at + width] = total[rows:].astype(BF16)
        at += width


def total_body(cuts, gots, *refs):
    at = 0
    for ref, width in zip(refs[1 + gots :], cuts):
        total = refs[0][:, at : at + width]
        for got_ref in refs[1 : 1 + gots]:
            total = total + got_ref[:, at : at + width].astype(F32)
        ref[...] = total
        at += width


def pack_body(tapq_ref, tapkv_ref, bias_ref, ffn_ref, mix_ref, ogain_ref, other_ref, out_ref):
    wide = tapq_ref.shape[1]
    out_ref[...] = jnp.zeros_like(out_ref)
    out_ref[:CONV, :wide] = tapq_ref[...]
    out_ref[:CONV, wide:] = tapkv_ref[...]
    out_ref[4:5, :LANES] = bias_ref[...]
    out_ref[5:6] = ffn_ref[...]
    out_ref[6:7] = mix_ref[...]
    out_ref[7:8, :DV] = ogain_ref[...] + other_ref[...]


def unpack_body(heads, count, start_ref, *refs):
    total = refs[0][...]
    for ref in refs[1:count]:
        total = total + ref[...]
    tapq_ref, tapk_ref, tapv_ref, bias_ref, ogain_ref, gains_ref = refs[count:]
    wide = tapq_ref.shape[1]
    share = gains_ref.shape[1]
    tapq_ref[...] = total[:CONV, :wide]
    tapk_ref[...] = total[:CONV, wide : 2 * wide]
    tapv_ref[...] = total[:CONV, 2 * wide :]
    for row in range(2):
        bias_ref[row : row + 1] = total[4:5, row * heads : (row + 1) * heads]
    ogain_ref[...] = total[7:8, : ogain_ref.shape[1]]
    width = total.shape[1]
    turned = pltpu.roll(total, lax.rem(width - start_ref[0], width), 1)
    gains_ref[...] = turned[5:7, :share]


def sum_body(count, *refs):
    total = refs[0][...]
    for ref in refs[1:count]:
        total = total + ref[...]
    refs[count][...] = total


def by_seq(shape):
    rest = len(shape) - 1
    return pl.BlockSpec((1,) + tuple(shape[1:]), lambda s: (s,) + (0,) * rest)


def whole(shape):
    rest = len(shape)
    return pl.BlockSpec(tuple(shape), lambda s: (0,) * rest)


def without(body, position, count):
    def shorter(*refs):
        return body(*refs[:position], *refs[position + count :])

    return shorter if count else body


def call(body, name, seqs, parts, shared, outs, sums=(), turned=(), after=(), flops=0, limit=None):
    operands = list(parts) + list(shared)
    listed = list(outs) + list(turned) + list(sums)
    out_shape = [jax.ShapeDtypeStruct(shape, kind) for shape, kind in listed]
    moved = sum(a.size * a.dtype.itemsize for a in operands + out_shape)
    return pl.pallas_call(
        without(body, len(operands), len(after)),
        grid=(seqs,),
        in_specs=[by_seq(a.shape) for a in parts]
        + [whole(a.shape) for a in shared]
        + [pl.BlockSpec(memory_space=pl.ANY)] * len(after),
        out_specs=[by_seq(shape) for shape, _ in outs]
        + [pl.BlockSpec((shape[0], shape[1] // seqs), lambda s: (0, s)) for shape, _ in turned]
        + [whole(shape) for shape, _ in sums],
        out_shape=out_shape,
        compiler_params=pltpu.CompilerParams(vmem_limit_bytes=limit or VMEM_LIMIT),
        cost_estimate=pl.CostEstimate(flops=int(flops), bytes_accessed=int(moved), transcendentals=0),
        name=name,
    )(*operands, *after)


def small_call(body, name, arrays, outs, after=(), scalars=(), scratch=(), flops=2e8):
    out_shape = [jax.ShapeDtypeStruct(shape, kind) for shape, kind in outs]
    moved = sum(a.size * a.dtype.itemsize for a in list(arrays) + out_shape)
    return pl.pallas_call(
        without(body, len(scalars) + len(arrays), len(after)),
        in_specs=[pl.BlockSpec(memory_space=pltpu.SMEM)] * len(scalars)
        + [pl.BlockSpec(memory_space=pltpu.VMEM)] * len(arrays)
        + [pl.BlockSpec(memory_space=pl.ANY)] * len(after),
        out_specs=[pl.BlockSpec(memory_space=pltpu.VMEM)] * len(outs),
        out_shape=out_shape,
        scratch_shapes=list(scratch),
        compiler_params=pltpu.CompilerParams(vmem_limit_bytes=SMALL_LIMIT),
        cost_estimate=pl.CostEstimate(flops=int(flops), bytes_accessed=int(moved), transcendentals=0),
        name=name,
    )(*scalars, *arrays, *after)


class Halved:
    def __init__(self, name, steps, me, lefts, rights, terms):
        self.name, self.lefts, self.rights, self.terms = (name, lefts, rights, terms)
        order = [bit for step in steps for bit in step]
        self.steps = steps
        self.index = block_index(order, me)
        self.count = 1 << len(order)
        self.share, self.tokens = lefts[0].shape[1:]
        self.columns = sum(width for _, width in terms)
        self.done = 0

    def trade(self, sends):
        bits = self.steps[self.done]
        self.done += 1
        self.gots = []
        for part, send in enumerate(sends, 1):
            moved = sum(
                ((part >> (len(bits) - 1 - place)) & 1) << bit for place, bit in enumerate(bits)
            )
            self.gots.append(traded(send, moved))

    def multiplied(self, body, suffix, extra, outs, after):
        blocks = self.count // 2
        return small_call(
            body, self.name + suffix, list(self.lefts) + list(self.rights) + extra, outs, after,
            scalars=[self.index],
            scratch=[pltpu.VMEM((blocks * self.share, left.shape[2]), BF16) for left in self.lefts],
            flops=2 * blocks * self.share * self.tokens * self.columns,
        )

    def outs(self, rows):
        parts = 1 << len(self.steps[self.done])
        return parts, [((rows // parts, self.columns), F32)] + [
            ((rows // parts, self.columns), BF16)
        ] * (parts - 1)

    def send(self, *after):
        blocks = self.count // 2
        body = functools.partial(
            send_body, self.terms, blocks, blocks, len(self.lefts), len(self.rights)
        )
        rows = blocks * self.share
        sends = self.multiplied(body, "_send", [], [((rows, self.columns), BF16)], after)
        self.trade(sends)
        return sends[0]

    def keep(self, *after):
        blocks = self.count // 2
        parts, outs = self.outs(blocks * self.share)
        body = functools.partial(
            keep_body, self.terms, blocks, parts, len(self.lefts), len(self.rights)
        )
        self.kept, *sends = self.multiplied(body, "_keep", self.gots, outs, after)
        self.trade(sends)
        return self.kept

    def add(self, *after):
        parts, outs = self.outs(self.kept.shape[0])
        body = functools.partial(add_body, parts, len(self.gots))
        self.kept, *sends = small_call(
            body, self.name + "_add", [self.kept] + self.gots, outs, after, flops=1e6
        )
        self.trade(sends)
        return self.kept

    def left(self):
        return len(self.steps) - self.done

    def total(self, cuts, *after):
        rows = self.kept.shape[0]
        outs = [((rows, width), F32) for width in cuts]
        return small_call(
            functools.partial(total_body, tuple(cuts), len(self.gots)), self.name + "_total",
            [self.kept] + self.gots, outs, after, flops=1e6,
        )


def joined(name, groups, *after):
    whole_sum = copy.copy(groups[0])
    whole_sum.name = name
    whole_sum.columns = sum(group.columns for group in groups)
    rows = groups[0].kept.shape[0] // 2
    shape = (rows, whole_sum.columns)
    operands = [array for group in groups for array in [group.kept] + group.gots]
    body = functools.partial(joined_body, [group.columns for group in groups])
    whole_sum.kept, send = small_call(
        body, name, operands, [(shape, F32), (shape, BF16)], after, flops=1e6
    )
    whole_sum.trade([send])
    return whole_sum


def halving_steps(count, first):
    bits = list(range(count.bit_length() - 1))
    return [[bit] for bit in first] + [[bit] for bit in bits if bit not in first]


def block_index(order, me):
    count = 1 << len(order)
    moved = [
        sum(((place >> (len(order) - 1 - step)) & 1) << bit for step, bit in enumerate(order))
        for place in range(count)
    ]
    return jnp.bitwise_xor(jnp.array(moved, jnp.int32), me)


def traded(block, moved):
    count = lax.axis_size("seq")
    return lax.ppermute(block, "seq", [(i, i ^ moved) for i in range(count)])


def passed_along(block, axis, distance):
    devices = range(lax.axis_size(axis))
    route = [(i - distance, i) for i in devices if i - distance in devices]
    return lax.ppermute(block, axis, route)


def swapped(block):
    count = lax.axis_size("head")
    return lax.ppermute(block, "head", [(i, i ^ 1) for i in range(count)])


def on_device(
    tokens, w_query, w_key, w_value, w_outgate, w_gates, gate_bias, conv_query, conv_key,
    conv_value, out_gain, w_out, mix_gain, ffn_gain, w_gate, w_up, w_down, cotangent,
):
    seqs, size, width = tokens.shape
    heads = gate_bias.shape[1]
    pairs = seqs * heads
    units = w_gate.shape[1]
    count, me = lax.axis_size("seq"), lax.axis_index("seq")
    wide = heads * DK
    out_wide = heads * DV
    proj_wide = 2 * wide + out_wide

    halo = passed_along(tokens[:, size - HALO :], "seq", 1)
    gates_w = jnp.swapaxes(w_gates, 0, 1).reshape(width, 2 * heads)
    gates_w = jnp.pad(gates_w, ((0, 0), (0, LANES - 2 * heads)))
    bias = jnp.pad(gate_bias.reshape(1, 2 * heads), ((0, 0), (0, LANES - 2 * heads)))
    mix_row = mix_gain.reshape(1, width)
    ffn_row = ffn_gain.reshape(1, width)
    out_row = out_gain.reshape(1, DV)
    square = (seqs, heads, size, size)
    by_key = (seqs, heads, size, DK)
    by_value = (seqs, heads, size, DV)
    tokens_here = seqs * size
    steps_x, steps_y = halving_steps(count, (0, 1)), halving_steps(count, (1, 0))
    steps_yzx, steps_zxy = halving_steps(count, (1, 2, 0)), halving_steps(count, (2, 0, 1))
    turned_shape = (width, tokens_here)
    share = width // count

    def in_blocks(turned):
        return turned.reshape(count, share, tokens_here)

    def flat(field):
        return field.reshape(tokens_here, field.shape[2])

    (
        proj, proj_g, gates, sums, inv, mapk, fresh, score, reach, local, decay, piece, low,
        map_low, log, mixed_halo, mixed_t,
    ) = call(
        functools.partial(first_body, heads), "project_and_local", seqs, [halo, tokens],
        [mix_row, w_query, w_key, w_value, w_outgate, gates_w, bias, conv_query, conv_key, conv_value],
        [
            ((seqs, size + HALO, proj_wide), BF16),
            ((seqs, size, out_wide), F32), ((seqs, size, LANES), F32), ((seqs, size, LANES), F32),
            (square, F32), (by_key, F32), (by_value, F32), (square, F32), (by_key, F32),
            (by_value, F32), (square, F32), ((seqs, heads, DK, DK + DV), F32),
            ((seqs, heads, DK + NOTE, DK + DV), BF16),
            ((seqs, heads, DK + NOTE, DK), BF16), ((seqs, heads, 8, LANES), F32),
            ((seqs, HALO, width), BF16),
        ],
        turned=[(turned_shape, BF16)],
        flops=1e10,
        limit=WHOLE_LIMIT,
    )

    piece = piece.reshape(pairs, DK, DK + DV)
    low = low.reshape(pairs, DK + NOTE, DK + DV)
    log = log.reshape(pairs, 8, LANES)
    maps = [map_low.reshape(pairs, DK + NOTE, DK)]
    state_shape = (pairs, DK, DV)
    dists = []
    reach_by = 1
    while reach_by * 2 < count:
        dists.append(reach_by)
        reach_by *= 2
    for level, d in enumerate(dists):
        got = passed_along(low, "seq", d)
        last = level + 1 == len(dists)
        outs = [(piece.shape, F32), (log.shape, F32), (low.shape, BF16), (maps[0].shape, BF16)]
        if last:
            outs.append((state_shape, BF16))
        piece, log, low, map_low, *far = small_call(
            functools.partial(join_body, pairs, last), "join", [piece, log, got], outs
        )
        maps.append(map_low)
    near = passed_along(low, "seq", 1)
    far = passed_along(far[0], "seq", 1 + reach_by)
    back_maps = [maps[0]]
    for level in range(1, len(dists)):
        back_maps.append(passed_along(maps[level], "seq", 1 - dists[level]))
    near_map = passed_along(maps[-1], "seq", -reach_by)
    (state,) = small_call(
        functools.partial(entry_body, pairs), "entry", [near, far], [(state_shape, F32)]
    )
    state = state.reshape(seqs, heads, DK, DV)

    made, output, gated, attn = call(
        functools.partial(mixer_out_body, heads), "mixer_out", seqs,
        [state, fresh, mapk, reach, local, proj_g], [out_row, w_out],
        [
            (by_value, F32), ((seqs, size, out_wide), F32), ((seqs, size, out_wide), BF16),
            ((seqs, size, width), BF16),
        ],
        after=[near_map] + back_maps[1:],
        flops=1.5e9,
    )
    attn_other = swapped(attn)

    resid, hidden, d_gate, d_up, down, d_norm, normed_t, cot_t = call(
        feed_body, "feed_forward", seqs, [tokens, attn, attn_other, cotangent],
        [ffn_row, w_gate, w_up, w_down],
        [
            ((seqs, size, width), F32), ((seqs, size, units), BF16), ((seqs, size, units), BF16),
            ((seqs, size, units), BF16), ((seqs, size, width), BF16), ((seqs, size, width), BF16),
        ],
        turned=[(turned_shape, BF16), (turned_shape, BF16)],
        flops=1.2e10,
    )
    d_norm_other = swapped(d_norm)
    down_other = swapped(down)

    normed_b, cot_b, mixed_b = in_blocks(normed_t), in_blocks(cot_t), in_blocks(mixed_t)
    gate_sum = Halved("gate", steps_x, me, [normed_b], [flat(d_gate)], ((((0, 0),), units),))
    up_sum = Halved("up", steps_yzx, me, [normed_b], [flat(d_up)], ((((0, 0),), units),))
    down_sum = Halved("down", steps_zxy, me, [cot_b], [flat(hidden)], ((((0, 0),), units),))
    done = down_sum.send(up_sum.send(gate_sum.send()))

    d_resid, d_out, d_pg, back, low, d_attn_t, d_ffn_gain, d_out_gain = call(
        functools.partial(mixer_back_body, heads), "mixer_back", seqs,
        [resid, d_norm, d_norm_other, cotangent, output, proj_g, reach],
        [ffn_row, w_out, out_row],
        [
            ((seqs, size, width), F32), ((seqs, size, out_wide), F32),
            ((seqs, size, out_wide), BF16), ((seqs, heads, DK, DV), F32),
            ((seqs, heads, DK, DV), BF16),
        ],
        [((1, width), F32), ((1, DV), F32)],
        turned=[(turned_shape, BF16)],
        after=[done],
        flops=1.5e9,
    )

    outs_sum = Halved(
        "outs", steps_zxy, me, [in_blocks(d_attn_t), mixed_b], [flat(gated), flat(d_pg)],
        ((((0, 0),), out_wide), (((1, 1),), out_wide)),
    )
    back = back.reshape(state_shape)
    low = low.reshape(state_shape)
    x_one, x_map, d_key, d_col, dext_q, dtap_q = call(
        functools.partial(early_body, heads), "delta_back_early", seqs,
        [proj, gates, sums, d_out, state, made, inv, score, decay], [conv_query, conv_key],
        [
            (by_value, F32), (by_key, F32), (by_key, F32), ((seqs, size, LANES), F32),
            ((seqs, size + HALO, wide), F32),
        ],
        [((CONV, wide), F32)],
        flops=3e9,
        limit=WHOLE_LIMIT,
    )
    (result,) = call(
        result_body, "result", seqs, [resid, down, down_other], [],
        [((seqs, size, width), BF16)], after=[d_col],
    )
    done = result
    for level, d in enumerate(dists):
        got = passed_along(low, "seq", -d)
        back, low = small_call(
            functools.partial(back_body, pairs), "join_back", [back_maps[level], back, got],
            [(state_shape, F32), (state_shape, BF16)], after=[done],
        )
        done = low
    near = passed_along(low, "seq", -1)
    far = passed_along(low, "seq", -1 - reach_by)
    (d_end,) = small_call(
        functools.partial(exit_body, pairs), "exit", [near_map, near, far], [(state_shape, F32)],
        after=[done],
    )
    done = outs_sum.send(down_sum.keep(up_sum.keep(gate_sum.keep(d_end))))
    d_end = d_end.reshape(seqs, heads, DK, DV)
    d_ext, d_gates, dtap_kv, d_bias = call(
        functools.partial(late_body, heads), "delta_back_late", seqs,
        [
            proj, gates, sums, d_end, state, made, decay, x_one, x_map, d_key, d_col, dext_q,
        ],
        [conv_key, conv_value],
        [((seqs, size + HALO, proj_wide), F32), ((seqs, size, LANES), BF16)],
        [((CONV, wide + out_wide), F32), ((1, LANES), F32)],
        after=[done],
        flops=3e9,
        limit=WHOLE_LIMIT,
    )
    done = down_sum.add(up_sum.add(gate_sum.add(d_bias)))
    d_qk, d_v, d_qk_halo, d_v_halo, d_mixed, d_halo = call(
        input_back_body, "input_back", seqs, [d_ext, d_pg, d_gates],
        [w_query, w_key, w_value, w_outgate, gates_w],
        [
            ((seqs, size, 2 * wide), BF16), ((seqs, size, out_wide), BF16),
            ((seqs, HALO, 2 * wide), BF16), ((seqs, HALO, out_wide), BF16),
            ((seqs, size, width), BF16), ((seqs, HALO, width), BF16),
        ],
        after=[done],
        flops=1.7e9,
    )
    d_mixed_other = swapped(d_mixed)
    halo_rows = seqs * HALO
    halo_b = jnp.swapaxes(mixed_halo.reshape(halo_rows, width), 0, 1).reshape(count, share, halo_rows)
    query_sum = Halved(
        "query_key", steps_x, me, [mixed_b, halo_b],
        [flat(d_qk), d_qk_halo.reshape(halo_rows, 2 * wide), flat(d_gates)],
        ((((0, 0), (1, 1)), 2 * wide), (((0, 2),), LANES)),
    )
    value_sum = Halved(
        "value", steps_y, me, [mixed_b, halo_b],
        [flat(d_v), d_v_halo.reshape(halo_rows, out_wide)], ((((0, 0), (1, 1)), out_wide),),
    )
    done = value_sum.send(query_sum.send(d_mixed))
    feed_sum = joined("feed_last", [gate_sum, up_sum, down_sum], done)
    done = feed_sum.kept
    done = value_sum.keep(query_sum.keep(outs_sum.keep(done)))
    halo_grad = passed_along(d_halo, "seq", -1)
    halo_other = swapped(halo_grad)
    grad_input, d_mix_gain = call(
        last_body, "first_norm_back", seqs,
        [tokens, d_mixed, d_mixed_other, halo_grad, halo_other, d_resid], [mix_row],
        [((seqs, size, width), F32)], [((1, width), F32)], after=[done],
    )

    (small,) = small_call(
        pack_body, "pack",
        [dtap_q, dtap_kv, d_bias, d_ffn_gain, d_mix_gain, d_out_gain, swapped(d_out_gain)],
        [((8, width), F32)], flops=1e4,
    )

    def finish(group, cuts, done):
        while group.left():
            done = group.add(done)
        return group.total(cuts, done)

    def small_others(bits):
        return [
            traded(small, sum(((part >> place) & 1) << bit for place, bit in enumerate(bits)))
            for part in range(1, 1 << len(bits))
        ]

    def small_step(bits, done):
        others = small_others(bits)
        return small_call(
            functools.partial(sum_body, 1 + len(others)), "small_sum", [small] + others,
            [(small.shape, F32)], after=[done], flops=1e4,
        )[0]

    bits = [[0], [1]] + [[b for step in steps_x[at : at + 2] for b in step] for at in range(2, len(steps_x), 2)]
    grad_gate, grad_up, grad_down = finish(feed_sum, [units] * 3, small)
    done = outs_sum.add(grad_gate)
    done = small = small_step(bits.pop(0), done)
    ins_sum = joined("ins_join", [query_sum, value_sum], done)
    done = small = small_step(bits.pop(0), ins_sum.kept)
    ins_sum = joined("ins_last", [ins_sum, outs_sum], done)
    while len(bits) > 1:
        small = small_step(bits.pop(0), ins_sum.kept)
    others = small_others(bits.pop(0))
    tap_shape = (CONV, wide)
    taps_q, taps_k, taps_v, grad_bias, gain_out, gains = small_call(
        functools.partial(unpack_body, heads, 1 + len(others)), "unpack", [small] + others,
        [
            (tap_shape, F32), (tap_shape, F32), ((CONV, out_wide), F32), ((2, heads), F32),
            ((1, DV), F32), ((2, share), F32),
        ],
        after=[ins_sum.kept], scalars=[(me * share).astype(jnp.int32).reshape(1)], flops=1e4,
    )
    grad_query, grad_key, grad_gates, grad_value, grad_out, grad_outgate = finish(
        ins_sum, [wide, wide, LANES, out_wide, out_wide, out_wide], gains
    )
    grad_gates = grad_gates[:, : 2 * heads].reshape(share, 2, heads)

    return (
        result,
        grad_input,
        grad_query,
        grad_key,
        grad_value,
        grad_outgate,
        jnp.swapaxes(grad_gates, 0, 1),
        grad_bias,
        taps_q,
        taps_k,
        taps_v,
        gain_out.reshape(DV),
        jnp.swapaxes(grad_out, 0, 1),
        gains[1],
        gains[0],
        grad_gate,
        grad_up,
        jnp.swapaxes(grad_down, 0, 1),
    )


def solution(mesh):
    return jax.shard_map(
        on_device,
        mesh=mesh,
        in_specs=(
            P(None, "seq", None),
            P(None, "head"),
            P(None, "head"),
            P(None, "head"),
            P(None, "head"),
            P(None, None, "head"),
            P(None, "head"),
            P(None, "head"),
            P(None, "head"),
            P(None, "head"),
            P(),
            P("head", None),
            P(),
            P(),
            P(None, "head"),
            P(None, "head"),
            P("head", None),
            P(None, "seq", None),
        ),
        out_specs=(
            P(None, "seq", None),
            P(None, "seq", None),
            P("seq", "head"),
            P("seq", "head"),
            P("seq", "head"),
            P("seq", "head"),
            P(None, "seq", "head"),
            P(None, "head"),
            P(None, "head"),
            P(None, "head"),
            P(None, "head"),
            P(),
            P("head", "seq"),
            P("seq"),
            P("seq"),
            P("seq", "head"),
            P("seq", "head"),
            P("head", "seq"),
        ),
        check_vma=False,
    )
```
